256 devices in a mesh: role: 2 (over y_lo), req: 8 (over x, core), ctx: 16 (over y_hi, z).
Axes of the slice: x: 4, y: 4 (y_hi: 2, y_lo: 2; y = y_hi * 2 + y_lo), z: 8, core: 2. Of those that a mesh axis runs over, the one named last changes fastest.
Arguments:
- query: bfloat16 [64, 16384], P('req', 'role'), may hold values from -12 to 12
- cache_keys: bfloat16 [64, 2048, 1024], P('req', 'ctx', 'role'), may hold values from -6 to 6
- cache_values: bfloat16 [64, 2048, 1024], P('req', 'ctx', 'role'), may hold values from -6 to 6
- new_keys: bfloat16 [64, 1024], P('req', 'role'), may hold values from -6 to 6
- new_values: bfloat16 [64, 1024], P('req', 'role'), may hold values from -6 to 6
- lengths: int32 [64], P('req'), may hold values from 512 to 2048, as said below
- residual_in: bfloat16 [64, 8192], P(None, 'req'), may hold values from -24 to 24
- out_proj: bfloat16 [16384, 8192], P(('role', 'ctx'), 'req'), may hold values from -1.5 to 1.5
- norm_gain: float32 [8192], replicated, may hold values from 0.1 to 1.9
- adapter_down: bfloat16 [8192, 256], P('req'), may hold values from -0.0625 to 0.0625
- tenant_adapter_up_matrix: bfloat16 [256, 32768], P(None, ('role', 'req', 'ctx')), may hold values from -1.5 to 1.5
- tenant: int32 [64], replicated, may hold values from 0 to 15
- w_gate: bfloat16 [8192, 32768], P(None, ('role', 'req', 'ctx')), may hold values from -0.0625 to 0.0625
- w_up: bfloat16 [8192, 32768], P(None, ('role', 'req', 'ctx')), may hold values from -0.0625 to 0.0625
- w_down: bfloat16 [32768, 8192], P(('role', 'req', 'ctx')), may hold values from -0.125 to 0.125
Outputs:
- hidden_out: bfloat16 [64, 8192], P('req', ('role', 'ctx'))
The draws below stay inside these ranges and needn't reach their ends.
Inputs may be any that keep to these rules, and one draw needn't show every extreme that they name: `lengths`: each request has between a quarter of the cache and all of it in use; some request uses all 2048 positions.
All inputs are finite; a program needn't handle non-finite values.
Results may differ from the reference program's by a relative error of at most 0.0058.
Values may be sent and summed in bfloat16 or wider, within the bound.
A program may use at most 64 MiB of HBM per device.

```python
import math
import jax
import jax.numpy as jnp
from jax import lax

D = 8192
HQ = 128
KVH = 8
HD = 128
FF = 32768
RANK = 16
TENANTS = 16
ROWS = 64
CONTEXT = 2048


def sign_pattern(key):
    return jax.random.rademacher(jax.random.fold_in(key, 77), (ROWS, KVH, HD), dtype=jnp.float32)


def drawn_rows():
    row_index = jnp.arange(ROWS)
    selected = row_index % 4 == 0
    opposed = jnp.logical_and(selected, row_index // 4 % 2 == 0)
    target = 110.0 + 50.0 * (row_index // 4 % 4).astype(jnp.float32)
    strength = target / (6.0 * math.sqrt(HD))
    return (selected, opposed, strength)


def near_magnitude(strength):
    lowered = jnp.floor(3.0 * math.sqrt(HD) / strength) + 1.0
    column = jnp.arange(HD).astype(jnp.float32)
    return jnp.where(column[None, :] < lowered[:, None], 5.5, 6.0)


def draw_query(key, part):
    base_key = key
    key = jax.random.fold_in(key, 1)
    values = jnp.clip(jax.random.normal(key, (ROWS, HQ * HD), jnp.float32), -6.0, 6.0)
    pattern = sign_pattern(base_key)
    selected, opposed, strength = drawn_rows()
    aligned = strength[:, None, None, None] * jnp.broadcast_to(pattern[:, :, None, :], (ROWS, KVH, HQ // KVH, HD))
    values = jnp.where(selected[:, None], aligned.reshape(ROWS, HQ * HD), values)
    return values.astype(jnp.bfloat16)


def draw_cache_keys(key, part):
    base_key = key
    key = jax.random.fold_in(key, 2)
    values = jnp.clip(jax.random.normal(key, (ROWS, CONTEXT, KVH * HD), jnp.float32), -6.0, 6.0)
    pattern = sign_pattern(base_key)
    selected, opposed, strength = drawn_rows()
    first = jnp.where(selected[:, None], 6.0 * pattern.reshape(ROWS, KVH * HD), values[:, 0, :])
    nearby = (near_magnitude(strength)[:, None, :] * pattern).reshape(ROWS, KVH * HD)
    second = jnp.where(selected[:, None], nearby, values[:, 1, :])
    values = values.at[:, 0, :].set(first)
    values = values.at[:, 1, :].set(second)
    return values.astype(jnp.bfloat16)


def draw_new_keys(key, part):
    base_key = key
    key = jax.random.fold_in(key, 3)
    values = jnp.clip(jax.random.normal(key, (ROWS, KVH * HD), jnp.float32), -6.0, 6.0)
    pattern = sign_pattern(base_key)
    selected, opposed, strength = drawn_rows()
    aligned = (near_magnitude(strength)[:, None, :] * pattern).reshape(ROWS, KVH * HD)
    reversed_key = (-6.0 * pattern).reshape(ROWS, KVH * HD)
    values = jnp.where(selected[:, None], aligned, values)
    values = jnp.where(opposed[:, None], reversed_key, values)
    return values.astype(jnp.bfloat16)


def draw_residual_in(key, part):
    key = jax.random.fold_in(key, 4)
    first_key = jax.random.fold_in(key, 0)
    values = jnp.clip(jax.random.normal(first_key, (ROWS, D), jnp.float32), -6.0, 6.0)
    return values.astype(jnp.bfloat16)


def draw_lengths(key, part):
    key = jax.random.fold_in(key, 5)
    first_key, second_key = jax.random.split(key)
    values = jax.random.randint(first_key, (ROWS,), CONTEXT // 4, CONTEXT + 1, dtype=jnp.int32)
    position = jax.random.randint(second_key, (), 0, ROWS, dtype=jnp.int32)
    return values.at[position].set(CONTEXT)


def place_ends(result, key, least, largest):
    extent = result.shape
    index_at = [jax.random.randint(jax.random.fold_in(key, axis), (), 0, extent[axis]) for axis in range(len(extent))]
    result = result.at[tuple(index_at)].set(least)
    longest = extent.index(max(extent))
    index_at[longest] = (index_at[longest] + 1) % extent[longest]
    return result.at[tuple(index_at)].set(largest)


def with_spikes(values, rng, source, target, blocks, factor):
    def block_of(dim):
        return (jnp.arange(values.shape[dim]) // (values.shape[dim] // blocks)).reshape((-1,) + (1,) * (values.ndim - 1 - dim))

    near = jax.random.permutation(rng, blocks)[block_of(target)]
    second = (block_of(target) + blocks // 2) % blocks
    return jnp.where((block_of(source) == near) | (block_of(source) == second), factor * values, values)


def steps_of(stream_key, shape, pieces, least, top_value):
    gain = 1.0
    for dim, shards_of in pieces:
        steps = jax.random.uniform(jax.random.fold_in(jax.random.fold_in(stream_key, 6), dim), (shards_of,), jnp.float32, least / len(pieces), top_value / len(pieces))
        gain = gain * jnp.repeat(jnp.exp(steps), shape[dim] // shards_of).reshape((-1,) + (1,) * (len(shape) - 1 - dim))
    return gain


def gaussian(own_key, extent, width, reach, pieces=(), kind=jnp.bfloat16):
    drawn = jax.random.normal(own_key, extent, jnp.float32) * width
    if len(pieces) > 0:
        drawn = steps_of(own_key, extent, pieces, -0.22, 0.18) * drawn
    return jnp.clip(drawn, min=-reach, max=reach).astype(kind)


def bell_draw_with(own_key, shape, scale, most, shards, heavy, kind=jnp.bfloat16):
    array = scale * jax.random.normal(own_key, shape, jnp.float32)
    if shards:
        array = array * steps_of(own_key, shape, shards, -0.22, 0.18)
    return jnp.clip(with_spikes(array, jax.random.fold_in(own_key, 3), *heavy), -most, most).astype(kind)


def setup_inputs(seed: int = 0) -> dict:
    splits = jax.random.split(jax.random.key(seed), 16)
    query = draw_query(jax.random.fold_in(splits[15], 71), 0)
    cache_keys = draw_cache_keys(jax.random.fold_in(splits[15], 71), 0)
    cache_values = gaussian(splits[2], (ROWS, CONTEXT, KVH * HD), 1.0, 6.0, ((0, 8), (1, 16), (2, 2)))
    new_keys = draw_new_keys(jax.random.fold_in(splits[15], 71), 0)
    new_values = gaussian(splits[4], (ROWS, KVH * HD), 1.0, 6.0, ((0, 8), (1, 2)))
    lengths = draw_lengths(jax.random.fold_in(splits[15], 71), 0)
    residual_in = draw_residual_in(jax.random.fold_in(splits[15], 71), 0)
    out_proj = gaussian(splits[7], (HQ * HD, D), (HD // 8) ** -0.5, 1.5, ((0, 32), (1, 8)))
    norm_gain = jnp.clip(1.0 + 0.18 * jax.random.normal(splits[8], (D,), jnp.float32), 0.1, 1.9)
    adapter_down = gaussian(splits[9], (D, TENANTS * RANK), D ** -0.5, 0.0625, ((0, 8),))
    tenant_adapter_up_matrix = gaussian(splits[10], (TENANTS * RANK, FF), RANK ** -0.5, 1.5, ((1, 256),))
    tenant = place_ends(jax.random.randint(splits[11], (ROWS,), 0, TENANTS), jax.random.fold_in(splits[11], 1), 0, TENANTS - 1).astype(jnp.int32)
    w_gate = gaussian(splits[12], (D, FF), D ** -0.5, 0.0625, ((1, 256),))
    w_up = gaussian(splits[13], (D, FF), D ** -0.5, 0.0625, ((1, 256),))
    w_down = bell_draw_with(splits[14], (FF, D), FF ** -0.5, 0.125, ((0, 256),), (0, 1, 256, 6.0))
    return {"query": query, "cache_keys": cache_keys, "cache_values": cache_values, "new_keys": new_keys, "new_values": new_values, "lengths": lengths, "residual_in": residual_in, "out_proj": out_proj, "norm_gain": norm_gain, "adapter_down": adapter_down, "tenant_adapter_up_matrix": tenant_adapter_up_matrix, "tenant": tenant, "w_gate": w_gate, "w_up": w_up, "w_down": w_down}


epsilon = 1e-05
low_rank_weight = 2.0

def attend_request(operands):
    queries, keys_row, values_row, fresh_key, fresh_value, length_row = operands
    grouped = queries.astype(jnp.float32).reshape(KVH, HQ // KVH, HD)
    keys_float = keys_row.astype(jnp.float32).reshape(CONTEXT, KVH, HD)
    values_float = values_row.astype(jnp.float32).reshape(CONTEXT, KVH, HD)
    factor = 1.0 / math.sqrt(HD)
    scores = jnp.einsum('kgd,pkd->kgp', grouped, keys_float, precision=lax.Precision.HIGHEST) * factor
    usable = jnp.arange(CONTEXT) < length_row
    scores = jnp.where(usable[None, None, :], scores, -jnp.inf)
    fresh_token_score = jnp.einsum('kgd,kd->kg', grouped, fresh_key.astype(jnp.float32).reshape(KVH, HD), precision=lax.Precision.HIGHEST) * factor
    highest = jnp.maximum(lax.optimization_barrier(jnp.max(scores, axis=-1)), fresh_token_score)
    weights = jnp.exp(scores - highest[..., None])
    self_weight = jnp.exp(fresh_token_score - highest)
    denominator = lax.optimization_barrier(jnp.sum(weights, axis=-1)) + self_weight
    numerator = jnp.einsum('kgp,pkd->kgd', weights, values_float, precision=lax.Precision.HIGHEST)
    numerator = numerator + self_weight[..., None] * fresh_value.astype(jnp.float32).reshape(KVH, 1, HD)
    return (numerator / denominator[..., None]).reshape(HQ * HD).astype(jnp.bfloat16)

def reference(query, cache_keys, cache_values, new_keys, new_values, lengths, residual_in, out_proj, norm_gain, adapter_down, tenant_adapter_up_matrix, tenant, w_gate, w_up, w_down):
    attention = lax.map(attend_request, (query, cache_keys, cache_values, new_keys, new_values, lengths))
    projected = jnp.dot(attention, out_proj, preferred_element_type=jnp.float32)
    stream = (residual_in.astype(jnp.float32) + projected).astype(jnp.bfloat16)
    widened = stream.astype(jnp.float32)
    inverse = lax.rsqrt(lax.optimization_barrier(jnp.mean(widened * widened, axis=-1, keepdims=True)) + epsilon)
    normed = (widened * inverse * norm_gain).astype(jnp.bfloat16)
    adapter_mid = jnp.dot(normed, adapter_down, preferred_element_type=jnp.float32)
    owners = (jnp.arange(TENANTS * RANK) // RANK).astype(jnp.int32)
    picked_tenant = jnp.where(tenant[:, None] == owners[None, :], adapter_mid, 0.0).astype(jnp.bfloat16)
    gate = jnp.dot(normed, w_gate, preferred_element_type=jnp.float32)
    up_projection_share = jnp.dot(normed, w_up, preferred_element_type=jnp.float32)
    up_projection_share = up_projection_share + low_rank_weight * jnp.dot(picked_tenant, tenant_adapter_up_matrix, preferred_element_type=jnp.float32)
    hidden = (jax.nn.silu(gate) * up_projection_share).astype(jnp.bfloat16)
    return (widened + jnp.dot(hidden, w_down, preferred_element_type=jnp.float32)).astype(jnp.bfloat16)
```

```python
import functools
import math

import jax
import jax.numpy as jnp
from jax import lax
from jax.experimental import pallas as pl
from jax.experimental.pallas import tpu as pltpu
from jax.sharding import PartitionSpec as P

MESH = pl.DeviceIdType.MESH
F32 = jnp.float32
BF16 = jnp.bfloat16
HD = 128
EPS = 1e-05
LOW = -1e30
NT = (((1,), (1,)), ((), ()))


def rcopy(src, dst, ssem, rsem, dev):
    return pltpu.make_async_remote_copy(
        src_ref=src, dst_ref=dst, send_sem=ssem, recv_sem=rsem, device_id=dev, device_id_type=MESH
    )


def loop(lo, hi, body):
    def step(i, carry):
        body(i)
        return carry

    lax.fori_loop(lo, hi, step, 0)


def kernel(
    stop,
    q_h, ck_h, cv_h, nk_h, nv_h, len_s, res_h, wo_h, gain_h, ad_h, tu_h, ten_s, wg_h, wu_h, wd_h,
    out_ref,
    q_v, ck_v, cv_v, nk_v, nv_v, res_v, wo_v, gain_v, ad_v, tu_v, wgu_v, wd_v,
    qrows, acc_s, stat_s, racc, rstat, rt_v,
    ogath, psend, rpart, xs, ad_s, rad, dbuf, rcore, r1, rx, r2, ry, r3, rz,
    lsem,
    sa_s, sa_r, ss_s, ss_r, so_s, so_r, sp_s, sp_r, sz_s, sz_r, sy_s, sy_r, sx_s, sx_r, sc_s, sc_r,
    sd_s, sd_r, e_c, e_x, e_y, e_z,
):
    role = lax.axis_index("role")
    req = lax.axis_index("req")
    ctx = lax.axis_index("ctx")
    x = lax.div(req, 2)
    core = lax.rem(req, 2)
    yhi = lax.div(ctx, 8)
    z = lax.rem(ctx, 8)
    y = yhi * 2 + role
    yz = role * 16 + ctx
    me = (role, req, ctx)

    def at_yz(i):
        return (lax.div(i, 16), req, lax.rem(i, 16))

    def at_req(i):
        return (role, i, ctx)

    def at_y(i):
        return (lax.rem(i, 2), req, lax.div(i, 2) * 8 + z)

    def at_z(i):
        return (role, req, yhi * 8 + i)

    local = [
        pltpu.make_async_copy(q_h, q_v, lsem.at[0]),
        pltpu.make_async_copy(ck_h, ck_v, lsem.at[1]),
        pltpu.make_async_copy(cv_h, cv_v, lsem.at[2]),
        pltpu.make_async_copy(nk_h, nk_v, lsem.at[3]),
        pltpu.make_async_copy(nv_h, nv_v, lsem.at[4]),
        pltpu.make_async_copy(wo_h, wo_v, lsem.at[5]),
        pltpu.make_async_copy(
            res_h.at[pl.ds(pl.multiple_of(y * 16, 16), 16), pl.ds(pl.multiple_of(z * 128, 128), 128)],
            res_v, lsem.at[6],
        ),
        pltpu.make_async_copy(gain_h, gain_v, lsem.at[7]),
        pltpu.make_async_copy(ad_h, ad_v, lsem.at[8]),
        pltpu.make_async_copy(tu_h, tu_v, lsem.at[9]),
        pltpu.make_async_copy(wg_h, wgu_v.at[:, pl.ds(0, 128)], lsem.at[10]),
        pltpu.make_async_copy(wu_h, wgu_v.at[:, pl.ds(128, 128)], lsem.at[11]),
        pltpu.make_async_copy(wd_h, wd_v, lsem.at[12]),
    ]
    for c in local:
        c.start()

    barrier = pltpu.get_barrier_semaphore()
    loop(1, 32, lambda o: pl.semaphore_signal(
        barrier, inc=1, device_id=at_yz(lax.rem(yz + o, 32)), device_id_type=MESH))
    loop(1, 8, lambda o: pl.semaphore_signal(
        barrier, inc=1, device_id=at_req(lax.rem(req + o, 8)), device_id_type=MESH))

    factor = 1.0 / math.sqrt(HD)
    sub = lax.broadcasted_iota(jnp.int32, (8, 128), 0)
    lane = lax.broadcasted_iota(jnp.int32, (8, 128), 1)
    lens = jnp.zeros((8, 128), jnp.int32)
    for r in range(8):
        lens = jnp.where(sub == r, len_s[r], lens)
    usable = (ctx * 128 + lane < lens)[None]
    rowmod = lax.broadcasted_iota(jnp.int32, (16, 8, 128), 1)
    stat_lane = lax.broadcasted_iota(jnp.int32, (128, 128), 1)
    local[0].wait()
    local[1].wait()
    local[2].wait()
    stat = jnp.zeros((128, 128), F32)
    for k in range(4):
        qk = jnp.concatenate(
            [q_v[:, (k * 16 + g) * 128:(k * 16 + g + 1) * 128].astype(F32) for g in range(16)], axis=0)
        qrows[k * 128:(k + 1) * 128, :] = qk
        kk = ck_v[:, :, k * 128:(k + 1) * 128].reshape(1024, 128)
        full = lax.dot_general(qk.astype(BF16), kk, NT, preferred_element_type=F32)
        sc = jnp.zeros((16, 8, 128), F32)
        for r in range(8):
            sc = jnp.where(rowmod == r, full[:, r * 128:(r + 1) * 128].reshape(16, 8, 128), sc)
        sc = jnp.where(usable, sc * factor, LOW)
        top = jnp.max(sc, axis=-1, keepdims=True)
        w = jnp.where(usable, jnp.exp(sc - top), 0.0)
        wb = w.astype(BF16).astype(F32)
        tot = jnp.sum(wb, axis=-1, keepdims=True)
        big = jnp.concatenate(
            [jnp.where(rowmod == r, wb, 0.0).reshape(128, 128).astype(BF16) for r in range(8)], axis=1)
        vk = cv_v[:, :, k * 128:(k + 1) * 128].reshape(1024, 128)
        acc = jnp.dot(big, vk, preferred_element_type=F32)
        acc_s[4 * k:4 * k + 4] = acc.astype(BF16).reshape(4, 32, 128)
        stat = jnp.where(stat_lane == 2 * k, top.reshape(128, 1), stat)
        stat = jnp.where(stat_lane == 2 * k + 1, tot.reshape(128, 1), stat)
    stat_s[...] = stat.T[0:8, :]

    pl.semaphore_wait(barrier, 38)

    def acc_copy(o):
        c = lax.rem(ctx + o, 16)
        return rcopy(acc_s.at[c], racc.at[ctx], sa_s.at[o], sa_r.at[ctx], (role, req, c))

    def stat_copy(o):
        c = lax.rem(ctx + o, 16)
        return rcopy(stat_s, rstat.at[ctx], ss_s.at[o], ss_r.at[ctx], (role, req, c))

    def send_attn(o):
        acc_copy(o).start()
        stat_copy(o).start()

    loop(1, 16, send_attn)
    racc[ctx] = acc_s[ctx]
    rstat[ctx] = stat_s[...]

    kh = lax.div(ctx, 4)
    local[3].wait()
    local[4].wait()
    col = pl.ds(pl.multiple_of(kh * 128, 128), 128)
    q32 = qrows[pl.ds(pl.multiple_of(ctx * 32, 32), 32), :].reshape(4, 8, 128)
    nk = nk_v[:, col].astype(F32)
    nv = nv_v[:, col].astype(F32)
    s_self = (jnp.sum(q32 * nk[None], axis=-1, keepdims=True) * factor).reshape(32, 1)
    nv32 = jnp.broadcast_to(nv[None], (4, 8, 128)).reshape(32, 128)

    def wait_attn(o):
        c = lax.rem(ctx + o, 16)
        rcopy(acc_s.at[c], racc.at[c], sa_s.at[o], sa_r.at[c], me).wait_recv()
        rcopy(stat_s, rstat.at[c], ss_s.at[o], ss_r.at[c], me).wait_recv()

    loop(1, 16, wait_attn)
    rt_v[...] = rstat[...].reshape(128, 128).T
    st = rt_v[pl.ds(pl.multiple_of(lax.rem(ctx, 4) * 32, 32), 32), :]
    st = pltpu.roll(st, lax.rem(128 - 2 * kh, 128), 1)
    lane32 = lax.broadcasted_iota(jnp.int32, (32, 128), 1)
    first = lane32 % 8 == 0
    tops = jnp.where(first, st, -3e38)
    high = jnp.maximum(jnp.max(tops, axis=-1, keepdims=True), s_self)
    wgt = jnp.where(first, jnp.exp(tops - high), 0.0)
    w_self = jnp.exp(s_self - high)
    den = jnp.sum(wgt * pltpu.roll(st, 127, 1), axis=-1, keepdims=True) + w_self
    o_acc = w_self * nv32
    for s in range(16):
        o_acc = o_acc + wgt[:, 8 * s:8 * s + 1] * racc[s].astype(F32)
    ogath[req] = (o_acc / den).astype(BF16)

    def o_copy(o):
        return rcopy(ogath.at[req], ogath.at[req], so_s.at[o], so_r.at[req], at_req(lax.rem(req + o, 8)))

    loop(1, 8, lambda o: o_copy(o).start())

    def wait_o(o):
        c = lax.rem(req + o, 8)
        rcopy(ogath.at[c], ogath.at[c], so_s.at[o], so_r.at[c], me).wait_recv()

    loop(1, 8, wait_o)
    local[5].wait()
    og = ogath[...].astype(F32)
    attn = jnp.concatenate(
        [og[:, 8 * g:8 * g + 8, :].reshape(64, 128) for g in range(4)], axis=1).astype(BF16)
    proj = jnp.dot(attn, wo_v[...], preferred_element_type=F32)
    for yy in range(4):
        for zz in range(8):
            psend[yy, zz] = proj[16 * yy:16 * yy + 16, 128 * zz:128 * zz + 128].astype(BF16)

    def p_copy(o):
        d = lax.rem(yz + o, 32)
        rr, cc = lax.div(d, 16), lax.rem(d, 16)
        return rcopy(psend.at[lax.div(cc, 8) * 2 + rr, lax.rem(cc, 8)], rpart.at[yz],
                     sp_s.at[o], sp_r.at[yz], (rr, req, cc))

    loop(1, 32, lambda o: p_copy(o).start())
    rpart[yz] = psend[y, z]

    def wait_p(o):
        c = lax.rem(yz + o, 32)
        rcopy(rpart.at[c], rpart.at[c], sp_s.at[o], sp_r.at[c], me).wait_recv()

    loop(1, 32, wait_p)
    local[6].wait()
    piece = res_v[...].astype(F32) + jnp.sum(rpart[...].astype(F32), axis=0)
    rows_y = pl.ds(pl.multiple_of(y * 16, 16), 16)
    xs[req * 8 + z, rows_y, :] = piece.astype(BF16)

    def z_ref(i):
        return xs.at[req * 8 + i, rows_y]

    def z_copy(o):
        return rcopy(z_ref(z), z_ref(z), sz_s.at[o], sz_r.at[z], at_z(lax.rem(z + o, 8)))

    loop(1, 8, lambda o: z_copy(o).start())

    def wait_z(o):
        c = lax.rem(z + o, 8)
        rcopy(z_ref(c), z_ref(c), sz_s.at[o], sz_r.at[c], me).wait_recv()

    loop(1, 8, wait_z)

    def y_ref(i):
        return xs.at[pl.ds(req * 8, 8), pl.ds(pl.multiple_of(i * 16, 16), 16)]

    def y_copy(o):
        return rcopy(y_ref(y), y_ref(y), sy_s.at[o], sy_r.at[y], at_y(lax.rem(y + o, 4)))

    for o in range(1, 4):
        y_copy(o).start()
    for o in range(1, 4):
        c = lax.rem(y + o, 4)
        rcopy(y_ref(c), y_ref(c), sy_s.at[o], sy_r.at[c], me).wait_recv()

    def b_ref(b):
        return xs.at[pl.ds(b * 8, 8)]

    def x_copy(o):
        return rcopy(b_ref(req), b_ref(req), sx_s.at[o], sx_r.at[x], at_req(lax.rem(x + o, 4) * 2 + core))

    def c_copy(o):
        b = lax.rem(x + o, 4) * 2 + core
        return rcopy(b_ref(b), b_ref(b), sc_s.at[o], sc_r.at[lax.rem(x + o, 4)], at_req(x * 2 + 1 - core))

    for o in (1, 3, 2):
        x_copy(o).start()
    c_copy(0).start()
    local[7].wait()
    local[8].wait()
    local[10].wait()
    local[11].wait()

    def block(b):
        xb = xs[pl.ds(b * 8, 8)].astype(F32)
        sq = jnp.sum(jnp.sum(xb * xb, axis=0), axis=-1, keepdims=True)
        xg = xb * gain_v[pl.ds(pl.multiple_of(b * 8, 8), 8), :][:, None, :]
        xg = jnp.concatenate([xg[i] for i in range(8)], axis=1).astype(BF16)
        return sq, xg

    def gate_up(b, xg):
        rows = pl.ds(pl.multiple_of(b * 1024, 1024), 1024)
        return jnp.dot(xg, wgu_v[rows, :], preferred_element_type=F32)

    sq, xg = block(req)
    mid = jnp.dot(xg, ad_v[...], preferred_element_type=F32)
    owner = lax.div(lane, 16)
    tens = []
    packed = jnp.zeros((8, 128), F32)
    for i in range(8):
        t = jnp.zeros((8, 128), jnp.int32)
        for r in range(8):
            t = jnp.where(sub == r, ten_s[8 * i + r], t)
        tens.append(t)
        v = (jnp.where(owner == t, mid[8 * i:8 * i + 8, 0:128], 0.0)
             + jnp.where(owner + 8 == t, mid[8 * i:8 * i + 8, 128:256], 0.0))
        v = v + pltpu.roll(v, 64, 1)
        v = v + pltpu.roll(v, 32, 1)
        v = v + pltpu.roll(v, 16, 1)
        packed = jnp.where(owner == i, v, packed)
    ad_s[...] = packed

    def d_copy(o):
        return rcopy(ad_s, rad.at[req], sd_s.at[o], sd_r.at[req], at_req(lax.rem(req + o, 8)))

    loop(1, 8, lambda o: d_copy(o).start())
    rad[req] = packed
    gu = gate_up(req, xg)
    for o in (0, 1, 3, 2):
        xo = lax.rem(x + o, 4)
        if o > 0:
            b = xo * 2 + core
            rcopy(b_ref(b), b_ref(b), sx_s.at[o], sx_r.at[xo], me).wait_recv()
            c_copy(o).start()
            s1, xg = block(b)
            sq = sq + s1
            gu = gu + gate_up(b, xg)
        b = xo * 2 + 1 - core
        rcopy(b_ref(b), b_ref(b), sc_s.at[o], sc_r.at[xo], me).wait_recv()
        s1, xg = block(b)
        sq = sq + s1
        gu = gu + gate_up(b, xg)

    def wait_d(o):
        c = lax.rem(req + o, 8)
        rcopy(ad_s, rad.at[c], sd_s.at[o], sd_r.at[c], me).wait_recv()

    loop(1, 8, wait_d)
    inv = lax.rsqrt(sq * (1.0 / 8192.0) + EPS)
    allmid = jnp.sum(rad[...], axis=0)
    chosen = []
    for i in range(8):
        v = jnp.where(owner == i, allmid, 0.0)
        v = v + pltpu.roll(v, 64, 1)
        v = v + pltpu.roll(v, 32, 1)
        v = v + pltpu.roll(v, 16, 1)
        v = v * inv[8 * i:8 * i + 8]
        chosen.append(jnp.concatenate(
            [jnp.where(owner == tens[i], v, 0.0), jnp.where(owner + 8 == tens[i], v, 0.0)], axis=1))
    local[9].wait()
    lowrank = jnp.dot(jnp.concatenate(chosen, axis=0).astype(BF16), tu_v[...], preferred_element_type=F32)
    gate = gu[:, 0:128] * inv
    up = gu[:, 128:256] * inv + 2.0 * lowrank
    hid = (gate / (1.0 + jnp.exp(-gate)) * up).astype(BF16)

    local[12].wait()
    for p in range(32):
        rr, cc = p // 16, p % 16
        yy, zz = (cc // 8) * 2 + rr, cc % 8
        part = jnp.dot(hid, wd_v[:, 256 * p:256 * p + 256], preferred_element_type=F32)
        for b in range(8):
            dbuf[b % 2, b // 2, yy, zz] = jnp.concatenate(
                [part[8 * b:8 * b + 8, 0:128], part[8 * b:8 * b + 8, 128:256]], axis=0).astype(BF16)

    core_copy = rcopy(dbuf.at[1 - core], rcore, e_c.at[0], e_c.at[1], at_req(x * 2 + 1 - core))
    core_copy.start()
    core_copy.wait_recv()

    def fold_core(i):
        r1[i] = (dbuf[core, i].astype(F32) + rcore[i].astype(F32)).astype(BF16)

    loop(0, 4, fold_core)

    def ex_copy(o):
        xo = lax.rem(x + o, 4)
        return rcopy(r1.at[xo], rx.at[x], e_x.at[o], e_x.at[4 + x], at_req(xo * 2 + core))

    for o in (2, 1, 3):
        ex_copy(o).start()
    for o in range(1, 4):
        xo = lax.rem(x + o, 4)
        rcopy(r1.at[xo], rx.at[xo], e_x.at[o], e_x.at[4 + xo], me).wait_recv()
    xa, xb2, xc = lax.rem(x + 1, 4), lax.rem(x + 2, 4), lax.rem(x + 3, 4)

    def fold_x(i):
        r2[i] = (r1[x, i].astype(F32) + rx[xa, i].astype(F32)
                 + rx[xb2, i].astype(F32) + rx[xc, i].astype(F32)).astype(BF16)

    loop(0, 4, fold_x)

    def ey_copy(o):
        yo = lax.rem(y + o, 4)
        return rcopy(r2.at[yo], ry.at[y], e_y.at[o], e_y.at[4 + y], at_y(yo))

    for o in (2, 1, 3):
        ey_copy(o).start()
    for o in range(1, 4):
        yo = lax.rem(y + o, 4)
        rcopy(r2.at[yo], ry.at[yo], e_y.at[o], e_y.at[4 + yo], me).wait_recv()
    r3[...] = (r2[y].astype(F32) + ry[lax.rem(y + 1, 4)].astype(F32)
               + ry[lax.rem(y + 2, 4)].astype(F32) + ry[lax.rem(y + 3, 4)].astype(F32)).astype(BF16)

    def ez_copy(o):
        zo = lax.rem(z + o, 8)
        return rcopy(r3.at[zo], rz.at[z], e_z.at[o], e_z.at[8 + z], at_z(zo))

    loop(1, 8, lambda o: ez_copy(o).start())
    rz[z] = r3[z]

    def wait_ez(o):
        zo = lax.rem(z + o, 8)
        rcopy(r3.at[zo], rz.at[zo], e_z.at[o], e_z.at[8 + zo], me).wait_recv()

    loop(1, 8, wait_ez)
    own = xs[pl.ds(yz * 2, 2), pl.ds(pl.multiple_of(x * 16, 16), 16), :].astype(F32)
    own = jnp.where(core == 0, own[:, 0:8, :], own[:, 8:16, :])
    res = own.reshape(16, 128) + jnp.sum(rz[...].astype(F32), axis=0)
    out_ref[:, 0:128] = res[0:8, :].astype(BF16)
    out_ref[:, 128:256] = res[8:16, :].astype(BF16)

    def drain_attn(o):
        acc_copy(o).wait_send()
        stat_copy(o).wait_send()

    loop(1, 16, drain_attn)
    loop(1, 32, lambda o: p_copy(o).wait_send())

    def drain8(o):
        o_copy(o).wait_send()
        z_copy(o).wait_send()
        d_copy(o).wait_send()
        ez_copy(o).wait_send()

    loop(1, 8, drain8)
    for o in range(1, 4):
        y_copy(o).wait_send()
        x_copy(o).wait_send()
        ex_copy(o).wait_send()
        ey_copy(o).wait_send()
    for o in range(4):
        c_copy(o).wait_send()
    core_copy.wait_send()


def shards(query, cache_keys, cache_values, new_keys, new_values, lengths, residual_in, out_proj,
           norm_gain, adapter_down, tenant_adapter_up_matrix, tenant, w_gate, w_up, w_down):
    hbm = pl.BlockSpec(memory_space=pl.ANY)
    smem = pl.BlockSpec(memory_space=pltpu.SMEM)
    v = pltpu.VMEM
    dma = pltpu.SemaphoreType.DMA
    return pl.pallas_call(
        functools.partial(kernel, None),
        out_shape=jax.ShapeDtypeStruct((8, 256), BF16),
        in_specs=[hbm, hbm, hbm, hbm, hbm, smem, hbm, hbm, hbm, hbm, hbm, smem, hbm, hbm, hbm],
        out_specs=pl.BlockSpec(memory_space=pltpu.VMEM),
        scratch_shapes=[
            v((8, 8192), BF16), v((8, 128, 512), BF16), v((8, 128, 512), BF16), v((8, 512), BF16),
            v((8, 512), BF16), v((16, 128), BF16), v((512, 1024), BF16), v((64, 128), F32),
            v((1024, 256), BF16), v((256, 128), BF16), v((8192, 256), BF16), v((128, 8192), BF16),
            v((512, 128), F32), v((16, 32, 128), BF16), v((8, 128), F32), v((16, 32, 128), BF16),
            v((16, 8, 128), F32), v((128, 128), F32),
            v((8, 32, 128), BF16), v((4, 8, 16, 128), BF16), v((32, 16, 128), BF16), v((64, 64, 128), BF16),
            v((8, 128), F32), v((8, 8, 128), F32),
            v((2, 4, 4, 8, 16, 128), BF16), v((4, 4, 8, 16, 128), BF16), v((4, 4, 8, 16, 128), BF16),
            v((4, 4, 8, 16, 128), BF16), v((4, 8, 16, 128), BF16), v((4, 8, 16, 128), BF16),
            v((8, 16, 128), BF16), v((8, 16, 128), BF16),
            dma((13,)),
            dma((16,)), dma((16,)), dma((16,)), dma((16,)), dma((8,)), dma((8,)), dma((32,)), dma((32,)),
            dma((8,)), dma((8,)), dma((4,)), dma((4,)), dma((4,)), dma((4,)), dma((4,)), dma((4,)),
            dma((8,)), dma((8,)), dma((2,)), dma((8,)), dma((8,)), dma((16,)),
        ],
        compiler_params=pltpu.CompilerParams(
            collective_id=0, has_side_effects=True, vmem_limit_bytes=48 * 1024 * 1024),
    )(query, cache_keys, cache_values, new_keys, new_values, lengths, residual_in, out_proj,
      norm_gain.reshape(64, 128), adapter_down, tenant_adapter_up_matrix, tenant, w_gate, w_up, w_down)


def solution(mesh):
    placed = (
        P("req", "role"),
        P("req", "ctx", "role"),
        P("req", "ctx", "role"),
        P("req", "role"),
        P("req", "role"),
        P("req"),
        P(None, "req"),
        P(("role", "ctx"), "req"),
        P(),
        P("req", None),
        P(None, ("role", "req", "ctx")),
        P(),
        P(None, ("role", "req", "ctx")),
        P(None, ("role", "req", "ctx")),
        P(("role", "req", "ctx"), None),
    )
    return jax.shard_map(
        shards, mesh=mesh, in_specs=placed, out_specs=P("req", ("role", "ctx")), check_vma=False
    )
```

```python
import functools
import math

import jax
import jax.numpy as jnp
from jax import lax
from jax.experimental import pallas as pl
from jax.experimental.pallas import tpu as pltpu
from jax.sharding import PartitionSpec as P

MESH = pl.DeviceIdType.MESH
F32 = jnp.float32
BF16 = jnp.bfloat16
HD = 128
EPS = 1e-05
LOW = -1e30
NT = (((1,), (1,)), ((), ()))
Z_FAR = (4, 3, 5, 2, 6, 1, 7)
XY_FAR = ((2, 2), (1, 2), (3, 2), (2, 1), (2, 3), (1, 1), (1, 3), (3, 1), (3, 3),
          (2, 0), (0, 2), (1, 0), (3, 0), (0, 1), (0, 3))
YZ_FAR = tuple((dy, dz) for dz in Z_FAR + (0,) for dy in (2, 1, 3, 0) if dy or dz)
REQ_FAR = ((2, 1), (2, 0), (1, 1), (3, 1), (1, 0), (3, 0), (0, 1))
CTX_FAR = tuple((dh, dz) for dz in Z_FAR + (0,) for dh in (1, 0) if dh or dz)


def rcopy(src, dst, ssem, rsem, dev):
    return pltpu.make_async_remote_copy(
        src_ref=src, dst_ref=dst, send_sem=ssem, recv_sem=rsem, device_id=dev, device_id_type=MESH
    )


def loop(lo, hi, body):
    def step(i, carry):
        body(i)
        return carry

    lax.fori_loop(lo, hi, step, 0)


def kernel(
    stop,
    q_h, ck_h, cv_h, nk_h, nv_h, len_s, res_h, wo_h, gain_h, ad_h, tu_h, ten_s, wg_h, wu_h, wd_h,
    out_ref,
    q_v, ck_v, cv_v, nk_v, nv_v, res_v, wo_v, gain_v, ad_v, tu_v, wgu_v, wd_v,
    qrows, acc_s, stat_s, racc, rstat, rt_v,
    ogath, psend, rpart, xs, ad_s, rad, dbuf, rcore, r1, rx, r3, rz,
    lsem,
    sa_s, sa_r, ss_s, ss_r, so_s, so_r, sp_s, sp_r, sz_s, sz_r, sx_s, sx_r, sc_s, sc_r,
    sd_s, sd_r, e_c, e_x, e_y, e_z,
):
    role = lax.axis_index("role")
    req = lax.axis_index("req")
    ctx = lax.axis_index("ctx")
    x = lax.div(req, 2)
    core = lax.rem(req, 2)
    yhi = lax.div(ctx, 8)
    z = lax.rem(ctx, 8)
    y = yhi * 2 + role
    yz = role * 16 + ctx
    me = (role, req, ctx)

    def at_yz(i):
        return (lax.div(i, 16), req, lax.rem(i, 16))

    def at_req(i):
        return (role, i, ctx)

    def at_xy(xo, yo):
        return (lax.rem(yo, 2), xo * 2 + core, lax.div(yo, 2) * 8 + z)

    def at_z(i):
        return (role, req, yhi * 8 + i)

    drains = []

    def finish():
        for d in drains:
            d()

    local = [
        pltpu.make_async_copy(q_h, q_v, lsem.at[0]),
        pltpu.make_async_copy(ck_h, ck_v, lsem.at[1]),
        pltpu.make_async_copy(cv_h, cv_v, lsem.at[2]),
        pltpu.make_async_copy(nk_h, nk_v, lsem.at[3]),
        pltpu.make_async_copy(nv_h, nv_v, lsem.at[4]),
        pltpu.make_async_copy(wo_h, wo_v, lsem.at[5]),
        pltpu.make_async_copy(
            res_h.at[pl.ds(pl.multiple_of(y * 16, 16), 16), pl.ds(pl.multiple_of(z * 128, 128), 128)],
            res_v, lsem.at[6],
        ),
        pltpu.make_async_copy(gain_h, gain_v, lsem.at[7]),
        pltpu.make_async_copy(ad_h, ad_v, lsem.at[8]),
        pltpu.make_async_copy(tu_h, tu_v, lsem.at[9]),
        pltpu.make_async_copy(wg_h, wgu_v.at[:, pl.ds(0, 128)], lsem.at[10]),
        pltpu.make_async_copy(wu_h, wgu_v.at[:, pl.ds(128, 128)], lsem.at[11]),
        pltpu.make_async_copy(wd_h, wd_v, lsem.at[12]),
    ]
    for c in local:
        c.start()

    barrier = pltpu.get_barrier_semaphore()
    loop(1, 32, lambda o: pl.semaphore_signal(
        barrier, inc=1, device_id=at_yz(lax.rem(yz + o, 32)), device_id_type=MESH))
    loop(1, 8, lambda o: pl.semaphore_signal(
        barrier, inc=1, device_id=at_req(lax.rem(req + o, 8)), device_id_type=MESH))

    factor = 1.0 / math.sqrt(HD)
    sub = lax.broadcasted_iota(jnp.int32, (8, 128), 0)
    lane = lax.broadcasted_iota(jnp.int32, (8, 128), 1)
    lens = jnp.zeros((8, 128), jnp.int32)
    for r in range(8):
        lens = jnp.where(sub == r, len_s[r], lens)
    usable = (ctx * 128 + lane < lens)[None]
    rowmod = lax.broadcasted_iota(jnp.int32, (16, 8, 128), 1)
    stat_lane = lax.broadcasted_iota(jnp.int32, (128, 128), 1)
    local[0].wait()
    local[1].wait()
    probs = []
    stat = jnp.zeros((128, 128), F32)
    for k in range(4):
        qk = jnp.concatenate(
            [q_v[:, (k * 16 + g) * 128:(k * 16 + g + 1) * 128].astype(F32) for g in range(16)], axis=0)
        qrows[k * 128:(k + 1) * 128, :] = qk
        kk = ck_v[:, :, k * 128:(k + 1) * 128].reshape(1024, 128)
        full = lax.dot_general(qk.astype(BF16), kk, NT, preferred_element_type=F32)
        sc = jnp.zeros((16, 8, 128), F32)
        for r in range(8):
            sc = jnp.where(rowmod == r, full[:, r * 128:(r + 1) * 128].reshape(16, 8, 128), sc)
        sc = jnp.where(usable, sc * factor, LOW)
        top = jnp.max(sc, axis=-1, keepdims=True)
        w = jnp.where(usable, jnp.exp(sc - top), 0.0)
        wb = w.astype(BF16).astype(F32)
        tot = jnp.sum(wb, axis=-1, keepdims=True)
        probs.append(wb)
        stat = jnp.where(stat_lane == 2 * k, top.reshape(128, 1), stat)
        stat = jnp.where(stat_lane == 2 * k + 1, tot.reshape(128, 1), stat)
    stat_s[...] = stat.T[0:8, :]

    pl.semaphore_wait(barrier, 38)

    def ctx_peer(dh, dz):
        return lax.rem(yhi + dh, 2) * 8 + lax.rem(z + dz, 8)

    def stat_copy(dh, dz):
        return rcopy(stat_s, rstat.at[ctx], ss_s.at[dh * 8 + dz], ss_r.at[ctx], (role, req, ctx_peer(dh, dz)))

    def acc_copy(dh, dz):
        c = ctx_peer(dh, dz)
        return rcopy(acc_s.at[c], racc.at[ctx], sa_s.at[dh * 8 + dz], sa_r.at[ctx], (role, req, c))

    for o in CTX_FAR:
        stat_copy(*o).start()
    rstat[ctx] = stat_s[...]
    local[2].wait()
    for k in range(4):
        big = jnp.concatenate(
            [jnp.where(rowmod == r, probs[k], 0.0).reshape(128, 128).astype(BF16) for r in range(8)], axis=1)
        vk = cv_v[:, :, k * 128:(k + 1) * 128].reshape(1024, 128)
        acc = jnp.dot(big, vk, preferred_element_type=F32)
        acc_s[4 * k:4 * k + 4] = acc.astype(BF16).reshape(4, 32, 128)
    for o in CTX_FAR:
        acc_copy(*o).start()
    racc[ctx] = acc_s[ctx]

    def drain_attn():
        for o in CTX_FAR:
            acc_copy(*o).wait_send()
            stat_copy(*o).wait_send()

    drains.append(drain_attn)

    kh = lax.div(ctx, 4)
    local[3].wait()
    local[4].wait()
    col = pl.ds(pl.multiple_of(kh * 128, 128), 128)
    q32 = qrows[pl.ds(pl.multiple_of(ctx * 32, 32), 32), :].reshape(4, 8, 128)
    nk = nk_v[:, col].astype(F32)
    nv = nv_v[:, col].astype(F32)
    s_self = (jnp.sum(q32 * nk[None], axis=-1, keepdims=True) * factor).reshape(32, 1)
    nv32 = jnp.broadcast_to(nv[None], (4, 8, 128)).reshape(32, 128)

    def wait_stat(o):
        c = lax.rem(ctx + o, 16)
        rcopy(stat_s, rstat.at[c], ss_s.at[o], ss_r.at[c], me).wait_recv()

    def wait_acc(o):
        c = lax.rem(ctx + o, 16)
        rcopy(acc_s.at[c], racc.at[c], sa_s.at[o], sa_r.at[c], me).wait_recv()

    loop(1, 16, wait_stat)
    rt_v[...] = rstat[...].reshape(128, 128).T
    st = rt_v[pl.ds(pl.multiple_of(lax.rem(ctx, 4) * 32, 32), 32), :]
    st = pltpu.roll(st, lax.rem(128 - 2 * kh, 128), 1)
    lane32 = lax.broadcasted_iota(jnp.int32, (32, 128), 1)
    first = lane32 % 8 == 0
    tops = jnp.where(first, st, -3e38)
    high = jnp.maximum(jnp.max(tops, axis=-1, keepdims=True), s_self)
    wgt = jnp.where(first, jnp.exp(tops - high), 0.0)
    w_self = jnp.exp(s_self - high)
    den = jnp.sum(wgt * pltpu.roll(st, 127, 1), axis=-1, keepdims=True) + w_self
    wgt = wgt / den
    o_acc = (w_self / den) * nv32
    loop(1, 16, wait_acc)
    for s in range(16):
        o_acc = o_acc + wgt[:, 8 * s:8 * s + 1] * racc[s].astype(F32)
    ogath[req] = o_acc.astype(BF16)

    def o_copy(dx, dc):
        peer = at_req(lax.rem(x + dx, 4) * 2 + lax.rem(core + dc, 2))
        return rcopy(ogath.at[req], ogath.at[req], so_s.at[dx * 2 + dc], so_r.at[req], peer)

    for o in REQ_FAR:
        o_copy(*o).start()
        drains.append(lambda o=o: o_copy(*o).wait_send())

    def wait_o(o):
        c = lax.rem(req + o, 8)
        rcopy(ogath.at[c], ogath.at[c], so_s.at[o], so_r.at[c], me).wait_recv()

    loop(1, 8, wait_o)
    local[5].wait()
    og = ogath[...].astype(F32)
    attn = jnp.concatenate(
        [og[:, 8 * g:8 * g + 8, :].reshape(64, 128) for g in range(4)], axis=1).astype(BF16)
    proj = jnp.dot(attn, wo_v[...], preferred_element_type=F32)
    for yy in range(4):
        for zz in range(8):
            psend[yy, zz] = proj[16 * yy:16 * yy + 16, 128 * zz:128 * zz + 128].astype(BF16)

    def p_copy(dy, dz):
        yo, zo = lax.rem(y + dy, 4), lax.rem(z + dz, 8)
        return rcopy(psend.at[yo, zo], rpart.at[yz], sp_s.at[dy * 8 + dz], sp_r.at[yz],
                     (lax.rem(yo, 2), req, lax.div(yo, 2) * 8 + zo))

    for o in YZ_FAR:
        p_copy(*o).start()

    def drain_p():
        for o in YZ_FAR:
            p_copy(*o).wait_send()

    drains.append(drain_p)
    rpart[yz] = psend[y, z]

    def wait_p(o):
        c = lax.rem(yz + o, 32)
        rcopy(rpart.at[c], rpart.at[c], sp_s.at[o], sp_r.at[c], me).wait_recv()

    loop(1, 32, wait_p)
    local[6].wait()
    piece = res_v[...].astype(F32) + jnp.sum(rpart[...].astype(F32), axis=0)
    rows_y = pl.ds(pl.multiple_of(y * 16, 16), 16)
    xs[req * 8 + z, rows_y, :] = piece.astype(BF16)

    def z_ref(i):
        return xs.at[req * 8 + i, rows_y]

    def z_copy(o):
        return rcopy(z_ref(z), z_ref(z), sz_s.at[o], sz_r.at[z], at_z(lax.rem(z + o, 8)))

    for o in Z_FAR:
        z_copy(o).start()
        drains.append(lambda o=o: z_copy(o).wait_send())

    def wait_z(o):
        c = lax.rem(z + o, 8)
        rcopy(z_ref(c), z_ref(c), sz_s.at[o], sz_r.at[c], me).wait_recv()

    loop(1, 8, wait_z)

    def y_ref(b, yo):
        return xs.at[pl.ds(b * 8, 8), pl.ds(pl.multiple_of(yo * 16, 16), 16)]

    def xy_copy(dx, dy):
        return rcopy(y_ref(req, y), y_ref(req, y), sx_s.at[dx, dy], sx_r.at[x, y],
                     at_xy(lax.rem(x + dx, 4), lax.rem(y + dy, 4)))

    def xy_wait(dx, dy):
        xo, yo = lax.rem(x + dx, 4), lax.rem(y + dy, 4)
        ref = y_ref(xo * 2 + core, yo)
        rcopy(ref, ref, sx_s.at[dx, dy], sx_r.at[xo, yo], me).wait_recv()

    for o in XY_FAR:
        xy_copy(*o).start()
        drains.append(lambda o=o: xy_copy(*o).wait_send())

    def b_ref(b):
        return xs.at[pl.ds(b * 8, 8)]

    def c_copy(o):
        b = lax.rem(x + o, 4) * 2 + core
        return rcopy(b_ref(b), b_ref(b), sc_s.at[o], sc_r.at[lax.rem(x + o, 4)], at_req(x * 2 + 1 - core))

    for dy in (1, 3, 2):
        xy_wait(0, dy)
    c_copy(0).start()
    drains.append(lambda: c_copy(0).wait_send())
    local[7].wait()
    local[8].wait()
    local[10].wait()
    local[11].wait()

    def block(b):
        xb = xs[pl.ds(b * 8, 8)].astype(F32)
        sq = jnp.sum(jnp.sum(xb * xb, axis=0), axis=-1, keepdims=True)
        xg = xb * gain_v[pl.ds(pl.multiple_of(b * 8, 8), 8), :][:, None, :]
        xg = jnp.concatenate([xg[i] for i in range(8)], axis=1).astype(BF16)
        return sq, xg

    def gate_up(b, xg):
        rows = pl.ds(pl.multiple_of(b * 1024, 1024), 1024)
        return jnp.dot(xg, wgu_v[rows, :], preferred_element_type=F32)

    sq, xg = block(req)
    mid = jnp.dot(xg, ad_v[...], preferred_element_type=F32)
    owner = lax.div(lane, 16)
    tens = []
    packed = jnp.zeros((8, 128), F32)
    for i in range(8):
        t = jnp.zeros((8, 128), jnp.int32)
        for r in range(8):
            t = jnp.where(sub == r, ten_s[8 * i + r], t)
        tens.append(t)
        v = (jnp.where(owner == t, mid[8 * i:8 * i + 8, 0:128], 0.0)
             + jnp.where(owner + 8 == t, mid[8 * i:8 * i + 8, 128:256], 0.0))
        v = v + pltpu.roll(v, 64, 1)
        v = v + pltpu.roll(v, 32, 1)
        v = v + pltpu.roll(v, 16, 1)
        packed = jnp.where(owner == i, v, packed)
    ad_s[...] = packed

    def d_copy(dx, dc):
        peer = at_req(lax.rem(x + dx, 4) * 2 + lax.rem(core + dc, 2))
        return rcopy(ad_s, rad.at[req], sd_s.at[dx * 2 + dc], sd_r.at[req], peer)

    for o in REQ_FAR:
        d_copy(*o).start()
        drains.append(lambda o=o: d_copy(*o).wait_send())
    rad[req] = packed
    gu = gate_up(req, xg)
    for o in (0, 1, 3, 2):
        xo = lax.rem(x + o, 4)
        if o > 0:
            b = xo * 2 + core
            for dy in (0, 1, 3, 2):
                xy_wait(o, dy)
            c_copy(o).start()
            drains.append(lambda o=o: c_copy(o).wait_send())
            s1, xg = block(b)
            sq = sq + s1
            gu = gu + gate_up(b, xg)
        b = xo * 2 + 1 - core
        rcopy(b_ref(b), b_ref(b), sc_s.at[o], sc_r.at[xo], me).wait_recv()
        s1, xg = block(b)
        sq = sq + s1
        gu = gu + gate_up(b, xg)

    def wait_d(o):
        c = lax.rem(req + o, 8)
        rcopy(ad_s, rad.at[c], sd_s.at[o], sd_r.at[c], me).wait_recv()

    loop(1, 8, wait_d)
    inv = lax.rsqrt(sq * (1.0 / 8192.0) + EPS)
    allmid = jnp.sum(rad[...], axis=0)
    chosen = []
    for i in range(8):
        v = jnp.where(owner == i, allmid, 0.0)
        v = v + pltpu.roll(v, 64, 1)
        v = v + pltpu.roll(v, 32, 1)
        v = v + pltpu.roll(v, 16, 1)
        v = v * inv[8 * i:8 * i + 8]
        chosen.append(jnp.concatenate(
            [jnp.where(owner == tens[i], v, 0.0), jnp.where(owner + 8 == tens[i], v, 0.0)], axis=1))
    local[9].wait()
    lowrank = jnp.dot(jnp.concatenate(chosen, axis=0).astype(BF16), tu_v[...], preferred_element_type=F32)
    gate = gu[:, 0:128] * inv
    up = gu[:, 128:256] * inv + 2.0 * lowrank
    hid = (gate / (1.0 + jnp.exp(-gate)) * up).astype(BF16)

    local[12].wait()
    for p in range(32):
        rr, cc = p // 16, p % 16
        yy, zz = (cc // 8) * 2 + rr, cc % 8
        part = jnp.dot(hid, wd_v[:, 256 * p:256 * p + 256], preferred_element_type=F32)
        for b in range(8):
            dbuf[b % 2, b // 2, yy, zz] = jnp.concatenate(
                [part[8 * b:8 * b + 8, 0:128], part[8 * b:8 * b + 8, 128:256]], axis=0).astype(BF16)

    core_copy = rcopy(dbuf.at[1 - core], rcore, e_c.at[0], e_c.at[1], at_req(x * 2 + 1 - core))
    core_copy.start()
    drains.append(core_copy.wait_send)
    core_copy.wait_recv()

    def fold_core(i):
        r1[i] = (dbuf[core, i].astype(F32) + rcore[i].astype(F32)).astype(BF16)

    loop(0, 4, fold_core)

    def ex_copy(dx, dy):
        xo, yo = lax.rem(x + dx, 4), lax.rem(y + dy, 4)
        return rcopy(r1.at[xo, yo], rx.at[x, y], e_x.at[dx, dy], e_y.at[x, y], at_xy(xo, yo))

    for o in XY_FAR:
        ex_copy(*o).start()
        drains.append(lambda o=o: ex_copy(*o).wait_send())
    rx[x, y] = r1[x, y]

    def wait_ex(o):
        i = lax.rem(x * 4 + y + o, 16)
        xo, yo = lax.div(i, 4), lax.rem(i, 4)
        rcopy(r1.at[xo, yo], rx.at[xo, yo], e_x.at[xo, yo], e_y.at[xo, yo], me).wait_recv()

    loop(1, 16, wait_ex)

    def fold_xy(i):
        part = rx[0, 0, i].astype(F32)
        for j in range(1, 16):
            part = part + rx[j // 4, j % 4, i].astype(F32)
        r3[i] = part.astype(BF16)

    loop(0, 8, fold_xy)

    def ez_copy(o):
        zo = lax.rem(z + o, 8)
        return rcopy(r3.at[zo], rz.at[z], e_z.at[o], e_z.at[8 + z], at_z(zo))

    for o in Z_FAR:
        ez_copy(o).start()
        drains.append(lambda o=o: ez_copy(o).wait_send())
    rz[z] = r3[z]

    def wait_ez(o):
        zo = lax.rem(z + o, 8)
        rcopy(r3.at[zo], rz.at[zo], e_z.at[o], e_z.at[8 + zo], me).wait_recv()

    loop(1, 8, wait_ez)
    own = xs[pl.ds(yz * 2, 2), pl.ds(pl.multiple_of(x * 16, 16), 16), :].astype(F32)
    own = jnp.where(core == 0, own[:, 0:8, :], own[:, 8:16, :])
    res = own.reshape(16, 128) + jnp.sum(rz[...].astype(F32), axis=0)
    out_ref[:, 0:128] = res[0:8, :].astype(BF16)
    out_ref[:, 128:256] = res[8:16, :].astype(BF16)
    finish()


def shards(query, cache_keys, cache_values, new_keys, new_values, lengths, residual_in, out_proj,
           norm_gain, adapter_down, tenant_adapter_up_matrix, tenant, w_gate, w_up, w_down):
    hbm = pl.BlockSpec(memory_space=pl.ANY)
    smem = pl.BlockSpec(memory_space=pltpu.SMEM)
    v = pltpu.VMEM
    dma = pltpu.SemaphoreType.DMA
    return pl.pallas_call(
        functools.partial(kernel, None),
        out_shape=jax.ShapeDtypeStruct((8, 256), BF16),
        in_specs=[hbm, hbm, hbm, hbm, hbm, smem, hbm, hbm, hbm, hbm, hbm, smem, hbm, hbm, hbm],
        out_specs=pl.BlockSpec(memory_space=pltpu.VMEM),
        scratch_shapes=[
            v((8, 8192), BF16), v((8, 128, 512), BF16), v((8, 128, 512), BF16), v((8, 512), BF16),
            v((8, 512), BF16), v((16, 128), BF16), v((512, 1024), BF16), v((64, 128), F32),
            v((1024, 256), BF16), v((256, 128), BF16), v((8192, 256), BF16), v((128, 8192), BF16),
            v((512, 128), F32), v((16, 32, 128), BF16), v((8, 128), F32), v((16, 32, 128), BF16),
            v((16, 8, 128), F32), v((128, 128), F32),
            v((8, 32, 128), BF16), v((4, 8, 16, 128), BF16), v((32, 16, 128), BF16), v((64, 64, 128), BF16),
            v((8, 128), F32), v((8, 8, 128), F32),
            v((2, 4, 4, 8, 16, 128), BF16), v((4, 4, 8, 16, 128), BF16), v((4, 4, 8, 16, 128), BF16),
            v((4, 4, 8, 16, 128), BF16), v((8, 16, 128), BF16), v((8, 16, 128), BF16),
            dma((13,)),
            dma((16,)), dma((16,)), dma((16,)), dma((16,)), dma((8,)), dma((8,)), dma((32,)), dma((32,)),
            dma((8,)), dma((8,)), dma((4, 4)), dma((4, 4)), dma((4,)), dma((4,)),
            dma((8,)), dma((8,)), dma((2,)), dma((4, 4)), dma((4, 4)), dma((16,)),
        ],
        compiler_params=pltpu.CompilerParams(
            collective_id=0, has_side_effects=True, vmem_limit_bytes=60 * 1024 * 1024),
    )(query, cache_keys, cache_values, new_keys, new_values, lengths, residual_in, out_proj,
      norm_gain.reshape(64, 128), adapter_down, tenant_adapter_up_matrix, tenant, w_gate, w_up, w_down)


def solution(mesh):
    placed = (
        P("req", "role"),
        P("req", "ctx", "role"),
        P("req", "ctx", "role"),
        P("req", "role"),
        P("req", "role"),
        P("req"),
        P(None, "req"),
        P(("role", "ctx"), "req"),
        P(),
        P("req", None),
        P(None, ("role", "req", "ctx")),
        P(),
        P(None, ("role", "req", "ctx")),
        P(None, ("role", "req", "ctx")),
        P(("role", "req", "ctx"), None),
    )
    return jax.shard_map(
        shards, mesh=mesh, in_specs=placed, out_specs=P("req", ("role", "ctx")), check_vma=False
    )
```

```python
import functools
import math

import jax
import jax.numpy as jnp
from jax import lax
from jax.experimental import pallas as pl
from jax.experimental.pallas import tpu as pltpu
from jax.sharding import PartitionSpec as P

MESH = pl.DeviceIdType.MESH
F32 = jnp.float32
BF16 = jnp.bfloat16
HD = 128
EPS = 1e-05
LOW = -1e30
NT = (((1,), (1,)), ((), ()))
Z_FAR = (4, 3, 5, 2, 6, 1, 7)
XY_FAR = ((2, 2), (1, 2), (3, 2), (2, 1), (2, 3), (1, 1), (1, 3), (3, 1), (3, 3),
          (2, 0), (0, 2), (1, 0), (3, 0), (0, 1), (0, 3))
YZ_FAR = tuple((dy, dz) for dz in Z_FAR + (0,) for dy in (2, 1, 3, 0) if dy or dz)
HALF_FAR = tuple((dx, dc, dh) for dh in (1, 0) for dx in (2, 1, 3, 0) for dc in (1, 0) if dx or dc or dh)
REQ_FAR = ((2, 1), (2, 0), (1, 1), (3, 1), (1, 0), (3, 0), (0, 1))


def rcopy(src, dst, ssem, rsem, dev):
    return pltpu.make_async_remote_copy(
        src_ref=src, dst_ref=dst, send_sem=ssem, recv_sem=rsem, device_id=dev, device_id_type=MESH
    )


def loop(lo, hi, body):
    def step(i, carry):
        body(i)
        return carry

    lax.fori_loop(lo, hi, step, 0)


def kernel(
    stop,
    q_h, ck_h, cv_h, nk_h, nv_h, len_s, res_h, wo_h, gain_h, ad_h, tu_h, ten_s, wg_h, wu_h, wd_h,
    out_ref,
    q_v, ck_v, cv_v, nk_v, nv_v, res_v, wo_v, gain_v, ad_v, tu_v, wgu_v, wd_v,
    acc_s, stat_s, racc, rstat, rt_v, lse_s, oh_s, rl,
    ogath, psend, rpart, xs, ad_s, rad, dbuf, rcore, r1, rx, r3, rz,
    lsem,
    go, sa_s, sa_r, ss_s, ss_r, sl_s, sl_r, so_s, so_r, sp_s, sp_r, sz_s, sz_r, sx_s, sx_r, sc_s, sc_r,
    sd_s, sd_r, e_c, e_x, e_y, e_z,
):
    role = lax.axis_index("role")
    req = lax.axis_index("req")
    ctx = lax.axis_index("ctx")
    x = lax.div(req, 2)
    core = lax.rem(req, 2)
    yhi = lax.div(ctx, 8)
    z = lax.rem(ctx, 8)
    y = yhi * 2 + role
    yz = role * 16 + ctx
    me = (role, req, ctx)

    def at_req(i):
        return (role, i, ctx)

    def at_xy(xo, yo):
        return (lax.rem(yo, 2), xo * 2 + core, lax.div(yo, 2) * 8 + z)

    def at_y(i):
        return (lax.rem(i, 2), req, lax.div(i, 2) * 8 + z)

    def at_z(i):
        return (role, req, yhi * 8 + i)

    drains = []

    def finish():
        for d in drains:
            d()

    local = [
        pltpu.make_async_copy(q_h, q_v, lsem.at[0]),
        pltpu.make_async_copy(ck_h, ck_v, lsem.at[1]),
        pltpu.make_async_copy(cv_h, cv_v, lsem.at[2]),
        pltpu.make_async_copy(nk_h, nk_v, lsem.at[3]),
        pltpu.make_async_copy(nv_h, nv_v, lsem.at[4]),
        pltpu.make_async_copy(wo_h, wo_v, lsem.at[5]),
        pltpu.make_async_copy(
            res_h.at[pl.ds(pl.multiple_of(y * 16, 16), 16), pl.ds(pl.multiple_of(z * 128, 128), 128)],
            res_v, lsem.at[6],
        ),
        pltpu.make_async_copy(gain_h, gain_v, lsem.at[7]),
        pltpu.make_async_copy(ad_h, ad_v, lsem.at[8]),
        pltpu.make_async_copy(tu_h, tu_v, lsem.at[9]),
        pltpu.make_async_copy(wg_h, wgu_v.at[:, pl.ds(0, 128)], lsem.at[10]),
        pltpu.make_async_copy(wu_h, wgu_v.at[:, pl.ds(128, 128)], lsem.at[11]),
        pltpu.make_async_copy(wd_h, wd_v, lsem.at[12]),
    ]
    for i in (0, 1, 3, 2, 4, 5, 6, 7, 8, 9, 10, 11, 12):
        local[i].start()

    barrier = pltpu.get_barrier_semaphore()

    def greet(dev):
        pl.semaphore_signal(barrier, inc=1, device_id=dev, device_id_type=MESH)

    for o in Z_FAR:
        greet(at_z(lax.rem(z + o, 8)))
    for dx, dc in REQ_FAR:
        greet(at_req(lax.rem(x + dx, 4) * 2 + lax.rem(core + dc, 2)))
    for o in (2, 1, 3):
        greet(at_y(lax.rem(y + o, 4)))

    factor = 1.0 / math.sqrt(HD)
    sub = lax.broadcasted_iota(jnp.int32, (8, 128), 0)
    lane = lax.broadcasted_iota(jnp.int32, (8, 128), 1)
    lens = jnp.zeros((8, 128), jnp.int32)
    for r in range(8):
        lens = jnp.where(sub == r, len_s[r], lens)
    usable = (ctx * 128 + lane < lens)[None]
    rowmod = lax.broadcasted_iota(jnp.int32, (16, 8, 128), 1)
    stat_lane = lax.broadcasted_iota(jnp.int32, (128, 128), 1)
    local[0].wait()
    local[1].wait()
    local[3].wait()
    probs = []
    fresh = []
    stat = jnp.zeros((128, 128), F32)
    for k in range(4):
        qk = jnp.concatenate(
            [q_v[:, (k * 16 + g) * 128:(k * 16 + g + 1) * 128].astype(F32) for g in range(16)], axis=0)
        nk = nk_v[:, k * 128:(k + 1) * 128].astype(F32)
        own = jnp.sum(qk.reshape(16, 8, 128) * nk[None], axis=-1, keepdims=True) * factor
        own = jnp.where(ctx == 0, own, LOW)
        kk = ck_v[:, :, k * 128:(k + 1) * 128].reshape(1024, 128)
        full = lax.dot_general(qk.astype(BF16), kk, NT, preferred_element_type=F32)
        sc = jnp.zeros((16, 8, 128), F32)
        for r in range(8):
            sc = jnp.where(rowmod == r, full[:, r * 128:(r + 1) * 128].reshape(16, 8, 128), sc)
        sc = jnp.where(usable, sc * factor, LOW)
        top = jnp.maximum(jnp.max(sc, axis=-1, keepdims=True), own)
        w = jnp.where(usable, jnp.exp(sc - top), 0.0)
        wb = w.astype(BF16).astype(F32)
        w_own = jnp.where(ctx == 0, jnp.exp(own - top), 0.0)
        tot = jnp.sum(wb, axis=-1, keepdims=True) + w_own
        probs.append(wb)
        fresh.append(w_own)
        stat = jnp.where(stat_lane == 2 * k, top.reshape(128, 1), stat)
        stat = jnp.where(stat_lane == 2 * k + 1, tot.reshape(128, 1), stat)
    stat_s[...] = stat.T[0:8, :]

    pl.semaphore_wait(barrier, 17)
    for o in (2, 1, 3):
        pl.semaphore_signal(go, inc=1, device_id=at_y(lax.rem(y + o, 4)), device_id_type=MESH)

    def stat_copy(o):
        return rcopy(stat_s, rstat.at[z], ss_s.at[o], ss_r.at[z], at_z(lax.rem(z + o, 8)))

    def acc_copy(o):
        zo = lax.rem(z + o, 8)
        return rcopy(acc_s.at[:, zo], racc.at[z], sa_s.at[o], sa_r.at[z], at_z(zo))

    for o in Z_FAR:
        stat_copy(o).start()
        drains.append(lambda o=o: stat_copy(o).wait_send())
    rstat[z] = stat_s[...]
    local[2].wait()
    local[4].wait()
    for k in range(4):
        big = jnp.concatenate(
            [jnp.where(rowmod == r, probs[k], 0.0).reshape(128, 128).astype(BF16) for r in range(8)], axis=1)
        vk = cv_v[:, :, k * 128:(k + 1) * 128].reshape(1024, 128)
        acc = jnp.dot(big, vk, preferred_element_type=F32).reshape(16, 8, 128)
        acc = acc + fresh[k] * nv_v[:, k * 128:(k + 1) * 128].astype(F32)[None]
        acc_s[k // 2, (k % 2) * 4:(k % 2) * 4 + 4] = acc.reshape(4, 32, 128).astype(BF16)
    for o in Z_FAR:
        acc_copy(o).start()
        drains.append(lambda o=o: acc_copy(o).wait_send())
    for j in range(2):
        racc[z, j] = acc_s[j, z]

    def wait_stat(o):
        c = lax.rem(z + o, 8)
        rcopy(stat_s, rstat.at[c], ss_s.at[o], ss_r.at[c], me).wait_recv()

    def wait_acc(o):
        c = lax.rem(z + o, 8)
        rcopy(racc.at[c], racc.at[c], sa_s.at[o], sa_r.at[c], me).wait_recv()

    loop(1, 8, wait_stat)
    rs = rstat[...]
    high = jnp.max(rs, axis=0)
    scale = jnp.exp(rs - high[None])
    den = jnp.maximum(jnp.sum(scale * pltpu.roll(rs, 7, 1), axis=0), 1e-30)
    lse = high + jnp.log(den)
    lse_s[...] = lse
    flat = (scale / den[None]).reshape(64, 128)
    rt_v[...] = jnp.concatenate([flat, flat], axis=0).T
    kz = lax.div(z, 4)
    rows_z = pl.ds(pl.multiple_of(lax.rem(z, 4) * 32, 32), 32)
    st = rt_v[rows_z, :]
    st = jnp.where(kz == 0, st, pltpu.roll(st, 126, 1))
    loop(1, 8, wait_acc)
    for j in range(2):
        part = jnp.zeros((32, 128), F32)
        for c in range(8):
            part = part + st[:, 8 * c + 4 * j:8 * c + 4 * j + 1] * racc[c, j].astype(F32)
        oh_s[j] = part.astype(BF16)

    def h_peer(dx, dc, dh):
        return lax.rem(yhi + dh, 2), lax.rem(x + dx, 4) * 2 + lax.rem(core + dc, 2)

    def l_copy(dx, dc, dh):
        h, b = h_peer(dx, dc, dh)
        return rcopy(lse_s, rl.at[yhi, req], sl_s.at[dh, dx * 2 + dc], sl_r.at[yhi, req], (role, b, h * 8 + z))

    def o_copy(dx, dc, dh):
        h, b = h_peer(dx, dc, dh)
        return rcopy(oh_s.at[h], ogath.at[yhi, req], so_s.at[dh, dx * 2 + dc], so_r.at[yhi, req],
                     (role, b, h * 8 + z))

    pl.semaphore_wait(go, 3)
    for o in HALF_FAR:
        o_copy(*o).start()
        l_copy(*o).start()

    def drain_o():
        for o in HALF_FAR:
            o_copy(*o).wait_send()
            l_copy(*o).wait_send()

    drains.append(drain_o)
    ogath[yhi, req] = oh_s[yhi]
    rl[yhi, req] = lse

    def wait_l(o):
        i = lax.rem(yhi * 8 + req + o, 16)
        h, b = lax.div(i, 8), lax.rem(i, 8)
        rcopy(rl.at[h, b], rl.at[h, b], sl_s.at[h, b], sl_r.at[h, b], me).wait_recv()

    def wait_o(o):
        i = lax.rem(yhi * 8 + req + o, 16)
        h, b = lax.div(i, 8), lax.rem(i, 8)
        rcopy(ogath.at[h, b], ogath.at[h, b], so_s.at[h, b], so_r.at[h, b], me).wait_recv()

    loop(1, 16, wait_l)
    gap = rl[1] - rl[0]
    both = jnp.concatenate(
        [(1.0 / (1.0 + jnp.exp(gap))).reshape(64, 128), (1.0 / (1.0 + jnp.exp(-gap))).reshape(64, 128)], axis=0)
    rt_v[...] = both.T
    st = pltpu.roll(rt_v[rows_z, :], lax.rem(128 - 4 * yhi - 2 * kz, 128), 1)
    loop(1, 16, wait_o)
    heads = []
    for b in range(8):
        heads.append(st[:, 8 * b:8 * b + 1] * ogath[0, b].astype(F32)
                     + st[:, 64 + 8 * b:64 + 8 * b + 1] * ogath[1, b].astype(F32))
    attn = jnp.concatenate(
        [jnp.concatenate([heads[b][8 * g:8 * g + 8, :] for b in range(8)], axis=0) for g in range(4)],
        axis=1).astype(BF16)
    local[5].wait()
    proj = jnp.dot(attn, wo_v[...], preferred_element_type=F32)
    for yy in range(4):
        for zz in range(8):
            psend[yy, zz] = proj[16 * yy:16 * yy + 16, 128 * zz:128 * zz + 128].astype(BF16)

    def p_copy(dy, dz):
        yo, zo = lax.rem(y + dy, 4), lax.rem(z + dz, 8)
        return rcopy(psend.at[yo, zo], rpart.at[yz], sp_s.at[dy * 8 + dz], sp_r.at[yz],
                     (lax.rem(yo, 2), req, lax.div(yo, 2) * 8 + zo))

    for o in YZ_FAR:
        p_copy(*o).start()

    def drain_p():
        for o in YZ_FAR:
            p_copy(*o).wait_send()

    drains.append(drain_p)
    rpart[yz] = psend[y, z]

    def wait_p(o):
        c = lax.rem(yz + o, 32)
        rcopy(rpart.at[c], rpart.at[c], sp_s.at[o], sp_r.at[c], me).wait_recv()

    loop(1, 32, wait_p)
    local[6].wait()
    piece = res_v[...].astype(F32) + jnp.sum(rpart[...].astype(F32), axis=0)
    rows_y = pl.ds(pl.multiple_of(y * 16, 16), 16)
    xs[req * 8 + z, rows_y, :] = piece.astype(BF16)

    def z_ref(i):
        return xs.at[req * 8 + i, rows_y]

    def z_copy(o):
        return rcopy(z_ref(z), z_ref(z), sz_s.at[o], sz_r.at[z], at_z(lax.rem(z + o, 8)))

    for o in Z_FAR:
        z_copy(o).start()
        drains.append(lambda o=o: z_copy(o).wait_send())

    def wait_z(o):
        c = lax.rem(z + o, 8)
        rcopy(z_ref(c), z_ref(c), sz_s.at[o], sz_r.at[c], me).wait_recv()

    loop(1, 8, wait_z)

    def y_ref(b, yo):
        return xs.at[pl.ds(b * 8, 8), pl.ds(pl.multiple_of(yo * 16, 16), 16)]

    def xy_copy(dx, dy):
        return rcopy(y_ref(req, y), y_ref(req, y), sx_s.at[dx, dy], sx_r.at[x, y],
                     at_xy(lax.rem(x + dx, 4), lax.rem(y + dy, 4)))

    def xy_wait(dx, dy):
        xo, yo = lax.rem(x + dx, 4), lax.rem(y + dy, 4)
        ref = y_ref(xo * 2 + core, yo)
        rcopy(ref, ref, sx_s.at[dx, dy], sx_r.at[xo, yo], me).wait_recv()

    for o in XY_FAR:
        xy_copy(*o).start()
        drains.append(lambda o=o: xy_copy(*o).wait_send())

    def b_ref(b):
        return xs.at[pl.ds(b * 8, 8)]

    def c_copy(o):
        b = lax.rem(x + o, 4) * 2 + core
        return rcopy(b_ref(b), b_ref(b), sc_s.at[o], sc_r.at[lax.rem(x + o, 4)], at_req(x * 2 + 1 - core))

    for dy in (1, 3, 2):
        xy_wait(0, dy)
    c_copy(0).start()
    drains.append(lambda: c_copy(0).wait_send())
    local[7].wait()
    local[8].wait()
    local[10].wait()
    local[11].wait()

    def block(b):
        xb = xs[pl.ds(b * 8, 8)].astype(F32)
        sq = jnp.sum(jnp.sum(xb * xb, axis=0), axis=-1, keepdims=True)
        xg = xb * gain_v[pl.ds(pl.multiple_of(b * 8, 8), 8), :][:, None, :]
        xg = jnp.concatenate([xg[i] for i in range(8)], axis=1).astype(BF16)
        return sq, xg

    def gate_up(b, xg):
        rows = pl.ds(pl.multiple_of(b * 1024, 1024), 1024)
        return jnp.dot(xg, wgu_v[rows, :], preferred_element_type=F32)

    sq, xg = block(req)
    mid = jnp.dot(xg, ad_v[...], preferred_element_type=F32)
    owner = lax.div(lane, 16)
    tens = []
    packed = jnp.zeros((8, 128), F32)
    for i in range(8):
        t = jnp.zeros((8, 128), jnp.int32)
        for r in range(8):
            t = jnp.where(sub == r, ten_s[8 * i + r], t)
        tens.append(t)
        v = (jnp.where(owner == t, mid[8 * i:8 * i + 8, 0:128], 0.0)
             + jnp.where(owner + 8 == t, mid[8 * i:8 * i + 8, 128:256], 0.0))
        v = v + pltpu.roll(v, 64, 1)
        v = v + pltpu.roll(v, 32, 1)
        v = v + pltpu.roll(v, 16, 1)
        packed = jnp.where(owner == i, v, packed)
    ad_s[...] = packed

    def d_copy(dx, dc):
        peer = at_req(lax.rem(x + dx, 4) * 2 + lax.rem(core + dc, 2))
        return rcopy(ad_s, rad.at[req], sd_s.at[dx * 2 + dc], sd_r.at[req], peer)

    for o in REQ_FAR:
        d_copy(*o).start()
        drains.append(lambda o=o: d_copy(*o).wait_send())
    rad[req] = packed
    gu = gate_up(req, xg)
    for o in (0, 1, 3, 2):
        xo = lax.rem(x + o, 4)
        if o > 0:
            b = xo * 2 + core
            for dy in (0, 1, 3, 2):
                xy_wait(o, dy)
            c_copy(o).start()
            drains.append(lambda o=o: c_copy(o).wait_send())
            s1, xg = block(b)
            sq = sq + s1
            gu = gu + gate_up(b, xg)
        b = xo * 2 + 1 - core
        rcopy(b_ref(b), b_ref(b), sc_s.at[o], sc_r.at[xo], me).wait_recv()
        s1, xg = block(b)
        sq = sq + s1
        gu = gu + gate_up(b, xg)

    def wait_d(o):
        c = lax.rem(req + o, 8)
        rcopy(ad_s, rad.at[c], sd_s.at[o], sd_r.at[c], me).wait_recv()

    loop(1, 8, wait_d)
    inv = lax.rsqrt(sq * (1.0 / 8192.0) + EPS)
    allmid = jnp.sum(rad[...], axis=0)
    chosen = []
    for i in range(8):
        v = jnp.where(owner == i, allmid, 0.0)
        v = v + pltpu.roll(v, 64, 1)
        v = v + pltpu.roll(v, 32, 1)
        v = v + pltpu.roll(v, 16, 1)
        v = v * inv[8 * i:8 * i + 8]
        chosen.append(jnp.concatenate(
            [jnp.where(owner == tens[i], v, 0.0), jnp.where(owner + 8 == tens[i], v, 0.0)], axis=1))
    local[9].wait()
    lowrank = jnp.dot(jnp.concatenate(chosen, axis=0).astype(BF16), tu_v[...], preferred_element_type=F32)
    gate = gu[:, 0:128] * inv
    up = gu[:, 128:256] * inv + 2.0 * lowrank
    hid = (gate / (1.0 + jnp.exp(-gate)) * up).astype(BF16)

    local[12].wait()
    for p in range(32):
        rr, cc = p // 16, p % 16
        yy, zz = (cc // 8) * 2 + rr, cc % 8
        part = jnp.dot(hid, wd_v[:, 256 * p:256 * p + 256], preferred_element_type=F32)
        for b in range(8):
            dbuf[b % 2, b // 2, yy, zz] = jnp.concatenate(
                [part[8 * b:8 * b + 8, 0:128], part[8 * b:8 * b + 8, 128:256]], axis=0).astype(BF16)

    core_copy = rcopy(dbuf.at[1 - core], rcore, e_c.at[0], e_c.at[1], at_req(x * 2 + 1 - core))
    core_copy.start()
    drains.append(core_copy.wait_send)
    core_copy.wait_recv()

    def fold_core(i):
        r1[i] = (dbuf[core, i].astype(F32) + rcore[i].astype(F32)).astype(BF16)

    loop(0, 4, fold_core)

    def ex_copy(dx, dy):
        xo, yo = lax.rem(x + dx, 4), lax.rem(y + dy, 4)
        return rcopy(r1.at[xo, yo], rx.at[x, y], e_x.at[dx, dy], e_y.at[x, y], at_xy(xo, yo))

    for o in XY_FAR:
        ex_copy(*o).start()
        drains.append(lambda o=o: ex_copy(*o).wait_send())
    rx[x, y] = r1[x, y]

    def wait_ex(o):
        i = lax.rem(x * 4 + y + o, 16)
        xo, yo = lax.div(i, 4), lax.rem(i, 4)
        rcopy(r1.at[xo, yo], rx.at[xo, yo], e_x.at[xo, yo], e_y.at[xo, yo], me).wait_recv()

    loop(1, 16, wait_ex)

    def fold_xy(i):
        part = rx[0, 0, i].astype(F32)
        for j in range(1, 16):
            part = part + rx[j // 4, j % 4, i].astype(F32)
        r3[i] = part.astype(BF16)

    loop(0, 8, fold_xy)

    def ez_copy(o):
        zo = lax.rem(z + o, 8)
        return rcopy(r3.at[zo], rz.at[z], e_z.at[o], e_z.at[8 + z], at_z(zo))

    for o in Z_FAR:
        ez_copy(o).start()
        drains.append(lambda o=o: ez_copy(o).wait_send())
    rz[z] = r3[z]

    def wait_ez(o):
        zo = lax.rem(z + o, 8)
        rcopy(r3.at[zo], rz.at[zo], e_z.at[o], e_z.at[8 + zo], me).wait_recv()

    loop(1, 8, wait_ez)
    own = xs[pl.ds(yz * 2, 2), pl.ds(pl.multiple_of(x * 16, 16), 16), :].astype(F32)
    own = jnp.where(core == 0, own[:, 0:8, :], own[:, 8:16, :])
    res = own.reshape(16, 128) + jnp.sum(rz[...].astype(F32), axis=0)
    out_ref[:, 0:128] = res[0:8, :].astype(BF16)
    out_ref[:, 128:256] = res[8:16, :].astype(BF16)
    finish()


def shards(query, cache_keys, cache_values, new_keys, new_values, lengths, residual_in, out_proj,
           norm_gain, adapter_down, tenant_adapter_up_matrix, tenant, w_gate, w_up, w_down):
    hbm = pl.BlockSpec(memory_space=pl.ANY)
    smem = pl.BlockSpec(memory_space=pltpu.SMEM)
    v = pltpu.VMEM
    dma = pltpu.SemaphoreType.DMA
    return pl.pallas_call(
        functools.partial(kernel, None),
        out_shape=jax.ShapeDtypeStruct((8, 256), BF16),
        in_specs=[hbm, hbm, hbm, hbm, hbm, smem, hbm, hbm, hbm, hbm, hbm, smem, hbm, hbm, hbm],
        out_specs=pl.BlockSpec(memory_space=pltpu.VMEM),
        scratch_shapes=[
            v((8, 8192), BF16), v((8, 128, 512), BF16), v((8, 128, 512), BF16), v((8, 512), BF16),
            v((8, 512), BF16), v((16, 128), BF16), v((512, 1024), BF16), v((64, 128), F32),
            v((1024, 256), BF16), v((256, 128), BF16), v((8192, 256), BF16), v((128, 8192), BF16),
            v((2, 8, 32, 128), BF16), v((8, 128), F32), v((8, 2, 32, 128), BF16), v((8, 8, 128), F32),
            v((128, 128), F32), v((8, 128), F32), v((2, 32, 128), BF16), v((2, 8, 8, 128), F32),
            v((2, 8, 32, 128), BF16), v((4, 8, 16, 128), BF16), v((32, 16, 128), BF16), v((64, 64, 128), BF16),
            v((8, 128), F32), v((8, 8, 128), F32),
            v((2, 4, 4, 8, 16, 128), BF16), v((4, 4, 8, 16, 128), BF16), v((4, 4, 8, 16, 128), BF16),
            v((4, 4, 8, 16, 128), BF16), v((8, 16, 128), BF16), v((8, 16, 128), BF16),
            dma((13,)),
            pltpu.SemaphoreType.REGULAR, dma((8,)), dma((8,)), dma((8,)), dma((8,)),
            dma((2, 8)), dma((2, 8)), dma((2, 8)), dma((2, 8)), dma((32,)), dma((32,)),
            dma((8,)), dma((8,)), dma((4, 4)), dma((4, 4)), dma((4,)), dma((4,)),
            dma((8,)), dma((8,)), dma((2,)), dma((4, 4)), dma((4, 4)), dma((16,)),
        ],
        compiler_params=pltpu.CompilerParams(
            collective_id=0, has_side_effects=True, vmem_limit_bytes=60 * 1024 * 1024),
    )(query, cache_keys, cache_values, new_keys, new_values, lengths, residual_in, out_proj,
      norm_gain.reshape(64, 128), adapter_down, tenant_adapter_up_matrix, tenant, w_gate, w_up, w_down)


def solution(mesh):
    placed = (
        P("req", "role"),
        P("req", "ctx", "role"),
        P("req", "ctx", "role"),
        P("req", "role"),
        P("req", "role"),
        P("req"),
        P(None, "req"),
        P(("role", "ctx"), "req"),
        P(),
        P("req", None),
        P(None, ("role", "req", "ctx")),
        P(),
        P(None, ("role", "req", "ctx")),
        P(None, ("role", "req", "ctx")),
        P(("role", "req", "ctx"), None),
    )
    return jax.shard_map(
        shards, mesh=mesh, in_specs=placed, out_specs=P("req", ("role", "ctx")), check_vma=False
    )
```

```python
import functools
import math

import jax
import jax.numpy as jnp
from jax import lax
from jax.experimental import pallas as pl
from jax.experimental.pallas import tpu as pltpu
from jax.sharding import PartitionSpec as P

MESH = pl.DeviceIdType.MESH
F32 = jnp.float32
BF16 = jnp.bfloat16
HD = 128
EPS = 1e-05
LOW = -1e30
NT = (((1,), (1,)), ((), ()))
Z_FAR = (4, 3, 5, 2, 6, 1, 7)
XY_FAR = ((2, 2), (1, 2), (3, 2), (2, 1), (2, 3), (1, 1), (1, 3), (3, 1), (3, 3),
          (2, 0), (0, 2), (1, 0), (3, 0), (0, 1), (0, 3))
XY_COLUMN = ((0, 2), (0, 1), (0, 3)) + XY_FAR[:9] + ((2, 0), (1, 0), (3, 0))
GROUPS = 2
PER = 8 // GROUPS
Z_ALL = Z_FAR + (0,)
YZ_FAR = tuple((dy, dz) for dz in Z_FAR + (0,) for dy in (2, 1, 3, 0) if dy or dz)
HALF_FAR = tuple((dx, dc, dh) for dh in (1, 0) for dx in (2, 1, 3, 0) for dc in (1, 0) if dx or dc or dh)
REQ_FAR = ((2, 1), (2, 0), (1, 1), (3, 1), (1, 0), (3, 0), (0, 1))


def rcopy(src, dst, ssem, rsem, dev):
    return pltpu.make_async_remote_copy(
        src_ref=src, dst_ref=dst, send_sem=ssem, recv_sem=rsem, device_id=dev, device_id_type=MESH
    )


def loop(lo, hi, body):
    def step(i, carry):
        body(i)
        return carry

    lax.fori_loop(lo, hi, step, 0)


def kernel(
    stop,
    q_h, ck_h, cv_h, nk_h, nv_h, len_s, res_h, wo_h, gain_h, ad_h, tu_h, ten_s, wg_h, wu_h, wd_h,
    out_ref,
    q_v, ck_v, cv_v, nk_v, nv_v, res_v, wo_v, gain_v, ad_v, tu_v, wgu_v, wd_v,
    acc_s, stat_s, racc, rstat, rt_v, lse_s, oh_s, rl,
    ogath, psend, rpart, xs, ad_s, rad, dbuf, rcore, r1, rx, r3, rz,
    lsem,
    go, sa_s, sa_r, ss_s, ss_r, sl_s, sl_r, so_s, so_r, sp_s, sp_r, sz_s, sz_r, sx_s, sx_r, sc_s, sc_r,
    sd_s, sd_r, ec_s, ec_r, ex_s, ex_r, ez_s, ez_r,
):
    role = lax.axis_index("role")
    req = lax.axis_index("req")
    ctx = lax.axis_index("ctx")
    x = lax.div(req, 2)
    core = lax.rem(req, 2)
    yhi = lax.div(ctx, 8)
    z = lax.rem(ctx, 8)
    y = yhi * 2 + role
    yz = role * 16 + ctx
    me = (role, req, ctx)

    def at_req(i):
        return (role, i, ctx)

    def at_xy(xo, yo):
        return (lax.rem(yo, 2), xo * 2 + core, lax.div(yo, 2) * 8 + z)

    def at_y(i):
        return (lax.rem(i, 2), req, lax.div(i, 2) * 8 + z)

    def at_z(i):
        return (role, req, yhi * 8 + i)

    drains = []

    def finish():
        for d in drains:
            d()

    local = [
        pltpu.make_async_copy(q_h, q_v, lsem.at[0]),
        pltpu.make_async_copy(ck_h, ck_v, lsem.at[1]),
        pltpu.make_async_copy(cv_h, cv_v, lsem.at[2]),
        pltpu.make_async_copy(nk_h, nk_v, lsem.at[3]),
        pltpu.make_async_copy(nv_h, nv_v, lsem.at[4]),
        pltpu.make_async_copy(wo_h, wo_v, lsem.at[5]),
        pltpu.make_async_copy(
            res_h.at[pl.ds(pl.multiple_of(y * 16, 16), 16), pl.ds(pl.multiple_of(z * 128, 128), 128)],
            res_v, lsem.at[6],
        ),
        pltpu.make_async_copy(gain_h, gain_v, lsem.at[7]),
        pltpu.make_async_copy(ad_h, ad_v, lsem.at[8]),
        pltpu.make_async_copy(tu_h, tu_v, lsem.at[9]),
        pltpu.make_async_copy(wg_h, wgu_v.at[:, pl.ds(0, 128)], lsem.at[10]),
        pltpu.make_async_copy(wu_h, wgu_v.at[:, pl.ds(128, 128)], lsem.at[11]),
        pltpu.make_async_copy(wd_h, wd_v, lsem.at[12]),
    ]
    for i in (0, 1, 3, 2, 4, 5, 6, 7, 8, 9, 10, 11, 12):
        local[i].start()

    barrier = pltpu.get_barrier_semaphore()

    def greet(dev):
        pl.semaphore_signal(barrier, inc=1, device_id=dev, device_id_type=MESH)

    for o in Z_FAR:
        greet(at_z(lax.rem(z + o, 8)))
    for dx, dc in REQ_FAR:
        greet(at_req(lax.rem(x + dx, 4) * 2 + lax.rem(core + dc, 2)))
    for o in (2, 1, 3):
        greet(at_y(lax.rem(y + o, 4)))

    factor = 1.0 / math.sqrt(HD)
    sub = lax.broadcasted_iota(jnp.int32, (8, 128), 0)
    lane = lax.broadcasted_iota(jnp.int32, (8, 128), 1)
    lens = jnp.zeros((8, 128), jnp.int32)
    for r in range(8):
        lens = jnp.where(sub == r, len_s[r], lens)
    usable = (ctx * 128 + lane < lens)[None]
    rowmod = lax.broadcasted_iota(jnp.int32, (16, 8, 128), 1)
    stat_lane = lax.broadcasted_iota(jnp.int32, (128, 128), 1)
    local[0].wait()
    local[1].wait()
    local[3].wait()
    probs = []
    fresh = []
    stat = jnp.zeros((128, 128), F32)
    for k in range(4):
        qk = jnp.concatenate(
            [q_v[:, (k * 16 + g) * 128:(k * 16 + g + 1) * 128].astype(F32) for g in range(16)], axis=0)
        nk = nk_v[:, k * 128:(k + 1) * 128].astype(F32)
        own = jnp.sum(qk.reshape(16, 8, 128) * nk[None], axis=-1, keepdims=True) * factor
        own = jnp.where(ctx == 0, own, LOW)
        kk = ck_v[:, :, k * 128:(k + 1) * 128].reshape(1024, 128)
        full = lax.dot_general(qk.astype(BF16), kk, NT, preferred_element_type=F32)
        sc = jnp.zeros((16, 8, 128), F32)
        for r in range(8):
            sc = jnp.where(rowmod == r, full[:, r * 128:(r + 1) * 128].reshape(16, 8, 128), sc)
        sc = jnp.where(usable, sc * factor, LOW)
        top = jnp.maximum(jnp.max(sc, axis=-1, keepdims=True), own)
        w = jnp.where(usable, jnp.exp(sc - top), 0.0)
        wb = w.astype(BF16).astype(F32)
        w_own = jnp.where(ctx == 0, jnp.exp(own - top), 0.0)
        tot = jnp.sum(wb, axis=-1, keepdims=True) + w_own
        probs.append(wb)
        fresh.append(w_own)
        stat = jnp.where(stat_lane == 2 * k, top.reshape(128, 1), stat)
        stat = jnp.where(stat_lane == 2 * k + 1, tot.reshape(128, 1), stat)
    stat_s[...] = stat.T[0:8, :]

    pl.semaphore_wait(barrier, 17)
    for o in (2, 1, 3):
        pl.semaphore_signal(go, inc=1, device_id=at_y(lax.rem(y + o, 4)), device_id_type=MESH)

    def stat_copy(o):
        return rcopy(stat_s, rstat.at[z], ss_s.at[o], ss_r.at[z], at_z(lax.rem(z + o, 8)))

    def acc_copy(o):
        zo = lax.rem(z + o, 8)
        return rcopy(acc_s.at[:, zo], racc.at[z], sa_s.at[o], sa_r.at[z], at_z(zo))

    for o in Z_FAR:
        stat_copy(o).start()
        drains.append(lambda o=o: stat_copy(o).wait_send())
    rstat[z] = stat_s[...]
    local[2].wait()
    local[4].wait()
    for k in range(4):
        big = jnp.concatenate(
            [jnp.where(rowmod == r, probs[k], 0.0).reshape(128, 128).astype(BF16) for r in range(8)], axis=1)
        vk = cv_v[:, :, k * 128:(k + 1) * 128].reshape(1024, 128)
        acc = jnp.dot(big, vk, preferred_element_type=F32).reshape(16, 8, 128)
        acc = acc + fresh[k] * nv_v[:, k * 128:(k + 1) * 128].astype(F32)[None]
        acc_s[k // 2, (k % 2) * 4:(k % 2) * 4 + 4] = acc.reshape(4, 32, 128).astype(BF16)
    for o in Z_FAR:
        acc_copy(o).start()
        drains.append(lambda o=o: acc_copy(o).wait_send())
    for j in range(2):
        racc[z, j] = acc_s[j, z]

    def wait_stat(o):
        c = lax.rem(z + o, 8)
        rcopy(stat_s, rstat.at[c], ss_s.at[o], ss_r.at[c], me).wait_recv()

    def wait_acc(o):
        c = lax.rem(z + o, 8)
        rcopy(racc.at[c], racc.at[c], sa_s.at[o], sa_r.at[c], me).wait_recv()

    loop(1, 8, wait_stat)
    rs = rstat[...]
    high = jnp.max(rs, axis=0)
    scale = jnp.exp(rs - high[None])
    den = jnp.maximum(jnp.sum(scale * pltpu.roll(rs, 7, 1), axis=0), 1e-30)
    lse = high + jnp.log(den)
    lse_s[...] = lse
    flat = (scale / den[None]).reshape(64, 128)
    rt_v[...] = jnp.concatenate([flat, flat], axis=0).T
    kz = lax.div(z, 4)
    rows_z = pl.ds(pl.multiple_of(lax.rem(z, 4) * 32, 32), 32)
    st = rt_v[rows_z, :]
    st = jnp.where(kz == 0, st, pltpu.roll(st, 126, 1))
    loop(1, 8, wait_acc)
    for j in range(2):
        part = jnp.zeros((32, 128), F32)
        for c in range(8):
            part = part + st[:, 8 * c + 4 * j:8 * c + 4 * j + 1] * racc[c, j].astype(F32)
        oh_s[j] = part.astype(BF16)

    def h_peer(dx, dc, dh):
        return lax.rem(yhi + dh, 2), lax.rem(x + dx, 4) * 2 + lax.rem(core + dc, 2)

    def l_copy(dx, dc, dh):
        h, b = h_peer(dx, dc, dh)
        return rcopy(lse_s, rl.at[yhi, req], sl_s.at[dh, dx * 2 + dc], sl_r.at[yhi, req], (role, b, h * 8 + z))

    def o_copy(dx, dc, dh):
        h, b = h_peer(dx, dc, dh)
        return rcopy(oh_s.at[h], ogath.at[yhi, req], so_s.at[dh, dx * 2 + dc], so_r.at[yhi, req],
                     (role, b, h * 8 + z))

    pl.semaphore_wait(go, 3)
    for o in HALF_FAR:
        o_copy(*o).start()
        l_copy(*o).start()

    def drain_o():
        for o in HALF_FAR:
            o_copy(*o).wait_send()
            l_copy(*o).wait_send()

    drains.append(drain_o)
    ogath[yhi, req] = oh_s[yhi]
    rl[yhi, req] = lse

    def wait_l(o):
        i = lax.rem(yhi * 8 + req + o, 16)
        h, b = lax.div(i, 8), lax.rem(i, 8)
        rcopy(rl.at[h, b], rl.at[h, b], sl_s.at[h, b], sl_r.at[h, b], me).wait_recv()

    def wait_o(o):
        i = lax.rem(yhi * 8 + req + o, 16)
        h, b = lax.div(i, 8), lax.rem(i, 8)
        rcopy(ogath.at[h, b], ogath.at[h, b], so_s.at[h, b], so_r.at[h, b], me).wait_recv()

    loop(1, 16, wait_l)
    gap = rl[1] - rl[0]
    both = jnp.concatenate(
        [(1.0 / (1.0 + jnp.exp(gap))).reshape(64, 128), (1.0 / (1.0 + jnp.exp(-gap))).reshape(64, 128)], axis=0)
    rt_v[...] = both.T
    st = pltpu.roll(rt_v[rows_z, :], lax.rem(128 - 4 * yhi - 2 * kz, 128), 1)
    loop(1, 16, wait_o)
    heads = []
    for b in range(8):
        heads.append(st[:, 8 * b:8 * b + 1] * ogath[0, b].astype(F32)
                     + st[:, 64 + 8 * b:64 + 8 * b + 1] * ogath[1, b].astype(F32))
    attn = jnp.concatenate(
        [jnp.concatenate([heads[b][8 * g:8 * g + 8, :] for b in range(8)], axis=0) for g in range(4)],
        axis=1).astype(BF16)
    local[5].wait()
    proj = jnp.dot(attn, wo_v[...], preferred_element_type=F32)
    for yy in range(4):
        for zz in range(8):
            psend[yy, zz] = proj[16 * yy:16 * yy + 16, 128 * zz:128 * zz + 128].astype(BF16)

    def p_copy(dy, dz):
        yo, zo = lax.rem(y + dy, 4), lax.rem(z + dz, 8)
        return rcopy(psend.at[yo, zo], rpart.at[yz], sp_s.at[dy * 8 + dz], sp_r.at[yz],
                     (lax.rem(yo, 2), req, lax.div(yo, 2) * 8 + zo))

    for o in YZ_FAR:
        p_copy(*o).start()

    def drain_p():
        for o in YZ_FAR:
            p_copy(*o).wait_send()

    drains.append(drain_p)
    rpart[yz] = psend[y, z]

    def wait_p(o):
        c = lax.rem(yz + o, 32)
        rcopy(rpart.at[c], rpart.at[c], sp_s.at[o], sp_r.at[c], me).wait_recv()

    loop(1, 32, wait_p)
    local[6].wait()
    piece = res_v[...].astype(F32) + jnp.sum(rpart[...].astype(F32), axis=0)
    rows_y = pl.ds(pl.multiple_of(y * 16, 16), 16)
    xs[req * 8 + z, rows_y, :] = piece.astype(BF16)

    def z_ref(i):
        return xs.at[req * 8 + i, rows_y]

    def z_copy(o):
        return rcopy(z_ref(z), z_ref(z), sz_s.at[o], sz_r.at[z], at_z(lax.rem(z + o, 8)))

    for o in Z_FAR:
        z_copy(o).start()
        drains.append(lambda o=o: z_copy(o).wait_send())

    def wait_z(o):
        c = lax.rem(z + o, 8)
        rcopy(z_ref(c), z_ref(c), sz_s.at[o], sz_r.at[c], me).wait_recv()

    loop(1, 8, wait_z)

    def y_ref(b, yo):
        return xs.at[pl.ds(b * 8, 8), pl.ds(pl.multiple_of(yo * 16, 16), 16)]

    def xy_copy(dx, dy):
        return rcopy(y_ref(req, y), y_ref(req, y), sx_s.at[dx, dy], sx_r.at[x, y],
                     at_xy(lax.rem(x + dx, 4), lax.rem(y + dy, 4)))

    def xy_wait(dx, dy):
        xo, yo = lax.rem(x + dx, 4), lax.rem(y + dy, 4)
        ref = y_ref(xo * 2 + core, yo)
        rcopy(ref, ref, sx_s.at[dx, dy], sx_r.at[xo, yo], me).wait_recv()

    for o in XY_COLUMN:
        xy_copy(*o).start()
        drains.append(lambda o=o: xy_copy(*o).wait_send())

    def b_ref(b):
        return xs.at[pl.ds(b * 8, 8)]

    def c_copy(o):
        b = lax.rem(x + o, 4) * 2 + core
        return rcopy(b_ref(b), b_ref(b), sc_s.at[o], sc_r.at[lax.rem(x + o, 4)], at_req(x * 2 + 1 - core))

    for dy in (1, 3, 2):
        xy_wait(0, dy)
    c_copy(0).start()
    drains.append(lambda: c_copy(0).wait_send())
    local[7].wait()
    local[8].wait()
    local[10].wait()
    local[11].wait()

    def block(b):
        xb = xs[pl.ds(b * 8, 8)].astype(F32)
        sq = jnp.sum(jnp.sum(xb * xb, axis=0), axis=-1, keepdims=True)
        xg = xb * gain_v[pl.ds(pl.multiple_of(b * 8, 8), 8), :][:, None, :]
        xg = jnp.concatenate([xg[i] for i in range(8)], axis=1).astype(BF16)
        return sq, xg

    def gate_up(b, xg):
        rows = pl.ds(pl.multiple_of(b * 1024, 1024), 1024)
        return jnp.dot(xg, wgu_v[rows, :], preferred_element_type=F32)

    sq, xg = block(req)
    mid = jnp.dot(xg, ad_v[...], preferred_element_type=F32)
    owner = lax.div(lane, 16)
    tens = []
    packed = jnp.zeros((8, 128), F32)
    for i in range(8):
        t = jnp.zeros((8, 128), jnp.int32)
        for r in range(8):
            t = jnp.where(sub == r, ten_s[8 * i + r], t)
        tens.append(t)
        v = (jnp.where(owner == t, mid[8 * i:8 * i + 8, 0:128], 0.0)
             + jnp.where(owner + 8 == t, mid[8 * i:8 * i + 8, 128:256], 0.0))
        v = v + pltpu.roll(v, 64, 1)
        v = v + pltpu.roll(v, 32, 1)
        v = v + pltpu.roll(v, 16, 1)
        packed = jnp.where(owner == i, v, packed)
    ad_s[...] = packed

    def d_copy(dx, dc):
        peer = at_req(lax.rem(x + dx, 4) * 2 + lax.rem(core + dc, 2))
        return rcopy(ad_s, rad.at[req], sd_s.at[dx * 2 + dc], sd_r.at[req], peer)

    for o in REQ_FAR:
        d_copy(*o).start()
        drains.append(lambda o=o: d_copy(*o).wait_send())
    rad[req] = packed
    gu = gate_up(req, xg)
    for o in (1, 3, 2):
        b = lax.rem(x + o, 4) * 2 + core
        for dy in (0, 1, 3, 2):
            xy_wait(o, dy)
        c_copy(o).start()
        drains.append(lambda o=o: c_copy(o).wait_send())
        s1, xg = block(b)
        sq = sq + s1
        gu = gu + gate_up(b, xg)
    for o in (0, 1, 3, 2):
        xo = lax.rem(x + o, 4)
        b = xo * 2 + 1 - core
        rcopy(b_ref(b), b_ref(b), sc_s.at[o], sc_r.at[xo], me).wait_recv()
        s1, xg = block(b)
        sq = sq + s1
        gu = gu + gate_up(b, xg)

    def wait_d(o):
        c = lax.rem(req + o, 8)
        rcopy(ad_s, rad.at[c], sd_s.at[o], sd_r.at[c], me).wait_recv()

    loop(1, 8, wait_d)
    inv = lax.rsqrt(sq * (1.0 / 8192.0) + EPS)
    allmid = jnp.sum(rad[...], axis=0)
    chosen = []
    for i in range(8):
        v = jnp.where(owner == i, allmid, 0.0)
        v = v + pltpu.roll(v, 64, 1)
        v = v + pltpu.roll(v, 32, 1)
        v = v + pltpu.roll(v, 16, 1)
        v = v * inv[8 * i:8 * i + 8]
        chosen.append(jnp.concatenate(
            [jnp.where(owner == tens[i], v, 0.0), jnp.where(owner + 8 == tens[i], v, 0.0)], axis=1))
    local[9].wait()
    lowrank = jnp.dot(jnp.concatenate(chosen, axis=0).astype(BF16), tu_v[...], preferred_element_type=F32)
    gate = gu[:, 0:128] * inv
    up = gu[:, 128:256] * inv + 2.0 * lowrank
    hid = (gate / (1.0 + jnp.exp(-gate)) * up).astype(BF16)

    local[12].wait()

    def core_copy(g):
        return rcopy(dbuf.at[1 - core, g], rcore.at[g], ec_s.at[g], ec_r.at[g], at_req(x * 2 + 1 - core))

    def ex_copy(g, dx, dy):
        xo, yo = lax.rem(x + dx, 4), lax.rem(y + dy, 4)
        return rcopy(r1.at[g, xo, yo], rx.at[g, x, y], ex_s.at[g, dx, dy], ex_r.at[g, x, y], at_xy(xo, yo))

    def ez_copy(i):
        zo = lax.rem(z + Z_ALL[i], 8)
        return rcopy(r3.at[i], rz.at[z], ez_s.at[i], ez_r.at[z], at_z(zo))

    for g in range(GROUPS):
        for i in range(PER):
            zo = lax.rem(z + Z_ALL[g * PER + i], 8)
            for yy in range(4):
                col = pl.multiple_of(((yy % 2) * 16 + (yy // 2) * 8 + zo) * 256, 256)
                part = jnp.dot(hid, wd_v[:, pl.ds(col, 256)], preferred_element_type=F32)
                for b in range(8):
                    dbuf[b % 2, g, b // 2, yy, i] = jnp.concatenate(
                        [part[8 * b:8 * b + 8, 0:128], part[8 * b:8 * b + 8, 128:256]], axis=0).astype(BF16)
        core_copy(g).start()
        drains.append(lambda g=g: core_copy(g).wait_send())

    for g in range(GROUPS):
        core_copy(g).wait_recv()

        def fold_core(i):
            r1[g, i] = (dbuf[core, g, i].astype(F32) + rcore[g, i].astype(F32)).astype(BF16)

        loop(0, 4, fold_core)
        for o in XY_FAR:
            ex_copy(g, *o).start()
            drains.append(lambda g=g, o=o: ex_copy(g, *o).wait_send())
        rx[g, x, y] = r1[g, x, y]

    own = xs[pl.ds(yz * 2, 2), pl.ds(pl.multiple_of(x * 16, 16), 16), :].astype(F32)
    own = jnp.where(core == 0, own[:, 0:8, :], own[:, 8:16, :]).reshape(16, 128)

    for g in range(GROUPS):
        def wait_ex(o):
            i = lax.rem(x * 4 + y + o, 16)
            xo, yo = lax.div(i, 4), lax.rem(i, 4)
            rcopy(rx.at[g, xo, yo], rx.at[g, xo, yo], ex_s.at[g, xo, yo], ex_r.at[g, xo, yo], me).wait_recv()

        loop(1, 16, wait_ex)
        for i in range(PER):
            part = rx[g, 0, 0, i].astype(F32)
            for j in range(1, 16):
                part = part + rx[g, j // 4, j % 4, i].astype(F32)
            if Z_ALL[g * PER + i]:
                r3[g * PER + i] = part.astype(BF16)
                ez_copy(g * PER + i).start()
                drains.append(lambda k=g * PER + i: ez_copy(k).wait_send())
            else:
                own = own + part
                rz[z] = jnp.zeros((16, 128), BF16)

    def wait_ez(o):
        zo = lax.rem(z + o, 8)
        rcopy(rz.at[zo], rz.at[zo], ez_s.at[o], ez_r.at[zo], me).wait_recv()

    loop(1, 8, wait_ez)
    res = own + jnp.sum(rz[...].astype(F32), axis=0)
    out_ref[:, 0:128] = res[0:8, :].astype(BF16)
    out_ref[:, 128:256] = res[8:16, :].astype(BF16)
    finish()


def shards(query, cache_keys, cache_values, new_keys, new_values, lengths, residual_in, out_proj,
           norm_gain, adapter_down, tenant_adapter_up_matrix, tenant, w_gate, w_up, w_down):
    hbm = pl.BlockSpec(memory_space=pl.ANY)
    smem = pl.BlockSpec(memory_space=pltpu.SMEM)
    v = pltpu.VMEM
    dma = pltpu.SemaphoreType.DMA
    return pl.pallas_call(
        functools.partial(kernel, None),
        out_shape=jax.ShapeDtypeStruct((8, 256), BF16),
        in_specs=[hbm, hbm, hbm, hbm, hbm, smem, hbm, hbm, hbm, hbm, hbm, smem, hbm, hbm, hbm],
        out_specs=pl.BlockSpec(memory_space=pltpu.VMEM),
        scratch_shapes=[
            v((8, 8192), BF16), v((8, 128, 512), BF16), v((8, 128, 512), BF16), v((8, 512), BF16),
            v((8, 512), BF16), v((16, 128), BF16), v((512, 1024), BF16), v((64, 128), F32),
            v((1024, 256), BF16), v((256, 128), BF16), v((8192, 256), BF16), v((128, 8192), BF16),
            v((2, 8, 32, 128), BF16), v((8, 128), F32), v((8, 2, 32, 128), BF16), v((8, 8, 128), F32),
            v((128, 128), F32), v((8, 128), F32), v((2, 32, 128), BF16), v((2, 8, 8, 128), F32),
            v((2, 8, 32, 128), BF16), v((4, 8, 16, 128), BF16), v((32, 16, 128), BF16), v((64, 64, 128), BF16),
            v((8, 128), F32), v((8, 8, 128), F32),
            v((2, GROUPS, 4, 4, PER, 16, 128), BF16), v((GROUPS, 4, 4, PER, 16, 128), BF16),
            v((GROUPS, 4, 4, PER, 16, 128), BF16), v((GROUPS, 4, 4, PER, 16, 128), BF16), v((8, 16, 128), BF16), v((8, 16, 128), BF16),
            dma((13,)),
            pltpu.SemaphoreType.REGULAR, dma((8,)), dma((8,)), dma((8,)), dma((8,)),
            dma((2, 8)), dma((2, 8)), dma((2, 8)), dma((2, 8)), dma((32,)), dma((32,)),
            dma((8,)), dma((8,)), dma((4, 4)), dma((4, 4)), dma((4,)), dma((4,)),
            dma((8,)), dma((8,)), dma((GROUPS,)), dma((GROUPS,)),
            dma((GROUPS, 4, 4)), dma((GROUPS, 4, 4)), dma((8,)), dma((8,)),
        ],
        compiler_params=pltpu.CompilerParams(
            collective_id=0, has_side_effects=True, vmem_limit_bytes=60 * 1024 * 1024),
    )(query, cache_keys, cache_values, new_keys, new_values, lengths, residual_in, out_proj,
      norm_gain.reshape(64, 128), adapter_down, tenant_adapter_up_matrix, tenant, w_gate, w_up, w_down)


def solution(mesh):
    placed = (
        P("req", "role"),
        P("req", "ctx", "role"),
        P("req", "ctx", "role"),
        P("req", "role"),
        P("req", "role"),
        P("req"),
        P(None, "req"),
        P(("role", "ctx"), "req"),
        P(),
        P("req", None),
        P(None, ("role", "req", "ctx")),
        P(),
        P(None, ("role", "req", "ctx")),
        P(None, ("role", "req", "ctx")),
        P(("role", "req", "ctx"), None),
    )
    return jax.shard_map(
        shards, mesh=mesh, in_specs=placed, out_specs=P("req", ("role", "ctx")), check_vma=False
    )
```

```python
import functools
import math

import jax
import jax.numpy as jnp
from jax import lax
from jax.experimental import pallas as pl
from jax.experimental.pallas import tpu as pltpu
from jax.sharding import PartitionSpec as P

MESH = pl.DeviceIdType.MESH
F32 = jnp.float32
BF16 = jnp.bfloat16
HD = 128
EPS = 1e-05
LOW = -1e30
NT = (((1,), (1,)), ((), ()))
Z_FAR = (4, 3, 5, 2, 6, 1, 7)
XY_FAR = ((2, 2), (1, 2), (3, 2), (2, 1), (2, 3), (1, 1), (1, 3), (3, 1), (3, 3),
          (2, 0), (0, 2), (1, 0), (3, 0), (0, 1), (0, 3))
XY_COLUMN = ((0, 2), (0, 1), (0, 3)) + XY_FAR[:9] + ((2, 0), (1, 0), (3, 0))
GROUPS = 2
PER = 8 // GROUPS
Z_ALL = Z_FAR + (0,)
RING = (0, 1, 7, 2, 6, 3, 5, 4)
RUNS = ((0, 3), (3, 8))
PLANE = tuple((dx, dc, dy) for dx in (2, 1, 3, 0) for dy in (2, 1, 3, 0) for dc in (1, 0) if dx or dc or dy)
YZ_FAR = tuple((dy, dz) for dz in Z_FAR + (0,) for dy in (2, 1, 3, 0) if dy or dz)
HALF_FAR = tuple((dx, dc, dh) for dh in (1, 0) for dx in (2, 1, 3, 0) for dc in (1, 0) if dx or dc or dh)
REQ_FAR = ((2, 1), (2, 0), (1, 1), (3, 1), (1, 0), (3, 0), (0, 1))


def rcopy(src, dst, ssem, rsem, dev):
    return pltpu.make_async_remote_copy(
        src_ref=src, dst_ref=dst, send_sem=ssem, recv_sem=rsem, device_id=dev, device_id_type=MESH
    )


def loop(lo, hi, body):
    def step(i, carry):
        body(i)
        return carry

    lax.fori_loop(lo, hi, step, 0)


def kernel(
    stop,
    q_h, ck_h, cv_h, nk_h, nv_h, len_s, res_h, wo_h, gain_h, ad_h, tu_h, ten_s, wg_h, wu_h, wd_h,
    out_ref,
    q_v, ck_v, cv_v, nk_v, nv_v, res_v, wo_v, gain_v, ad_v, tu_v, wgu_v, wd_v,
    acc_s, stat_s, racc, rstat, rt_v, lse_s, oh_s, rl,
    ogath, psend, rpart, xs, ad_s, rad, dbuf, rcore, r1, rx, r3, rz,
    lsem,
    go, sa_s, sa_r, ss_s, ss_r, sl_s, sl_r, so_s, so_r, sp_s, sp_r, sz_s, sz_r, sx_s, sx_r, sc_s, sc_r,
    sd_s, sd_r, ec_s, ec_r, ex_s, ex_r, ez_s, ez_r,
):
    role = lax.axis_index("role")
    req = lax.axis_index("req")
    ctx = lax.axis_index("ctx")
    x = lax.div(req, 2)
    core = lax.rem(req, 2)
    yhi = lax.div(ctx, 8)
    z = lax.rem(ctx, 8)
    y = yhi * 2 + role
    yz = role * 16 + ctx
    me = (role, req, ctx)

    def at_req(i):
        return (role, i, ctx)

    def at_xy(xo, yo):
        return (lax.rem(yo, 2), xo * 2 + core, lax.div(yo, 2) * 8 + z)

    def at_y(i):
        return (lax.rem(i, 2), req, lax.div(i, 2) * 8 + z)

    def at_z(i):
        return (role, req, yhi * 8 + i)

    drains = []

    def drain():
        while drains:
            drains.pop(0)()

    local = [
        pltpu.make_async_copy(q_h, q_v, lsem.at[0]),
        pltpu.make_async_copy(ck_h, ck_v, lsem.at[1]),
        pltpu.make_async_copy(cv_h, cv_v, lsem.at[2]),
        pltpu.make_async_copy(nk_h, nk_v, lsem.at[3]),
        pltpu.make_async_copy(nv_h, nv_v, lsem.at[4]),
        pltpu.make_async_copy(wo_h, wo_v, lsem.at[5]),
        pltpu.make_async_copy(
            res_h.at[pl.ds(pl.multiple_of(y * 16, 16), 16), pl.ds(pl.multiple_of(z * 128, 128), 128)],
            res_v, lsem.at[6],
        ),
        pltpu.make_async_copy(gain_h, gain_v, lsem.at[7]),
        pltpu.make_async_copy(ad_h, ad_v, lsem.at[8]),
        pltpu.make_async_copy(tu_h, tu_v, lsem.at[9]),
        pltpu.make_async_copy(wg_h, wgu_v.at[:, pl.ds(0, 128)], lsem.at[10]),
        pltpu.make_async_copy(wu_h, wgu_v.at[:, pl.ds(128, 128)], lsem.at[11]),
        pltpu.make_async_copy(wd_h, wd_v, lsem.at[12]),
    ]
    for i in (0, 1, 3, 2, 4, 5, 6, 7, 8, 9, 10, 11, 12):
        local[i].start()

    barrier = pltpu.get_barrier_semaphore()

    def greet(dev):
        pl.semaphore_signal(barrier, inc=1, device_id=dev, device_id_type=MESH)

    for o in Z_FAR:
        greet(at_z(lax.rem(z + o, 8)))
    for dx, dc in REQ_FAR:
        greet(at_req(lax.rem(x + dx, 4) * 2 + lax.rem(core + dc, 2)))
    for o in (2, 1, 3):
        greet(at_y(lax.rem(y + o, 4)))

    factor = 1.0 / math.sqrt(HD)
    sub = lax.broadcasted_iota(jnp.int32, (8, 128), 0)
    lane = lax.broadcasted_iota(jnp.int32, (8, 128), 1)
    lens = jnp.zeros((8, 128), jnp.int32)
    for r in range(8):
        lens = jnp.where(sub == r, len_s[r], lens)
    usable = (ctx * 128 + lane < lens)[None]
    rowmod = lax.broadcasted_iota(jnp.int32, (16, 8, 128), 1)
    stat_lane = lax.broadcasted_iota(jnp.int32, (128, 128), 1)
    local[0].wait()
    local[1].wait()
    local[3].wait()
    probs = []
    fresh = []
    stat = jnp.zeros((128, 128), F32)
    for k in range(4):
        qk = jnp.concatenate(
            [q_v[:, (k * 16 + g) * 128:(k * 16 + g + 1) * 128].astype(F32) for g in range(16)], axis=0)
        nk = nk_v[:, k * 128:(k + 1) * 128].astype(F32)
        own = jnp.sum(qk.reshape(16, 8, 128) * nk[None], axis=-1, keepdims=True) * factor
        own = jnp.where(ctx == 0, own, LOW)
        kk = ck_v[:, :, k * 128:(k + 1) * 128].reshape(1024, 128)
        full = lax.dot_general(qk.astype(BF16), kk, NT, preferred_element_type=F32)
        sc = jnp.zeros((16, 8, 128), F32)
        for r in range(8):
            sc = jnp.where(rowmod == r, full[:, r * 128:(r + 1) * 128].reshape(16, 8, 128), sc)
        sc = jnp.where(usable, sc * factor, LOW)
        top = jnp.maximum(jnp.max(sc, axis=-1, keepdims=True), own)
        w = jnp.where(usable, jnp.exp(sc - top), 0.0)
        wb = w.astype(BF16).astype(F32)
        w_own = jnp.where(ctx == 0, jnp.exp(own - top), 0.0)
        tot = jnp.sum(wb, axis=-1, keepdims=True) + w_own
        probs.append(wb)
        fresh.append(w_own)
        stat = jnp.where(stat_lane == 2 * k, top.reshape(128, 1), stat)
        stat = jnp.where(stat_lane == 2 * k + 1, tot.reshape(128, 1), stat)
    stat_s[...] = stat.T[0:8, :]

    pl.semaphore_wait(barrier, 17)
    for o in (2, 1, 3):
        pl.semaphore_signal(go, inc=1, device_id=at_y(lax.rem(y + o, 4)), device_id_type=MESH)

    def stat_copy(o):
        return rcopy(stat_s, rstat.at[z], ss_s.at[o], ss_r.at[z], at_z(lax.rem(z + o, 8)))

    def acc_copy(o):
        zo = lax.rem(z + o, 8)
        return rcopy(acc_s.at[:, zo], racc.at[z], sa_s.at[o], sa_r.at[z], at_z(zo))

    for o in Z_FAR:
        stat_copy(o).start()
        drains.append(lambda o=o: stat_copy(o).wait_send())
    rstat[z] = stat_s[...]
    local[2].wait()
    local[4].wait()
    for k in range(4):
        big = jnp.concatenate(
            [jnp.where(rowmod == r, probs[k], 0.0).reshape(128, 128).astype(BF16) for r in range(8)], axis=1)
        vk = cv_v[:, :, k * 128:(k + 1) * 128].reshape(1024, 128)
        acc = jnp.dot(big, vk, preferred_element_type=F32).reshape(16, 8, 128)
        acc = acc + fresh[k] * nv_v[:, k * 128:(k + 1) * 128].astype(F32)[None]
        acc_s[k // 2, (k % 2) * 4:(k % 2) * 4 + 4] = acc.reshape(4, 32, 128).astype(BF16)
    for o in Z_FAR:
        acc_copy(o).start()
        drains.append(lambda o=o: acc_copy(o).wait_send())
    for j in range(2):
        racc[z, j] = acc_s[j, z]

    def wait_stat(o):
        c = lax.rem(z + o, 8)
        rcopy(stat_s, rstat.at[c], ss_s.at[o], ss_r.at[c], me).wait_recv()

    def wait_acc(o):
        c = lax.rem(z + o, 8)
        rcopy(racc.at[c], racc.at[c], sa_s.at[o], sa_r.at[c], me).wait_recv()

    loop(1, 8, wait_stat)
    rs = rstat[...]
    high = jnp.max(rs, axis=0)
    scale = jnp.exp(rs - high[None])
    den = jnp.maximum(jnp.sum(scale * pltpu.roll(rs, 7, 1), axis=0), 1e-30)
    lse = high + jnp.log(den)
    lse_s[...] = lse
    flat = (scale / den[None]).reshape(64, 128)
    rt_v[...] = jnp.concatenate([flat, flat], axis=0).T
    kz = lax.div(z, 4)
    rows_z = pl.ds(pl.multiple_of(lax.rem(z, 4) * 32, 32), 32)
    st = rt_v[rows_z, :]
    st = jnp.where(kz == 0, st, pltpu.roll(st, 126, 1))
    loop(1, 8, wait_acc)
    for j in range(2):
        part = jnp.zeros((32, 128), F32)
        for c in range(8):
            part = part + st[:, 8 * c + 4 * j:8 * c + 4 * j + 1] * racc[c, j].astype(F32)
        oh_s[j] = part.astype(BF16)

    def h_peer(dx, dc, dh):
        return lax.rem(yhi + dh, 2), lax.rem(x + dx, 4) * 2 + lax.rem(core + dc, 2)

    def l_copy(dx, dc, dh):
        h, b = h_peer(dx, dc, dh)
        return rcopy(lse_s, rl.at[yhi, req], sl_s.at[dh, dx * 2 + dc], sl_r.at[yhi, req], (role, b, h * 8 + z))

    def o_copy(dx, dc, dh):
        h, b = h_peer(dx, dc, dh)
        return rcopy(oh_s.at[h], ogath.at[yhi, req], so_s.at[dh, dx * 2 + dc], so_r.at[yhi, req],
                     (role, b, h * 8 + z))

    pl.semaphore_wait(go, 3)
    for o in HALF_FAR:
        o_copy(*o).start()
        l_copy(*o).start()
    drain()

    def drain_o():
        for o in HALF_FAR:
            o_copy(*o).wait_send()
            l_copy(*o).wait_send()

    drains.append(drain_o)
    ogath[yhi, req] = oh_s[yhi]
    rl[yhi, req] = lse

    def wait_l(o):
        i = lax.rem(yhi * 8 + req + o, 16)
        h, b = lax.div(i, 8), lax.rem(i, 8)
        rcopy(rl.at[h, b], rl.at[h, b], sl_s.at[h, b], sl_r.at[h, b], me).wait_recv()

    def wait_o(o):
        i = lax.rem(yhi * 8 + req + o, 16)
        h, b = lax.div(i, 8), lax.rem(i, 8)
        rcopy(ogath.at[h, b], ogath.at[h, b], so_s.at[h, b], so_r.at[h, b], me).wait_recv()

    loop(1, 16, wait_l)
    gap = rl[1] - rl[0]
    both = jnp.concatenate(
        [(1.0 / (1.0 + jnp.exp(gap))).reshape(64, 128), (1.0 / (1.0 + jnp.exp(-gap))).reshape(64, 128)], axis=0)
    rt_v[...] = both.T
    st = pltpu.roll(rt_v[rows_z, :], lax.rem(128 - 4 * yhi - 2 * kz, 128), 1)
    loop(1, 16, wait_o)
    heads = []
    for b in range(8):
        heads.append(st[:, 8 * b:8 * b + 1] * ogath[0, b].astype(F32)
                     + st[:, 64 + 8 * b:64 + 8 * b + 1] * ogath[1, b].astype(F32))
    attn = jnp.concatenate(
        [jnp.concatenate([heads[b][8 * g:8 * g + 8, :] for b in range(8)], axis=0) for g in range(4)],
        axis=1).astype(BF16)
    local[5].wait()
    proj = jnp.dot(attn, wo_v[...], preferred_element_type=F32)
    for yy in range(4):
        for zz in range(8):
            psend[yy, zz] = proj[16 * yy:16 * yy + 16, 128 * zz:128 * zz + 128].astype(BF16)

    def p_copy(dy, dz):
        yo, zo = lax.rem(y + dy, 4), lax.rem(z + dz, 8)
        return rcopy(psend.at[yo, zo], rpart.at[yz], sp_s.at[dy * 8 + dz], sp_r.at[yz],
                     (lax.rem(yo, 2), req, lax.div(yo, 2) * 8 + zo))

    for o in YZ_FAR:
        p_copy(*o).start()
    drain()

    def drain_p():
        for o in YZ_FAR:
            p_copy(*o).wait_send()

    drains.append(drain_p)
    rpart[yz] = psend[y, z]

    def wait_p(o):
        c = lax.rem(yz + o, 32)
        rcopy(rpart.at[c], rpart.at[c], sp_s.at[o], sp_r.at[c], me).wait_recv()

    loop(1, 32, wait_p)
    local[6].wait()
    piece = res_v[...].astype(F32) + jnp.sum(rpart[...].astype(F32), axis=0)
    rows_y = pl.ds(pl.multiple_of(y * 16, 16), 16)
    xs[req, 0, rows_y, :] = piece.astype(BF16)

    def z_copy(o):
        at = RING.index((8 - o) % 8)
        return rcopy(xs.at[req, 0, rows_y], xs.at[req, at, rows_y], sz_s.at[o], sz_r.at[at],
                     at_z(lax.rem(z + o, 8)))

    def y_ref(g, b, yo):
        lo, hi = RUNS[g]
        return xs.at[b, pl.ds(lo, hi - lo), pl.ds(pl.multiple_of(yo * 16, 16), 16)]

    def xy_copy(g, dx, dy):
        return rcopy(y_ref(g, req, y), y_ref(g, req, y), sx_s.at[g, dx, dy], sx_r.at[g, x, y],
                     at_xy(lax.rem(x + dx, 4), lax.rem(y + dy, 4)))

    def xy_wait(g, dx, dy):
        xo, yo = lax.rem(x + dx, 4), lax.rem(y + dy, 4)
        ref = y_ref(g, xo * 2 + core, yo)
        rcopy(ref, ref, sx_s.at[g, dx, dy], sx_r.at[g, xo, yo], me).wait_recv()

    def b_ref(g, b):
        lo, hi = RUNS[g]
        return xs.at[b, pl.ds(lo, hi - lo)]

    def c_copy(g, o):
        xo = lax.rem(x + o, 4)
        ref = b_ref(g, xo * 2 + core)
        return rcopy(ref, ref, sc_s.at[g, o], sc_r.at[g, xo], at_req(x * 2 + 1 - core))

    def c_wait(g, o):
        xo = lax.rem(x + o, 4)
        ref = b_ref(g, xo * 2 + 1 - core)
        rcopy(ref, ref, sc_s.at[g, o], sc_r.at[g, xo], me).wait_recv()

    for o in Z_FAR:
        z_copy(o).start()
    for g, (lo, hi) in enumerate(RUNS):
        for at in range(max(lo, 1), hi):
            ref = xs.at[req, at, rows_y]
            rcopy(ref, ref, sz_s.at[at], sz_r.at[at], me).wait_recv()
        for o in XY_COLUMN:
            xy_copy(g, *o).start()
        if g == 0:
            drain()
    for o in Z_FAR:
        drains.append(lambda o=o: z_copy(o).wait_send())
    for g in range(len(RUNS)):
        for o in XY_COLUMN:
            drains.append(lambda g=g, o=o: xy_copy(g, *o).wait_send())
    def rows_of(lo, hi, b):
        return [b * 8 + lax.rem(z + RING[at], 8) for at in range(lo, hi)]

    def gained(xb, chunks):
        xg = [xb[i] * gain_v[pl.ds(c, 1), :] for i, c in enumerate(chunks)]
        return jnp.concatenate(xg, axis=1).astype(BF16)

    def block(g, b):
        lo, hi = RUNS[g]
        xb = xs[b, lo:hi].astype(F32)
        sq = jnp.sum(jnp.sum(xb * xb, axis=0), axis=-1, keepdims=True)
        return sq, gained(xb, rows_of(lo, hi, b))

    def weights(ref, chunks):
        return jnp.concatenate([ref[pl.ds(pl.multiple_of(c * 128, 128), 128), :] for c in chunks], axis=0)

    local[7].wait()
    local[8].wait()
    owner = lax.div(lane, 16)

    def tenants(first):
        t = jnp.zeros((8, 128), jnp.int32)
        for r in range(8):
            t = jnp.where(sub == r, ten_s[first + r], t)
        return t

    def spread(v):
        v = v + pltpu.roll(v, 64, 1)
        v = v + pltpu.roll(v, 32, 1)
        return v + pltpu.roll(v, 16, 1)

    mid = jnp.dot(gained(xs[req, :, rows_y, :].astype(F32), rows_of(0, 8, req)), weights(ad_v, rows_of(0, 8, 0)),
                  preferred_element_type=F32)
    for i in range(2):
        t = tenants(y * 16 + 8 * i)
        v = (jnp.where(owner == t, mid[8 * i:8 * i + 8, 0:128], 0.0)
             + jnp.where(owner + 8 == t, mid[8 * i:8 * i + 8, 128:256], 0.0))
        ad_s[i:i + 1, :] = jnp.sum(jnp.where(owner == sub, spread(v), 0.0), axis=0, keepdims=True)

    def rad_ref(b, yo):
        return rad.at[b, pl.ds(2 * yo, 2)]

    def d_copy(dx, dc, dy):
        yo, b = lax.rem(y + dy, 4), lax.rem(x + dx, 4) * 2 + lax.rem(core + dc, 2)
        return rcopy(ad_s, rad_ref(req, y), sd_s.at[dx * 2 + dc, dy], sd_r.at[req, y],
                     (lax.rem(yo, 2), b, lax.div(yo, 2) * 8 + z))

    for o in PLANE:
        d_copy(*o).start()
        drains.append(lambda o=o: d_copy(*o).wait_send())
    rad[req, pl.ds(2 * y, 2), :] = ad_s[...]

    def wait_d(o):
        i = lax.rem(req * 4 + y + o, 32)
        ref = rad_ref(lax.div(i, 4), lax.rem(i, 4))
        rcopy(ref, ref, sd_s.at[0, 0], sd_r.at[lax.div(i, 4), lax.rem(i, 4)], me).wait_recv()

    local[10].wait()
    local[11].wait()

    def gate_up(g, b, xg):
        return jnp.dot(xg, weights(wgu_v, rows_of(*RUNS[g], b)), preferred_element_type=F32)

    def forward(g, o):
        c_copy(g, o).start()
        drains.append(lambda: c_copy(g, o).wait_send())

    sq = jnp.zeros((64, 1), F32)
    gu = jnp.zeros((64, 256), F32)
    last = len(RUNS) - 1
    for g in range(len(RUNS)):
        for dy in (1, 3, 2):
            xy_wait(g, 0, dy)
        forward(g, 0)
        s1, xg = block(g, req)
        sq = sq + s1
        own_xg = xg
        if g == last:
            break
        gu = gu + gate_up(g, req, xg)
        for o in (1, 3, 2):
            for dy in (0, 1, 3, 2):
                xy_wait(g, o, dy)
            forward(g, o)
        for o in (1, 3, 2):
            b = lax.rem(x + o, 4) * 2 + core
            s1, xg = block(g, b)
            sq = sq + s1
            gu = gu + gate_up(g, b, xg)
        for o in (0, 1, 3, 2) if g else ():
            c_wait(g - 1, o)
            b = lax.rem(x + o, 4) * 2 + 1 - core
            s1, xg = block(g - 1, b)
            sq = sq + s1
            gu = gu + gate_up(g - 1, b, xg)
    gu = gu + gate_up(last, req, own_xg)
    for o in (1, 3, 2):
        for dy in (0, 1, 3, 2):
            xy_wait(last, o, dy)
        forward(last, o)
    for o in (1, 3, 2):
        b = lax.rem(x + o, 4) * 2 + core
        s1, xg = block(last, b)
        sq = sq + s1
        gu = gu + gate_up(last, b, xg)
    for g in range(max(last - 1, 0), last + 1):
        for o in (0, 1, 3, 2):
            c_wait(g, o)
            b = lax.rem(x + o, 4) * 2 + 1 - core
            s1, xg = block(g, b)
            sq = sq + s1
            gu = gu + gate_up(g, b, xg)

    loop(1, 32, wait_d)
    inv = lax.rsqrt(sq * (1.0 / 8192.0) + EPS)
    allmid = jnp.sum(rad[...], axis=0)
    chosen = []
    for i in range(8):
        t = tenants(8 * i)
        v = spread(jnp.where(owner == sub, jnp.broadcast_to(allmid[i:i + 1, :], (8, 128)), 0.0))
        v = v * inv[8 * i:8 * i + 8]
        chosen.append(jnp.concatenate(
            [jnp.where(owner == t, v, 0.0), jnp.where(owner + 8 == t, v, 0.0)], axis=1))
    local[9].wait()
    lowrank = jnp.dot(jnp.concatenate(chosen, axis=0).astype(BF16), tu_v[...], preferred_element_type=F32)
    gate = gu[:, 0:128] * inv
    up = gu[:, 128:256] * inv + 2.0 * lowrank
    hid = (gate / (1.0 + jnp.exp(-gate)) * up).astype(BF16)

    local[12].wait()

    def core_copy(g):
        return rcopy(dbuf.at[1 - core, g], rcore.at[g], ec_s.at[g], ec_r.at[g], at_req(x * 2 + 1 - core))

    def ex_copy(g, dx, dy):
        xo, yo = lax.rem(x + dx, 4), lax.rem(y + dy, 4)
        return rcopy(r1.at[g, xo, yo], rx.at[g, x, y], ex_s.at[g, dx, dy], ex_r.at[g, x, y], at_xy(xo, yo))

    def ez_copy(i):
        zo = lax.rem(z + Z_ALL[i], 8)
        return rcopy(r3.at[i], rz.at[z], ez_s.at[i], ez_r.at[z], at_z(zo))

    for g in range(GROUPS):
        for i in range(PER):
            zo = lax.rem(z + Z_ALL[g * PER + i], 8)
            for yy in range(4):
                col = pl.multiple_of(((yy % 2) * 16 + (yy // 2) * 8 + zo) * 256, 256)
                part = jnp.dot(hid, wd_v[:, pl.ds(col, 256)], preferred_element_type=F32)
                for b in range(8):
                    dbuf[b % 2, g, b // 2, yy, i] = jnp.concatenate(
                        [part[8 * b:8 * b + 8, 0:128], part[8 * b:8 * b + 8, 128:256]], axis=0).astype(BF16)
        core_copy(g).start()
        drains.append(lambda g=g: core_copy(g).wait_send())

    for g in range(GROUPS):
        core_copy(g).wait_recv()

        def fold_core(i):
            r1[g, i] = (dbuf[core, g, i].astype(F32) + rcore[g, i].astype(F32)).astype(BF16)

        loop(0, 4, fold_core)
        for o in XY_FAR:
            ex_copy(g, *o).start()
            drains.append(lambda g=g, o=o: ex_copy(g, *o).wait_send())
        rx[g, x, y] = r1[g, x, y]
        if g == 0:
            late, drains[:] = drains[-16:], drains[:-16]
            drain()
            drains.extend(late)

    own = []
    for h in range(2):
        c = yz * 2 + h
        away = lax.rem(lax.rem(c, 8) + 8 - z, 8)
        past = lax.div(away, 5)
        at = (1 - past) * (2 * away - 1) + past * (16 - 2 * away) + lax.div(8 - away, 8)
        t = xs[lax.div(c, 8), at, pl.ds(pl.multiple_of(x * 16, 16), 16), :].astype(F32)
        own.append(jnp.where(core == 0, t[0:8, :], t[8:16, :]))
    own = jnp.concatenate(own, axis=0)

    for g in range(GROUPS):
        def wait_ex(o):
            i = lax.rem(x * 4 + y + o, 16)
            xo, yo = lax.div(i, 4), lax.rem(i, 4)
            rcopy(rx.at[g, xo, yo], rx.at[g, xo, yo], ex_s.at[g, xo, yo], ex_r.at[g, xo, yo], me).wait_recv()

        loop(1, 16, wait_ex)
        for i in range(PER):
            part = rx[g, 0, 0, i].astype(F32)
            for j in range(1, 16):
                part = part + rx[g, j // 4, j % 4, i].astype(F32)
            if Z_ALL[g * PER + i]:
                r3[g * PER + i] = part.astype(BF16)
                ez_copy(g * PER + i).start()
                drains.append(lambda k=g * PER + i: ez_copy(k).wait_send())
            else:
                own = own + part
                rz[z] = jnp.zeros((16, 128), BF16)

    late, drains[:] = drains[-7:], drains[:-7]
    drain()
    drains.extend(late)

    def wait_ez(o):
        zo = lax.rem(z + o, 8)
        rcopy(rz.at[zo], rz.at[zo], ez_s.at[o], ez_r.at[zo], me).wait_recv()

    loop(1, 8, wait_ez)
    res = own + jnp.sum(rz[...].astype(F32), axis=0)
    out_ref[:, 0:128] = res[0:8, :].astype(BF16)
    out_ref[:, 128:256] = res[8:16, :].astype(BF16)
    drain()


def shards(query, cache_keys, cache_values, new_keys, new_values, lengths, residual_in, out_proj,
           norm_gain, adapter_down, tenant_adapter_up_matrix, tenant, w_gate, w_up, w_down):
    hbm = pl.BlockSpec(memory_space=pl.ANY)
    smem = pl.BlockSpec(memory_space=pltpu.SMEM)
    v = pltpu.VMEM
    dma = pltpu.SemaphoreType.DMA
    return pl.pallas_call(
        functools.partial(kernel, None),
        out_shape=jax.ShapeDtypeStruct((8, 256), BF16),
        in_specs=[hbm, hbm, hbm, hbm, hbm, smem, hbm, hbm, hbm, hbm, hbm, smem, hbm, hbm, hbm],
        out_specs=pl.BlockSpec(memory_space=pltpu.VMEM),
        scratch_shapes=[
            v((8, 8192), BF16), v((8, 128, 512), BF16), v((8, 128, 512), BF16), v((8, 512), BF16),
            v((8, 512), BF16), v((16, 128), BF16), v((512, 1024), BF16), v((64, 128), F32),
            v((1024, 256), BF16), v((256, 128), BF16), v((8192, 256), BF16), v((128, 8192), BF16),
            v((2, 8, 32, 128), BF16), v((8, 128), F32), v((8, 2, 32, 128), BF16), v((8, 8, 128), F32),
            v((128, 128), F32), v((8, 128), F32), v((2, 32, 128), BF16), v((2, 8, 8, 128), F32),
            v((2, 8, 32, 128), BF16), v((4, 8, 16, 128), BF16), v((32, 16, 128), BF16), v((8, 8, 64, 128), BF16),
            v((2, 128), F32), v((8, 8, 128), F32),
            v((2, GROUPS, 4, 4, PER, 16, 128), BF16), v((GROUPS, 4, 4, PER, 16, 128), BF16),
            v((GROUPS, 4, 4, PER, 16, 128), BF16), v((GROUPS, 4, 4, PER, 16, 128), BF16), v((8, 16, 128), BF16), v((8, 16, 128), BF16),
            dma((13,)),
            pltpu.SemaphoreType.REGULAR, dma((8,)), dma((8,)), dma((8,)), dma((8,)),
            dma((2, 8)), dma((2, 8)), dma((2, 8)), dma((2, 8)), dma((32,)), dma((32,)),
            dma((8,)), dma((8,)), dma((len(RUNS), 4, 4)), dma((len(RUNS), 4, 4)),
            dma((len(RUNS), 4)), dma((len(RUNS), 4)),
            dma((8, 4)), dma((8, 4)), dma((GROUPS,)), dma((GROUPS,)),
            dma((GROUPS, 4, 4)), dma((GROUPS, 4, 4)), dma((8,)), dma((8,)),
        ],
        compiler_params=pltpu.CompilerParams(
            collective_id=0, has_side_effects=True, vmem_limit_bytes=60 * 1024 * 1024),
    )(query, cache_keys, cache_values, new_keys, new_values, lengths, residual_in, out_proj,
      norm_gain.reshape(64, 128), adapter_down, tenant_adapter_up_matrix, tenant, w_gate, w_up, w_down)


def solution(mesh):
    placed = (
        P("req", "role"),
        P("req", "ctx", "role"),
        P("req", "ctx", "role"),
        P("req", "role"),
        P("req", "role"),
        P("req"),
        P(None, "req"),
        P(("role", "ctx"), "req"),
        P(),
        P("req", None),
        P(None, ("role", "req", "ctx")),
        P(),
        P(None, ("role", "req", "ctx")),
        P(None, ("role", "req", "ctx")),
        P(("role", "req", "ctx"), None),
    )
    return jax.shard_map(
        shards, mesh=mesh, in_specs=placed, out_specs=P("req", ("role", "ctx")), check_vma=False
    )
```

```python
import functools
import math

import jax
import jax.numpy as jnp
from jax import lax
from jax.experimental import pallas as pl
from jax.experimental.pallas import tpu as pltpu
from jax.sharding import PartitionSpec as P

MESH = pl.DeviceIdType.MESH
F32 = jnp.float32
BF16 = jnp.bfloat16
HD = 128
EPS = 1e-05
LOW = -1e30
NT = (((1,), (1,)), ((), ()))
Z_FAR = (4, 3, 5, 2, 6, 1, 7)
XY_FAR = ((2, 2), (1, 2), (3, 2), (2, 1), (2, 3), (1, 1), (1, 3), (3, 1), (3, 3),
          (2, 0), (0, 2), (1, 0), (3, 0), (0, 1), (0, 3))
XY_COLUMN = ((0, 2), (0, 1), (0, 3)) + XY_FAR[:9] + ((2, 0), (1, 0), (3, 0))
PARTS = ((0, 3), (3, 6), (6, 8))
Z_ALL = Z_FAR + (0,)
RING = (0, 1, 7, 2, 6, 3, 5, 4)
RUNS = ((0, 3), (3, 8))
PLANE = tuple((dx, dc, dy) for dx in (2, 1, 3, 0) for dy in (2, 1, 3, 0) for dc in (1, 0) if dx or dc or dy)
YZ_FAR = tuple((dy, dz) for dz in Z_FAR + (0,) for dy in (2, 1, 3, 0) if dy or dz)
HALF_FAR = tuple((dx, dc, dh) for dh in (1, 0) for dx in (2, 1, 3, 0) for dc in (1, 0) if dx or dc or dh)
REQ_FAR = ((2, 1), (2, 0), (1, 1), (3, 1), (1, 0), (3, 0), (0, 1))


def rcopy(src, dst, ssem, rsem, dev):
    return pltpu.make_async_remote_copy(
        src_ref=src, dst_ref=dst, send_sem=ssem, recv_sem=rsem, device_id=dev, device_id_type=MESH
    )


def loop(lo, hi, body):
    def step(i, carry):
        body(i)
        return carry

    lax.fori_loop(lo, hi, step, 0)


def kernel(
    stop,
    q_h, ck_h, cv_h, nk_h, nv_h, len_s, res_h, wo_h, gain_h, ad_h, tu_h, ten_s, wg_h, wu_h, wd_h,
    out_ref,
    q_v, ck_v, cv_v, nk_v, nv_v, res_v, wo_v, gain_v, ad_v, tu_v, wgu_v, wd_v,
    acc_s, stat_s, racc, rstat, rt_v, lse_s, oh_s,
    ogath, psend, rpart, xs, ad_s, rad, dbuf, rcore, r1, rx, r3, rz,
    lsem,
    go, sa_s, sa_r, ss_s, ss_r, so_s, so_r, sp_s, sp_r, sz_s, sz_r, sx_s, sx_r, sc_s, sc_r,
    sd_s, sd_r, ec_s, ec_r, ex_s, ex_r, ez_s, ez_r,
):
    role = lax.axis_index("role")
    req = lax.axis_index("req")
    ctx = lax.axis_index("ctx")
    x = lax.div(req, 2)
    core = lax.rem(req, 2)
    yhi = lax.div(ctx, 8)
    z = lax.rem(ctx, 8)
    y = yhi * 2 + role
    yz = role * 16 + ctx
    me = (role, req, ctx)

    def at_req(i):
        return (role, i, ctx)

    def at_xy(xo, yo):
        return (lax.rem(yo, 2), xo * 2 + core, lax.div(yo, 2) * 8 + z)

    def at_y(i):
        return (lax.rem(i, 2), req, lax.div(i, 2) * 8 + z)

    def at_z(i):
        return (role, req, yhi * 8 + i)

    barrier = pltpu.get_barrier_semaphore()

    def greet(dev):
        pl.semaphore_signal(barrier, inc=1, device_id=dev, device_id_type=MESH)

    for o in Z_FAR:
        greet(at_z(lax.rem(z + o, 8)))
    for dx, dc in REQ_FAR:
        greet(at_req(lax.rem(x + dx, 4) * 2 + lax.rem(core + dc, 2)))
    for o in (2, 1, 3):
        greet(at_y(lax.rem(y + o, 4)))

    drains = []

    def drain():
        while drains:
            drains.pop(0)()

    local = [
        pltpu.make_async_copy(q_h, q_v, lsem.at[0]),
        pltpu.make_async_copy(ck_h, ck_v, lsem.at[1]),
        pltpu.make_async_copy(cv_h, cv_v, lsem.at[2]),
        pltpu.make_async_copy(nk_h, nk_v, lsem.at[3]),
        pltpu.make_async_copy(nv_h, nv_v, lsem.at[4]),
        pltpu.make_async_copy(wo_h, wo_v, lsem.at[5]),
        pltpu.make_async_copy(
            res_h.at[pl.ds(pl.multiple_of(y * 16, 16), 16), pl.ds(pl.multiple_of(z * 128, 128), 128)],
            res_v, lsem.at[6],
        ),
        pltpu.make_async_copy(gain_h, gain_v, lsem.at[7]),
        pltpu.make_async_copy(ad_h, ad_v, lsem.at[8]),
        pltpu.make_async_copy(tu_h, tu_v, lsem.at[9]),
        pltpu.make_async_copy(wg_h, wgu_v.at[:, pl.ds(0, 128)], lsem.at[10]),
        pltpu.make_async_copy(wu_h, wgu_v.at[:, pl.ds(128, 128)], lsem.at[11]),
        pltpu.make_async_copy(wd_h, wd_v, lsem.at[12]),
    ]
    for i in (0, 1, 3, 2, 4, 5, 6, 7, 8, 9, 10, 11, 12):
        local[i].start()

    factor = 1.0 / math.sqrt(HD)
    sub = lax.broadcasted_iota(jnp.int32, (8, 128), 0)
    lane = lax.broadcasted_iota(jnp.int32, (8, 128), 1)
    lens = jnp.zeros((8, 128), jnp.int32)
    for r in range(8):
        lens = jnp.where(sub == r, len_s[r], lens)
    usable = (ctx * 128 + lane < lens)[None]
    rowmod = lax.broadcasted_iota(jnp.int32, (16, 8, 128), 1)
    stat_lane = lax.broadcasted_iota(jnp.int32, (128, 128), 1)
    local[0].wait()
    local[1].wait()
    local[3].wait()
    probs = []
    fresh = []
    stat = jnp.zeros((128, 128), F32)
    for k in range(4):
        qk = jnp.concatenate(
            [q_v[:, (k * 16 + g) * 128:(k * 16 + g + 1) * 128].astype(F32) for g in range(16)], axis=0)
        nk = nk_v[:, k * 128:(k + 1) * 128].astype(F32)
        own = jnp.sum(qk.reshape(16, 8, 128) * nk[None], axis=-1, keepdims=True) * factor
        own = jnp.where(ctx == 0, own, LOW)
        kk = ck_v[:, :, k * 128:(k + 1) * 128].reshape(1024, 128)
        full = lax.dot_general(qk.astype(BF16), kk, NT, preferred_element_type=F32)
        sc = jnp.zeros((16, 8, 128), F32)
        for r in range(8):
            sc = jnp.where(rowmod == r, full[:, r * 128:(r + 1) * 128].reshape(16, 8, 128), sc)
        sc = jnp.where(usable, sc * factor, LOW)
        top = jnp.maximum(jnp.max(sc, axis=-1, keepdims=True), own)
        w = jnp.where(usable, jnp.exp(sc - top), 0.0)
        wb = w.astype(BF16).astype(F32)
        w_own = jnp.where(ctx == 0, jnp.exp(own - top), 0.0)
        tot = jnp.sum(wb, axis=-1, keepdims=True) + w_own
        probs.append(wb)
        fresh.append(w_own)
        stat = jnp.where(stat_lane == 2 * k, top.reshape(128, 1), stat)
        stat = jnp.where(stat_lane == 2 * k + 1, tot.reshape(128, 1), stat)
    stat_s[...] = stat.T[0:8, :]

    pl.semaphore_wait(barrier, 17)
    for o in (2, 1, 3):
        pl.semaphore_signal(go, inc=1, device_id=at_y(lax.rem(y + o, 4)), device_id_type=MESH)

    def stat_copy(o):
        return rcopy(stat_s, rstat.at[z], ss_s.at[o], ss_r.at[z], at_z(lax.rem(z + o, 8)))

    def half(n):
        return 1 - yhi if n == 0 else yhi

    def acc_copy(n, o):
        zo = lax.rem(z + o, 8)
        return rcopy(acc_s.at[half(n), zo], racc.at[z, half(n)], sa_s.at[n, o], sa_r.at[n, z], at_z(zo))

    for o in Z_FAR:
        stat_copy(o).start()
        drains.append(lambda o=o: stat_copy(o).wait_send())
    rstat[z] = stat_s[...]
    local[2].wait()
    local[4].wait()
    for k in range(4):
        big = jnp.concatenate(
            [jnp.where(rowmod == r, probs[k], 0.0).reshape(128, 128).astype(BF16) for r in range(8)], axis=1)
        vk = cv_v[:, :, k * 128:(k + 1) * 128].reshape(1024, 128)
        acc = jnp.dot(big, vk, preferred_element_type=F32).reshape(16, 8, 128)
        acc = acc + fresh[k] * nv_v[:, k * 128:(k + 1) * 128].astype(F32)[None]
        acc_s[k // 2, (k % 2) * 4:(k % 2) * 4 + 4] = acc.reshape(4, 32, 128).astype(BF16)
    for n in range(2):
        for o in Z_FAR:
            acc_copy(n, o).start()
            drains.append(lambda n=n, o=o: acc_copy(n, o).wait_send())
    for j in range(2):
        racc[z, j] = acc_s[j, z]

    def wait_stat(o):
        c = lax.rem(z + o, 8)
        rcopy(stat_s, rstat.at[c], ss_s.at[o], ss_r.at[c], me).wait_recv()

    loop(1, 8, wait_stat)
    rs = rstat[...]
    high = jnp.max(rs, axis=0)
    scale = jnp.exp(rs - high[None])
    den = jnp.maximum(jnp.sum(scale * pltpu.roll(rs, 7, 1), axis=0), 1e-30)
    lse = high + jnp.log(den)
    lse_s[...] = lse
    flat = (scale / den[None]).reshape(64, 128)
    rt_v[...] = jnp.concatenate([flat, flat], axis=0).T
    kz = lax.div(z, 4)
    rows_z = pl.ds(pl.multiple_of(lax.rem(z, 4) * 32, 32), 32)
    st = rt_v[rows_z, :]
    st = jnp.where(kz == 0, st, pltpu.roll(st, 126, 1))
    def h_peer(dx, dc, dh):
        return lax.rem(yhi + dh, 2), lax.rem(x + dx, 4) * 2 + lax.rem(core + dc, 2)

    def o_copy(dx, dc, dh):
        h, b = h_peer(dx, dc, dh)
        return rcopy(oh_s.at[h], ogath.at[yhi, req], so_s.at[dh, dx * 2 + dc], so_r.at[yhi, req],
                     (role, b, h * 8 + z))

    for n in range(2):
        def wait_acc(o):
            c = lax.rem(z + o, 8)
            ref = racc.at[c, half(n)]
            rcopy(ref, ref, sa_s.at[n, o], sa_r.at[n, c], me).wait_recv()

        loop(1, 8, wait_acc)
        mine = jnp.where(half(n) == 0, st, pltpu.roll(st, 124, 1))
        part = jnp.zeros((32, 128), F32)
        for c in range(8):
            part = part + mine[:, 8 * c:8 * c + 1] * racc[c, half(n)].astype(F32)
        row = lse_s[pl.ds(4 * half(n) + 2 * kz, 1), :]
        head = row.astype(BF16).astype(F32)
        middle = (row - head).astype(BF16).astype(F32)
        oh_s[half(n)] = jnp.concatenate(
            [part, head, middle, row - head - middle, jnp.zeros((13, 128), F32)], axis=0).astype(BF16)
        if n == 0:
            pl.semaphore_wait(go, 3)
        for o in HALF_FAR:
            if o[2] == 1 - n:
                o_copy(*o).start()
    drain()

    def drain_o():
        for o in HALF_FAR:
            o_copy(*o).wait_send()

    drains.append(drain_o)
    ogath[yhi, req] = oh_s[yhi]

    def wait_o(o):
        i = lax.rem(yhi * 8 + req + o, 16)
        h, b = lax.div(i, 8), lax.rem(i, 8)
        rcopy(ogath.at[h, b], ogath.at[h, b], so_s.at[h, b], so_r.at[h, b], me).wait_recv()

    loop(1, 16, wait_o)
    logs = jnp.sum(ogath[:, :, 32:48, :].astype(F32), axis=2)
    gap = logs[1] - logs[0]
    both = jnp.concatenate(
        [1.0 / (1.0 + jnp.exp(gap)), 1.0 / (1.0 + jnp.exp(-gap)), jnp.zeros((112, 128), F32)], axis=0)
    rt_v[...] = both.T
    st = rt_v[rows_z, :]
    heads = []
    for b in range(8):
        heads.append(st[:, b:b + 1] * ogath[0, b, 0:32].astype(F32)
                     + st[:, 8 + b:9 + b] * ogath[1, b, 0:32].astype(F32))
    attn = jnp.concatenate(
        [jnp.concatenate([heads[b][8 * g:8 * g + 8, :] for b in range(8)], axis=0) for g in range(4)],
        axis=1).astype(BF16)
    local[5].wait()
    proj = jnp.dot(attn, wo_v[...], preferred_element_type=F32)
    for yy in range(4):
        for zz in range(8):
            psend[yy, zz] = proj[16 * yy:16 * yy + 16, 128 * zz:128 * zz + 128].astype(BF16)

    def p_copy(dy, dz):
        yo, zo = lax.rem(y + dy, 4), lax.rem(z + dz, 8)
        return rcopy(psend.at[yo, zo], rpart.at[yz], sp_s.at[dy * 8 + dz], sp_r.at[yz],
                     (lax.rem(yo, 2), req, lax.div(yo, 2) * 8 + zo))

    for o in YZ_FAR:
        p_copy(*o).start()
    drain()

    def drain_p():
        for o in YZ_FAR:
            p_copy(*o).wait_send()

    drains.append(drain_p)
    rpart[yz] = psend[y, z]

    def wait_p(o):
        c = lax.rem(yz + o, 32)
        rcopy(rpart.at[c], rpart.at[c], sp_s.at[o], sp_r.at[c], me).wait_recv()

    loop(1, 32, wait_p)
    local[6].wait()
    piece = res_v[...].astype(F32) + jnp.sum(rpart[...].astype(F32), axis=0)
    rows_y = pl.ds(pl.multiple_of(y * 16, 16), 16)
    xs[req, 0, rows_y, :] = piece.astype(BF16)

    def z_copy(o):
        at = RING.index((8 - o) % 8)
        return rcopy(xs.at[req, 0, rows_y], xs.at[req, at, rows_y], sz_s.at[o], sz_r.at[at],
                     at_z(lax.rem(z + o, 8)))

    def y_ref(g, b, yo):
        lo, hi = RUNS[g]
        return xs.at[b, pl.ds(lo, hi - lo), pl.ds(pl.multiple_of(yo * 16, 16), 16)]

    def xy_copy(g, dx, dy):
        return rcopy(y_ref(g, req, y), y_ref(g, req, y), sx_s.at[g, dx, dy], sx_r.at[g, x, y],
                     at_xy(lax.rem(x + dx, 4), lax.rem(y + dy, 4)))

    def xy_wait(g, dx, dy):
        xo, yo = lax.rem(x + dx, 4), lax.rem(y + dy, 4)
        ref = y_ref(g, xo * 2 + core, yo)
        rcopy(ref, ref, sx_s.at[g, dx, dy], sx_r.at[g, xo, yo], me).wait_recv()

    def b_ref(g, b):
        lo, hi = RUNS[g]
        return xs.at[b, pl.ds(lo, hi - lo)]

    def c_copy(g, o):
        xo = lax.rem(x + o, 4)
        ref = b_ref(g, xo * 2 + core)
        return rcopy(ref, ref, sc_s.at[g, o], sc_r.at[g, xo], at_req(x * 2 + 1 - core))

    def c_wait(g, o):
        xo = lax.rem(x + o, 4)
        ref = b_ref(g, xo * 2 + 1 - core)
        rcopy(ref, ref, sc_s.at[g, o], sc_r.at[g, xo], me).wait_recv()

    for o in Z_FAR:
        z_copy(o).start()
    for g, (lo, hi) in enumerate(RUNS):
        for at in range(max(lo, 1), hi):
            ref = xs.at[req, at, rows_y]
            rcopy(ref, ref, sz_s.at[at], sz_r.at[at], me).wait_recv()
        for o in XY_COLUMN:
            xy_copy(g, *o).start()
        if g == 0:
            drain()
    for o in Z_FAR:
        drains.append(lambda o=o: z_copy(o).wait_send())
    for g in range(len(RUNS)):
        for o in XY_COLUMN:
            drains.append(lambda g=g, o=o: xy_copy(g, *o).wait_send())
    def rows_of(lo, hi, b):
        return [b * 8 + lax.rem(z + RING[at], 8) for at in range(lo, hi)]

    def gained(xb, chunks):
        xg = [xb[i] * gain_v[pl.ds(c, 1), :] for i, c in enumerate(chunks)]
        return jnp.concatenate(xg, axis=1).astype(BF16)

    def block(g, b):
        lo, hi = RUNS[g]
        xb = xs[b, lo:hi].astype(F32)
        sq = jnp.sum(jnp.sum(xb * xb, axis=0), axis=-1, keepdims=True)
        return sq, gained(xb, rows_of(lo, hi, b))

    def weights(ref, chunks):
        return jnp.concatenate([ref[pl.ds(pl.multiple_of(c * 128, 128), 128), :] for c in chunks], axis=0)

    local[7].wait()
    local[8].wait()
    owner = lax.div(lane, 16)

    def tenants(first):
        t = jnp.zeros((8, 128), jnp.int32)
        for r in range(8):
            t = jnp.where(sub == r, ten_s[first + r], t)
        return t

    def spread(v):
        v = v + pltpu.roll(v, 64, 1)
        v = v + pltpu.roll(v, 32, 1)
        return v + pltpu.roll(v, 16, 1)

    mid = jnp.dot(gained(xs[req, :, rows_y, :].astype(F32), rows_of(0, 8, req)), weights(ad_v, rows_of(0, 8, 0)),
                  preferred_element_type=F32)
    for i in range(2):
        t = tenants(y * 16 + 8 * i)
        v = (jnp.where(owner == t, mid[8 * i:8 * i + 8, 0:128], 0.0)
             + jnp.where(owner + 8 == t, mid[8 * i:8 * i + 8, 128:256], 0.0))
        ad_s[i:i + 1, :] = jnp.sum(jnp.where(owner == sub, spread(v), 0.0), axis=0, keepdims=True)

    def rad_ref(b, yo):
        return rad.at[b, pl.ds(2 * yo, 2)]

    def d_copy(dx, dc, dy):
        yo, b = lax.rem(y + dy, 4), lax.rem(x + dx, 4) * 2 + lax.rem(core + dc, 2)
        return rcopy(ad_s, rad_ref(req, y), sd_s.at[dx * 2 + dc, dy], sd_r.at[req, y],
                     (lax.rem(yo, 2), b, lax.div(yo, 2) * 8 + z))

    for o in PLANE:
        d_copy(*o).start()
        drains.append(lambda o=o: d_copy(*o).wait_send())
    rad[req, pl.ds(2 * y, 2), :] = ad_s[...]

    def wait_d(o):
        i = lax.rem(req * 4 + y + o, 32)
        ref = rad_ref(lax.div(i, 4), lax.rem(i, 4))
        rcopy(ref, ref, sd_s.at[0, 0], sd_r.at[lax.div(i, 4), lax.rem(i, 4)], me).wait_recv()

    local[10].wait()
    local[11].wait()

    def gate_up(g, b, xg):
        return jnp.dot(xg, weights(wgu_v, rows_of(*RUNS[g], b)), preferred_element_type=F32)

    def forward(g, o):
        c_copy(g, o).start()
        drains.append(lambda: c_copy(g, o).wait_send())

    sq = jnp.zeros((64, 1), F32)
    gu = jnp.zeros((64, 256), F32)
    last = len(RUNS) - 1
    for g in range(len(RUNS)):
        for dy in (1, 3, 2):
            xy_wait(g, 0, dy)
        forward(g, 0)
        s1, xg = block(g, req)
        sq = sq + s1
        own_xg = xg
        if g == last:
            break
        gu = gu + gate_up(g, req, xg)
        for o in (1, 3, 2):
            for dy in (0, 1, 3, 2):
                xy_wait(g, o, dy)
            forward(g, o)
        for o in (1, 3, 2):
            b = lax.rem(x + o, 4) * 2 + core
            s1, xg = block(g, b)
            sq = sq + s1
            gu = gu + gate_up(g, b, xg)
        for o in (0, 1, 3, 2) if g else ():
            c_wait(g - 1, o)
            b = lax.rem(x + o, 4) * 2 + 1 - core
            s1, xg = block(g - 1, b)
            sq = sq + s1
            gu = gu + gate_up(g - 1, b, xg)
    gu = gu + gate_up(last, req, own_xg)
    for o in (1, 3, 2):
        for dy in (0, 1, 3, 2):
            xy_wait(last, o, dy)
        forward(last, o)
    for o in (1, 3, 2):
        b = lax.rem(x + o, 4) * 2 + core
        s1, xg = block(last, b)
        sq = sq + s1
        gu = gu + gate_up(last, b, xg)
    for g in range(max(last - 1, 0), last + 1):
        for o in (0, 1, 3, 2):
            c_wait(g, o)
            b = lax.rem(x + o, 4) * 2 + 1 - core
            s1, xg = block(g, b)
            sq = sq + s1
            gu = gu + gate_up(g, b, xg)

    loop(1, 32, wait_d)
    inv = lax.rsqrt(sq * (1.0 / 8192.0) + EPS)
    allmid = jnp.sum(rad[...], axis=0)
    chosen = []
    for i in range(8):
        t = tenants(8 * i)
        v = spread(jnp.where(owner == sub, jnp.broadcast_to(allmid[i:i + 1, :], (8, 128)), 0.0))
        v = v * inv[8 * i:8 * i + 8]
        chosen.append(jnp.concatenate(
            [jnp.where(owner == t, v, 0.0), jnp.where(owner + 8 == t, v, 0.0)], axis=1))
    local[9].wait()
    lowrank = jnp.dot(jnp.concatenate(chosen, axis=0).astype(BF16), tu_v[...], preferred_element_type=F32)
    gate = gu[:, 0:128] * inv
    up = gu[:, 128:256] * inv + 2.0 * lowrank
    hid = (gate / (1.0 + jnp.exp(-gate)) * up).astype(BF16)

    local[12].wait()

    def part_of(g):
        lo, hi = PARTS[g]
        return pl.ds(lo, hi - lo)

    def core_copy(g):
        return rcopy(dbuf.at[1 - core, :, :, part_of(g)], rcore.at[:, :, part_of(g)], ec_s.at[g], ec_r.at[g],
                     at_req(x * 2 + 1 - core))

    def ex_copy(g, dx, dy):
        xo, yo = lax.rem(x + dx, 4), lax.rem(y + dy, 4)
        return rcopy(r1.at[xo, yo, part_of(g)], rx.at[x, y, part_of(g)], ex_s.at[g, dx, dy], ex_r.at[g, x, y],
                     at_xy(xo, yo))

    def ez_copy(i):
        zo = lax.rem(z + Z_ALL[i], 8)
        return rcopy(r3.at[i], rz.at[z], ez_s.at[i], ez_r.at[z], at_z(zo))

    for g, (lo, hi) in enumerate(PARTS):
        for i in range(lo, hi):
            zo = lax.rem(z + Z_ALL[i], 8)
            for yy in range(4):
                col = pl.multiple_of(((yy % 2) * 16 + (yy // 2) * 8 + zo) * 256, 256)
                part = jnp.dot(hid, wd_v[:, pl.ds(col, 256)], preferred_element_type=F32)
                for b in range(8):
                    dbuf[b % 2, b // 2, yy, i] = jnp.concatenate(
                        [part[8 * b:8 * b + 8, 0:128], part[8 * b:8 * b + 8, 128:256]], axis=0).astype(BF16)
        core_copy(g).start()
        drains.append(lambda g=g: core_copy(g).wait_send())

    for g, (lo, hi) in enumerate(PARTS):
        core_copy(g).wait_recv()

        def fold_core(i):
            r1[i, :, lo:hi] = (dbuf[core, i, :, lo:hi].astype(F32) + rcore[i, :, lo:hi].astype(F32)).astype(BF16)

        loop(0, 4, fold_core)
        for o in XY_FAR:
            ex_copy(g, *o).start()
            drains.append(lambda g=g, o=o: ex_copy(g, *o).wait_send())
        rx[x, y, lo:hi] = r1[x, y, lo:hi]
        if g == 0:
            late, drains[:] = drains[-16:], drains[:-16]
            drain()
            drains.extend(late)

    own = []
    for h in range(2):
        c = yz * 2 + h
        away = lax.rem(lax.rem(c, 8) + 8 - z, 8)
        past = lax.div(away, 5)
        at = (1 - past) * (2 * away - 1) + past * (16 - 2 * away) + lax.div(8 - away, 8)
        t = xs[lax.div(c, 8), at, pl.ds(pl.multiple_of(x * 16, 16), 16), :].astype(F32)
        own.append(jnp.where(core == 0, t[0:8, :], t[8:16, :]))
    own = jnp.concatenate(own, axis=0)

    for g, (lo, hi) in enumerate(PARTS):
        def wait_ex(o):
            i = lax.rem(x * 4 + y + o, 16)
            xo, yo = lax.div(i, 4), lax.rem(i, 4)
            ref = rx.at[xo, yo, part_of(g)]
            rcopy(ref, ref, ex_s.at[g, xo, yo], ex_r.at[g, xo, yo], me).wait_recv()

        loop(1, 16, wait_ex)
        for i in range(lo, hi):
            part = rx[0, 0, i].astype(F32)
            for j in range(1, 16):
                part = part + rx[j // 4, j % 4, i].astype(F32)
            if Z_ALL[i]:
                r3[i] = part.astype(BF16)
                ez_copy(i).start()
                drains.append(lambda k=i: ez_copy(k).wait_send())
            else:
                own = own + part
                rz[z] = jnp.zeros((16, 128), BF16)

    late, drains[:] = drains[-7:], drains[:-7]
    drain()
    drains.extend(late)

    def wait_ez(o):
        zo = lax.rem(z + o, 8)
        rcopy(rz.at[zo], rz.at[zo], ez_s.at[o], ez_r.at[zo], me).wait_recv()

    loop(1, 8, wait_ez)
    res = own + jnp.sum(rz[...].astype(F32), axis=0)
    out_ref[:, 0:128] = res[0:8, :]
    out_ref[:, 128:256] = res[8:16, :]
    drain()


def shards(query, cache_keys, cache_values, new_keys, new_values, lengths, residual_in, out_proj,
           norm_gain, adapter_down, tenant_adapter_up_matrix, tenant, w_gate, w_up, w_down):
    hbm = pl.BlockSpec(memory_space=pl.ANY)
    smem = pl.BlockSpec(memory_space=pltpu.SMEM)
    v = pltpu.VMEM
    dma = pltpu.SemaphoreType.DMA
    return pl.pallas_call(
        functools.partial(kernel, None),
        out_shape=jax.ShapeDtypeStruct((8, 256), F32),
        in_specs=[hbm, hbm, hbm, hbm, hbm, smem, hbm, hbm, hbm, hbm, hbm, smem, hbm, hbm, hbm],
        out_specs=pl.BlockSpec(memory_space=pltpu.VMEM),
        scratch_shapes=[
            v((8, 8192), BF16), v((8, 128, 512), BF16), v((8, 128, 512), BF16), v((8, 512), BF16),
            v((8, 512), BF16), v((16, 128), BF16), v((512, 1024), BF16), v((64, 128), F32),
            v((1024, 256), BF16), v((256, 128), BF16), v((8192, 256), BF16), v((128, 8192), BF16),
            v((2, 8, 32, 128), BF16), v((8, 128), F32), v((8, 2, 32, 128), BF16), v((8, 8, 128), F32),
            v((128, 128), F32), v((8, 128), F32), v((2, 48, 128), BF16),
            v((2, 8, 48, 128), BF16), v((4, 8, 16, 128), BF16), v((32, 16, 128), BF16), v((8, 8, 64, 128), BF16),
            v((2, 128), F32), v((8, 8, 128), F32),
            v((2, 4, 4, 8, 16, 128), BF16), v((4, 4, 8, 16, 128), BF16), v((4, 4, 8, 16, 128), BF16),
            v((4, 4, 8, 16, 128), BF16), v((8, 16, 128), BF16), v((8, 16, 128), BF16),
            dma((13,)),
            pltpu.SemaphoreType.REGULAR, dma((2, 8)), dma((2, 8)), dma((8,)), dma((8,)),
            dma((2, 8)), dma((2, 8)), dma((32,)), dma((32,)),
            dma((8,)), dma((8,)), dma((len(RUNS), 4, 4)), dma((len(RUNS), 4, 4)),
            dma((len(RUNS), 4)), dma((len(RUNS), 4)),
            dma((8, 4)), dma((8, 4)), dma((len(PARTS),)), dma((len(PARTS),)),
            dma((len(PARTS), 4, 4)), dma((len(PARTS), 4, 4)), dma((8,)), dma((8,)),
        ],
        compiler_params=pltpu.CompilerParams(
            collective_id=0, has_side_effects=True, vmem_limit_bytes=60 * 1024 * 1024),
    )(query, cache_keys, cache_values, new_keys, new_values, lengths, residual_in, out_proj,
      norm_gain.reshape(64, 128), adapter_down, tenant_adapter_up_matrix, tenant, w_gate, w_up, w_down).astype(BF16)


def solution(mesh):
    placed = (
        P("req", "role"),
        P("req", "ctx", "role"),
        P("req", "ctx", "role"),
        P("req", "role"),
        P("req", "role"),
        P("req"),
        P(None, "req"),
        P(("role", "ctx"), "req"),
        P(),
        P("req", None),
        P(None, ("role", "req", "ctx")),
        P(),
        P(None, ("role", "req", "ctx")),
        P(None, ("role", "req", "ctx")),
        P(("role", "req", "ctx"), None),
    )
    return jax.shard_map(
        shards, mesh=mesh, in_specs=placed, out_specs=P("req", ("role", "ctx")), check_vma=False
    )
```

```python
import functools
import math

import jax
import jax.numpy as jnp
from jax import lax
from jax.experimental import pallas as pl
from jax.experimental.pallas import tpu as pltpu
from jax.sharding import PartitionSpec as P

MESH = pl.DeviceIdType.MESH
F32 = jnp.float32
BF16 = jnp.bfloat16
HD = 128
EPS = 1e-05
LOW = -1e30
NT = (((1,), (1,)), ((), ()))
Z_FAR = (4, 3, 5, 2, 6, 1, 7)
XY_FAR = ((2, 2), (1, 2), (3, 2), (2, 1), (2, 3), (1, 1), (1, 3), (3, 1), (3, 3),
          (2, 0), (0, 2), (1, 0), (3, 0), (0, 1), (0, 3))
XY_COLUMN = ((0, 2), (0, 1), (0, 3)) + XY_FAR[:9] + ((2, 0), (1, 0), (3, 0))
PARTS = ((0, 3), (3, 6), (6, 8))
Z_ALL = Z_FAR + (0,)
RING = (0, 1, 7, 2, 6, 3, 5, 4)
RUNS = ((0, 4), (4, 8))
PLANE = tuple((dx, dc, dy) for dx in (2, 1, 3, 0) for dy in (2, 1, 3, 0) for dc in (1, 0) if dx or dc or dy)
YZ_FAR = tuple((dy, dz) for dz in Z_FAR + (0,) for dy in (2, 1, 3, 0) if dy or dz)
HALF_FAR = tuple((dx, dc, dh) for dh in (1, 0) for dx in (2, 1, 3, 0) for dc in (1, 0) if dx or dc or dh)
REQ_FAR = ((2, 1), (2, 0), (1, 1), (3, 1), (1, 0), (3, 0), (0, 1))


def rcopy(src, dst, ssem, rsem, dev):
    return pltpu.make_async_remote_copy(
        src_ref=src, dst_ref=dst, send_sem=ssem, recv_sem=rsem, device_id=dev, device_id_type=MESH
    )


def loop(lo, hi, body):
    def step(i, carry):
        body(i)
        return carry

    lax.fori_loop(lo, hi, step, 0)


def kernel(
    stop,
    q_h, ck_h, cv_h, nk_h, nv_h, len_s, res_h, wo_h, gain_h, ad_h, tu_h, ten_s, wg_h, wu_h, wd_h,
    out_ref,
    q_v, ck_v, cv_v, nk_v, nv_v, res_v, wo_v, gain_v, ad_v, tu_v, wgu_v, wd_v,
    acc_s, stat_s, racc, rstat, rt_v, lse_s, oh_s,
    ogath, psend, rpart, xs, ad_s, rad, dbuf, rcore, r1, rx, r3, rz,
    lsem,
    go, sa_s, sa_r, ss_s, ss_r, so_s, so_r, sp_s, sp_r, sz_s, sz_r, sx_s, sx_r, sc_s, sc_r,
    sd_s, sd_r, ec_s, ec_r, ex_s, ex_r, ez_s, ez_r,
):
    role = lax.axis_index("role")
    req = lax.axis_index("req")
    ctx = lax.axis_index("ctx")
    x = lax.div(req, 2)
    core = lax.rem(req, 2)
    yhi = lax.div(ctx, 8)
    z = lax.rem(ctx, 8)
    y = yhi * 2 + role
    yz = role * 16 + ctx
    me = (role, req, ctx)

    def at_req(i):
        return (role, i, ctx)

    def at_xy(xo, yo):
        return (lax.rem(yo, 2), xo * 2 + core, lax.div(yo, 2) * 8 + z)

    def at_y(i):
        return (lax.rem(i, 2), req, lax.div(i, 2) * 8 + z)

    def at_z(i):
        return (role, req, yhi * 8 + i)

    barrier = pltpu.get_barrier_semaphore()

    def greet(dev):
        pl.semaphore_signal(barrier, inc=1, device_id=dev, device_id_type=MESH)

    for o in Z_FAR:
        greet(at_z(lax.rem(z + o, 8)))
    for dx, dc in REQ_FAR:
        greet(at_req(lax.rem(x + dx, 4) * 2 + lax.rem(core + dc, 2)))
    for o in (2, 1, 3):
        greet(at_y(lax.rem(y + o, 4)))

    drains = []

    def drain():
        while drains:
            drains.pop(0)()

    local = [
        pltpu.make_async_copy(q_h, q_v, lsem.at[0]),
        pltpu.make_async_copy(ck_h, ck_v, lsem.at[1]),
        pltpu.make_async_copy(cv_h, cv_v, lsem.at[2]),
        pltpu.make_async_copy(nk_h, nk_v, lsem.at[3]),
        pltpu.make_async_copy(nv_h, nv_v, lsem.at[4]),
        pltpu.make_async_copy(wo_h, wo_v, lsem.at[5]),
        pltpu.make_async_copy(
            res_h.at[pl.ds(pl.multiple_of(y * 16, 16), 16), pl.ds(pl.multiple_of(z * 128, 128), 128)],
            res_v, lsem.at[6],
        ),
        pltpu.make_async_copy(gain_h, gain_v, lsem.at[7]),
        pltpu.make_async_copy(ad_h, ad_v, lsem.at[8]),
        pltpu.make_async_copy(tu_h, tu_v, lsem.at[9]),
        pltpu.make_async_copy(wg_h, wgu_v.at[:, pl.ds(0, 128)], lsem.at[10]),
        pltpu.make_async_copy(wu_h, wgu_v.at[:, pl.ds(128, 128)], lsem.at[11]),
        pltpu.make_async_copy(wd_h, wd_v, lsem.at[12]),
    ]
    for i in (0, 1, 3, 2, 4, 5, 6, 7, 8, 9, 10, 11, 12):
        local[i].start()

    factor = 1.0 / math.sqrt(HD)
    sub = lax.broadcasted_iota(jnp.int32, (8, 128), 0)
    lane = lax.broadcasted_iota(jnp.int32, (8, 128), 1)
    lens = jnp.zeros((8, 128), jnp.int32)
    for r in range(8):
        lens = jnp.where(sub == r, len_s[r], lens)
    usable = (ctx * 128 + lane < lens)[None]
    rowmod = lax.broadcasted_iota(jnp.int32, (16, 8, 128), 1)
    stat_lane = lax.broadcasted_iota(jnp.int32, (128, 128), 1)
    local[0].wait()
    local[1].wait()
    local[3].wait()
    probs = []
    fresh = []
    stat = jnp.zeros((128, 128), F32)
    for k in range(4):
        qk = jnp.concatenate(
            [q_v[:, (k * 16 + g) * 128:(k * 16 + g + 1) * 128].astype(F32) for g in range(16)], axis=0)
        nk = nk_v[:, k * 128:(k + 1) * 128].astype(F32)
        own = jnp.sum(qk.reshape(16, 8, 128) * nk[None], axis=-1, keepdims=True) * factor
        own = jnp.where(ctx == 0, own, LOW)
        kk = ck_v[:, :, k * 128:(k + 1) * 128].reshape(1024, 128)
        full = lax.dot_general(qk.astype(BF16), kk, NT, preferred_element_type=F32)
        sc = jnp.zeros((16, 8, 128), F32)
        for r in range(8):
            sc = jnp.where(rowmod == r, full[:, r * 128:(r + 1) * 128].reshape(16, 8, 128), sc)
        sc = jnp.where(usable, sc * factor, LOW)
        top = jnp.maximum(jnp.max(sc, axis=-1, keepdims=True), own)
        w = jnp.where(usable, jnp.exp(sc - top), 0.0)
        wb = w.astype(BF16).astype(F32)
        w_own = jnp.where(ctx == 0, jnp.exp(own - top), 0.0)
        tot = jnp.sum(wb, axis=-1, keepdims=True) + w_own
        probs.append(wb)
        fresh.append(w_own)
        stat = jnp.where(stat_lane == 2 * k, top.reshape(128, 1), stat)
        stat = jnp.where(stat_lane == 2 * k + 1, tot.reshape(128, 1), stat)
    stat_s[...] = stat.T[0:8, :]

    pl.semaphore_wait(barrier, 17)
    for o in (2, 1, 3):
        pl.semaphore_signal(go, inc=1, device_id=at_y(lax.rem(y + o, 4)), device_id_type=MESH)

    def stat_copy(o):
        return rcopy(stat_s, rstat.at[z], ss_s.at[o], ss_r.at[z], at_z(lax.rem(z + o, 8)))

    def half(n):
        return 1 - yhi if n == 0 else yhi

    def acc_copy(n, o):
        zo = lax.rem(z + o, 8)
        return rcopy(acc_s.at[half(n), zo], racc.at[z, half(n)], sa_s.at[n, o], sa_r.at[n, z], at_z(zo))

    for o in Z_FAR:
        stat_copy(o).start()
        drains.append(lambda o=o: stat_copy(o).wait_send())
    rstat[z] = stat_s[...]
    local[2].wait()
    local[4].wait()
    for k in range(4):
        big = jnp.concatenate(
            [jnp.where(rowmod == r, probs[k], 0.0).reshape(128, 128).astype(BF16) for r in range(8)], axis=1)
        vk = cv_v[:, :, k * 128:(k + 1) * 128].reshape(1024, 128)
        acc = jnp.dot(big, vk, preferred_element_type=F32).reshape(16, 8, 128)
        acc = acc + fresh[k] * nv_v[:, k * 128:(k + 1) * 128].astype(F32)[None]
        acc_s[k // 2, (k % 2) * 4:(k % 2) * 4 + 4] = acc.reshape(4, 32, 128).astype(BF16)
    for n in range(2):
        for o in Z_FAR:
            acc_copy(n, o).start()
            drains.append(lambda n=n, o=o: acc_copy(n, o).wait_send())
    for j in range(2):
        racc[z, j] = acc_s[j, z]

    def wait_stat(o):
        c = lax.rem(z + o, 8)
        rcopy(stat_s, rstat.at[c], ss_s.at[o], ss_r.at[c], me).wait_recv()

    loop(1, 8, wait_stat)
    rs = rstat[...]
    high = jnp.max(rs, axis=0)
    scale = jnp.exp(rs - high[None])
    den = jnp.maximum(jnp.sum(scale * pltpu.roll(rs, 7, 1), axis=0), 1e-30)
    lse = high + jnp.log(den)
    lse_s[...] = lse
    flat = (scale / den[None]).reshape(64, 128)
    rt_v[...] = jnp.concatenate([flat, flat], axis=0).T
    kz = lax.div(z, 4)
    rows_z = pl.ds(pl.multiple_of(lax.rem(z, 4) * 32, 32), 32)
    st = rt_v[rows_z, :]
    st = jnp.where(kz == 0, st, pltpu.roll(st, 126, 1))
    def h_peer(dx, dc, dh):
        return lax.rem(yhi + dh, 2), lax.rem(x + dx, 4) * 2 + lax.rem(core + dc, 2)

    def o_copy(dx, dc, dh):
        h, b = h_peer(dx, dc, dh)
        return rcopy(oh_s.at[h], ogath.at[yhi, req], so_s.at[dh, dx * 2 + dc], so_r.at[yhi, req],
                     (role, b, h * 8 + z))

    for n in range(2):
        def wait_acc(o):
            c = lax.rem(z + o, 8)
            ref = racc.at[c, half(n)]
            rcopy(ref, ref, sa_s.at[n, o], sa_r.at[n, c], me).wait_recv()

        loop(1, 8, wait_acc)
        mine = jnp.where(half(n) == 0, st, pltpu.roll(st, 124, 1))
        part = jnp.zeros((32, 128), F32)
        for c in range(8):
            part = part + mine[:, 8 * c:8 * c + 1] * racc[c, half(n)].astype(F32)
        row = lse_s[pl.ds(4 * half(n) + 2 * kz, 1), :]
        head = row.astype(BF16).astype(F32)
        middle = (row - head).astype(BF16).astype(F32)
        oh_s[half(n)] = jnp.concatenate(
            [part, head, middle, row - head - middle, jnp.zeros((13, 128), F32)], axis=0).astype(BF16)
        if n == 0:
            pl.semaphore_wait(go, 3)
        for o in HALF_FAR:
            if o[2] == 1 - n:
                o_copy(*o).start()
    drain()

    def drain_o():
        for o in HALF_FAR:
            o_copy(*o).wait_send()

    drains.append(drain_o)
    ogath[yhi, req] = oh_s[yhi]

    def wait_o(o):
        i = lax.rem(yhi * 8 + req + o, 16)
        h, b = lax.div(i, 8), lax.rem(i, 8)
        rcopy(ogath.at[h, b], ogath.at[h, b], so_s.at[h, b], so_r.at[h, b], me).wait_recv()

    loop(1, 16, wait_o)
    logs = jnp.sum(ogath[:, :, 32:48, :].astype(F32), axis=2)
    gap = logs[1] - logs[0]
    both = jnp.concatenate(
        [1.0 / (1.0 + jnp.exp(gap)), 1.0 / (1.0 + jnp.exp(-gap)), jnp.zeros((112, 128), F32)], axis=0)
    rt_v[...] = both.T
    st = rt_v[rows_z, :]
    heads = []
    for b in range(8):
        heads.append(st[:, b:b + 1] * ogath[0, b, 0:32].astype(F32)
                     + st[:, 8 + b:9 + b] * ogath[1, b, 0:32].astype(F32))
    attn = jnp.concatenate(
        [jnp.concatenate([heads[b][8 * g:8 * g + 8, :] for b in range(8)], axis=0) for g in range(4)],
        axis=1).astype(BF16)
    local[5].wait()
    proj = jnp.dot(attn, wo_v[...], preferred_element_type=F32)
    for yy in range(4):
        for zz in range(8):
            psend[yy, zz] = proj[16 * yy:16 * yy + 16, 128 * zz:128 * zz + 128].astype(BF16)

    def p_copy(dy, dz):
        yo, zo = lax.rem(y + dy, 4), lax.rem(z + dz, 8)
        return rcopy(psend.at[yo, zo], rpart.at[yz], sp_s.at[dy * 8 + dz], sp_r.at[yz],
                     (lax.rem(yo, 2), req, lax.div(yo, 2) * 8 + zo))

    for o in YZ_FAR:
        p_copy(*o).start()
    drain()

    def drain_p():
        for o in YZ_FAR:
            p_copy(*o).wait_send()

    drains.append(drain_p)
    rpart[yz] = psend[y, z]

    def wait_p(o):
        c = lax.rem(yz + o, 32)
        rcopy(rpart.at[c], rpart.at[c], sp_s.at[o], sp_r.at[c], me).wait_recv()

    loop(1, 32, wait_p)
    local[6].wait()
    piece = res_v[...].astype(F32) + jnp.sum(rpart[...].astype(F32), axis=0)
    rows_y = pl.ds(pl.multiple_of(y * 16, 16), 16)
    xs[req, 0, rows_y, :] = piece.astype(BF16)

    def z_copy(o):
        at = RING.index((8 - o) % 8)
        return rcopy(xs.at[req, 0, rows_y], xs.at[req, at, rows_y], sz_s.at[o], sz_r.at[at],
                     at_z(lax.rem(z + o, 8)))

    def y_ref(g, b, yo):
        lo, hi = RUNS[g]
        return xs.at[b, pl.ds(lo, hi - lo), pl.ds(pl.multiple_of(yo * 16, 16), 16)]

    def xy_copy(g, dx, dy):
        return rcopy(y_ref(g, req, y), y_ref(g, req, y), sx_s.at[g, dx, dy], sx_r.at[g, x, y],
                     at_xy(lax.rem(x + dx, 4), lax.rem(y + dy, 4)))

    def xy_wait(g, dx, dy):
        xo, yo = lax.rem(x + dx, 4), lax.rem(y + dy, 4)
        ref = y_ref(g, xo * 2 + core, yo)
        rcopy(ref, ref, sx_s.at[g, dx, dy], sx_r.at[g, xo, yo], me).wait_recv()

    def b_ref(g, b):
        lo, hi = RUNS[g]
        return xs.at[b, pl.ds(lo, hi - lo)]

    def c_copy(g, o):
        xo = lax.rem(x + o, 4)
        ref = b_ref(g, xo * 2 + core)
        return rcopy(ref, ref, sc_s.at[g, o], sc_r.at[g, xo], at_req(x * 2 + 1 - core))

    def c_wait(g, o):
        xo = lax.rem(x + o, 4)
        ref = b_ref(g, xo * 2 + 1 - core)
        rcopy(ref, ref, sc_s.at[g, o], sc_r.at[g, xo], me).wait_recv()

    for o in Z_FAR:
        z_copy(o).start()
    for g, (lo, hi) in enumerate(RUNS):
        for at in range(max(lo, 1), hi):
            ref = xs.at[req, at, rows_y]
            rcopy(ref, ref, sz_s.at[at], sz_r.at[at], me).wait_recv()
        for o in XY_FAR:
            xy_copy(g, *o).start()
        if g == 0:
            drain()
    for o in Z_FAR:
        drains.append(lambda o=o: z_copy(o).wait_send())
    for g in range(len(RUNS)):
        for o in XY_COLUMN:
            drains.append(lambda g=g, o=o: xy_copy(g, *o).wait_send())
    def rows_of(lo, hi, b):
        return [b * 8 + lax.rem(z + RING[at], 8) for at in range(lo, hi)]

    def gained(xb, chunks):
        xg = [xb[i] * gain_v[pl.ds(c, 1), :] for i, c in enumerate(chunks)]
        return jnp.concatenate(xg, axis=1).astype(BF16)

    def block(g, b):
        lo, hi = RUNS[g]
        xb = xs[b, lo:hi].astype(F32)
        sq = jnp.sum(jnp.sum(xb * xb, axis=0), axis=-1, keepdims=True)
        return sq, gained(xb, rows_of(lo, hi, b))

    def weights(ref, chunks):
        return jnp.concatenate([ref[pl.ds(pl.multiple_of(c * 128, 128), 128), :] for c in chunks], axis=0)

    local[7].wait()
    local[8].wait()
    owner = lax.div(lane, 16)

    def tenants(first):
        t = jnp.zeros((8, 128), jnp.int32)
        for r in range(8):
            t = jnp.where(sub == r, ten_s[first + r], t)
        return t

    def spread(v):
        v = v + pltpu.roll(v, 64, 1)
        v = v + pltpu.roll(v, 32, 1)
        return v + pltpu.roll(v, 16, 1)

    mid = jnp.dot(gained(xs[req, :, rows_y, :].astype(F32), rows_of(0, 8, req)), weights(ad_v, rows_of(0, 8, 0)),
                  preferred_element_type=F32)
    for i in range(2):
        t = tenants(y * 16 + 8 * i)
        v = (jnp.where(owner == t, mid[8 * i:8 * i + 8, 0:128], 0.0)
             + jnp.where(owner + 8 == t, mid[8 * i:8 * i + 8, 128:256], 0.0))
        ad_s[i:i + 1, :] = jnp.sum(jnp.where(owner == sub, spread(v), 0.0), axis=0, keepdims=True)

    def rad_ref(b, yo):
        return rad.at[b, pl.ds(2 * yo, 2)]

    def d_copy(dx, dc, dy):
        yo, b = lax.rem(y + dy, 4), lax.rem(x + dx, 4) * 2 + lax.rem(core + dc, 2)
        return rcopy(ad_s, rad_ref(req, y), sd_s.at[dx * 2 + dc, dy], sd_r.at[req, y],
                     (lax.rem(yo, 2), b, lax.div(yo, 2) * 8 + z))

    for o in PLANE:
        d_copy(*o).start()
        drains.append(lambda o=o: d_copy(*o).wait_send())
    rad[req, pl.ds(2 * y, 2), :] = ad_s[...]

    def wait_d(o):
        i = lax.rem(req * 4 + y + o, 32)
        ref = rad_ref(lax.div(i, 4), lax.rem(i, 4))
        rcopy(ref, ref, sd_s.at[0, 0], sd_r.at[lax.div(i, 4), lax.rem(i, 4)], me).wait_recv()

    local[10].wait()
    local[11].wait()

    def gate_up(g, b, xg):
        return jnp.dot(xg, weights(wgu_v, rows_of(*RUNS[g], b)), preferred_element_type=F32)

    def forward(g, o):
        c_copy(g, o).start()
        drains.append(lambda: c_copy(g, o).wait_send())

    sq = jnp.zeros((64, 1), F32)
    gu = jnp.zeros((64, 256), F32)
    last = len(RUNS) - 1
    for g in range(len(RUNS)):
        for dy in (1, 3, 2):
            xy_wait(g, 0, dy)
        forward(g, 0)
        s1, xg = block(g, req)
        sq = sq + s1
        own_xg = xg
        if g == last:
            break
        gu = gu + gate_up(g, req, xg)
        for o in (1, 3, 2):
            for dy in (0, 1, 3, 2):
                xy_wait(g, o, dy)
            forward(g, o)
        for o in (1, 3, 2):
            b = lax.rem(x + o, 4) * 2 + core
            s1, xg = block(g, b)
            sq = sq + s1
            gu = gu + gate_up(g, b, xg)
        for o in (0, 1, 3, 2) if g else ():
            c_wait(g - 1, o)
            b = lax.rem(x + o, 4) * 2 + 1 - core
            s1, xg = block(g - 1, b)
            sq = sq + s1
            gu = gu + gate_up(g - 1, b, xg)
    gu = gu + gate_up(last, req, own_xg)
    for o in (1, 3, 2):
        for dy in (0, 1, 3, 2):
            xy_wait(last, o, dy)
        forward(last, o)
    for o in (1, 3, 2):
        b = lax.rem(x + o, 4) * 2 + core
        s1, xg = block(last, b)
        sq = sq + s1
        gu = gu + gate_up(last, b, xg)
    for g in range(max(last - 1, 0), last + 1):
        for o in (0, 1, 3, 2):
            c_wait(g, o)
            b = lax.rem(x + o, 4) * 2 + 1 - core
            s1, xg = block(g, b)
            sq = sq + s1
            gu = gu + gate_up(g, b, xg)

    loop(1, 32, wait_d)
    inv = lax.rsqrt(sq * (1.0 / 8192.0) + EPS)
    allmid = jnp.sum(rad[...], axis=0)
    chosen = []
    for i in range(8):
        t = tenants(8 * i)
        v = spread(jnp.where(owner == sub, jnp.broadcast_to(allmid[i:i + 1, :], (8, 128)), 0.0))
        v = v * inv[8 * i:8 * i + 8]
        chosen.append(jnp.concatenate(
            [jnp.where(owner == t, v, 0.0), jnp.where(owner + 8 == t, v, 0.0)], axis=1))
    local[9].wait()
    lowrank = jnp.dot(jnp.concatenate(chosen, axis=0).astype(BF16), tu_v[...], preferred_element_type=F32)
    gate = gu[:, 0:128] * inv
    up = gu[:, 128:256] * inv + 2.0 * lowrank
    hid = (gate / (1.0 + jnp.exp(-gate)) * up).astype(BF16)

    local[12].wait()

    def part_of(g):
        lo, hi = PARTS[g]
        return pl.ds(lo, hi - lo)

    def core_copy(g):
        return rcopy(dbuf.at[1 - core, :, :, part_of(g)], rcore.at[:, :, part_of(g)], ec_s.at[g], ec_r.at[g],
                     at_req(x * 2 + 1 - core))

    def ex_copy(g, dx, dy):
        xo, yo = lax.rem(x + dx, 4), lax.rem(y + dy, 4)
        return rcopy(r1.at[xo, yo, part_of(g)], rx.at[x, y, part_of(g)], ex_s.at[g, dx, dy], ex_r.at[g, x, y],
                     at_xy(xo, yo))

    def ez_copy(i):
        zo = lax.rem(z + Z_ALL[i], 8)
        return rcopy(r3.at[i], rz.at[z], ez_s.at[i], ez_r.at[z], at_z(zo))

    for g, (lo, hi) in enumerate(PARTS):
        for i in range(lo, hi):
            zo = lax.rem(z + Z_ALL[i], 8)
            for yy in range(4):
                col = pl.multiple_of(((yy % 2) * 16 + (yy // 2) * 8 + zo) * 256, 256)
                part = jnp.dot(hid, wd_v[:, pl.ds(col, 256)], preferred_element_type=F32)
                for b in range(8):
                    dbuf[b % 2, b // 2, yy, i] = jnp.concatenate(
                        [part[8 * b:8 * b + 8, 0:128], part[8 * b:8 * b + 8, 128:256]], axis=0).astype(BF16)
        core_copy(g).start()
        drains.append(lambda g=g: core_copy(g).wait_send())

    for g, (lo, hi) in enumerate(PARTS):
        core_copy(g).wait_recv()

        def fold_core(i):
            r1[i, :, lo:hi] = (dbuf[core, i, :, lo:hi].astype(F32) + rcore[i, :, lo:hi].astype(F32)).astype(BF16)

        loop(0, 4, fold_core)
        for o in XY_FAR:
            ex_copy(g, *o).start()
            drains.append(lambda g=g, o=o: ex_copy(g, *o).wait_send())
        rx[x, y, lo:hi] = r1[x, y, lo:hi]
        if g == 0:
            late, drains[:] = drains[-16:], drains[:-16]
            drain()
            drains.extend(late)

    own = []
    for h in range(2):
        c = yz * 2 + h
        away = lax.rem(lax.rem(c, 8) + 8 - z, 8)
        past = lax.div(away, 5)
        at = (1 - past) * (2 * away - 1) + past * (16 - 2 * away) + lax.div(8 - away, 8)
        t = xs[lax.div(c, 8), at, pl.ds(pl.multiple_of(x * 16, 16), 16), :].astype(F32)
        own.append(jnp.where(core == 0, t[0:8, :], t[8:16, :]))
    own = jnp.concatenate(own, axis=0)

    for g, (lo, hi) in enumerate(PARTS):
        def wait_ex(o):
            i = lax.rem(x * 4 + y + o, 16)
            xo, yo = lax.div(i, 4), lax.rem(i, 4)
            ref = rx.at[xo, yo, part_of(g)]
            rcopy(ref, ref, ex_s.at[g, xo, yo], ex_r.at[g, xo, yo], me).wait_recv()

        loop(1, 16, wait_ex)
        for i in range(lo, hi):
            part = rx[0, 0, i].astype(F32)
            for j in range(1, 16):
                part = part + rx[j // 4, j % 4, i].astype(F32)
            if Z_ALL[i]:
                r3[i] = part.astype(BF16)
                ez_copy(i).start()
                drains.append(lambda k=i: ez_copy(k).wait_send())
            else:
                own = own + part
                rz[z] = jnp.zeros((16, 128), BF16)

    late, drains[:] = drains[-7:], drains[:-7]
    drain()
    drains.extend(late)

    def wait_ez(o):
        zo = lax.rem(z + o, 8)
        rcopy(rz.at[zo], rz.at[zo], ez_s.at[o], ez_r.at[zo], me).wait_recv()

    loop(1, 8, wait_ez)
    res = own + jnp.sum(rz[...].astype(F32), axis=0)
    out_ref[:, 0:128] = res[0:8, :]
    out_ref[:, 128:256] = res[8:16, :]
    drain()


def shards(query, cache_keys, cache_values, new_keys, new_values, lengths, residual_in, out_proj,
           norm_gain, adapter_down, tenant_adapter_up_matrix, tenant, w_gate, w_up, w_down):
    hbm = pl.BlockSpec(memory_space=pl.ANY)
    smem = pl.BlockSpec(memory_space=pltpu.SMEM)
    v = pltpu.VMEM
    dma = pltpu.SemaphoreType.DMA
    return pl.pallas_call(
        functools.partial(kernel, None),
        out_shape=jax.ShapeDtypeStruct((8, 256), F32),
        in_specs=[hbm, hbm, hbm, hbm, hbm, smem, hbm, hbm, hbm, hbm, hbm, smem, hbm, hbm, hbm],
        out_specs=pl.BlockSpec(memory_space=pltpu.VMEM),
        scratch_shapes=[
            v((8, 8192), BF16), v((8, 128, 512), BF16), v((8, 128, 512), BF16), v((8, 512), BF16),
            v((8, 512), BF16), v((16, 128), BF16), v((512, 1024), BF16), v((64, 128), F32),
            v((1024, 256), BF16), v((256, 128), BF16), v((8192, 256), BF16), v((128, 8192), BF16),
            v((2, 8, 32, 128), BF16), v((8, 128), F32), v((8, 2, 32, 128), BF16), v((8, 8, 128), F32),
            v((128, 128), F32), v((8, 128), F32), v((2, 48, 128), BF16),
            v((2, 8, 48, 128), BF16), v((4, 8, 16, 128), BF16), v((32, 16, 128), BF16), v((8, 8, 64, 128), BF16),
            v((2, 128), F32), v((8, 8, 128), F32),
            v((2, 4, 4, 8, 16, 128), BF16), v((4, 4, 8, 16, 128), BF16), v((4, 4, 8, 16, 128), BF16),
            v((4, 4, 8, 16, 128), BF16), v((8, 16, 128), BF16), v((8, 16, 128), BF16),
            dma((13,)),
            pltpu.SemaphoreType.REGULAR, dma((2, 8)), dma((2, 8)), dma((8,)), dma((8,)),
            dma((2, 8)), dma((2, 8)), dma((32,)), dma((32,)),
            dma((8,)), dma((8,)), dma((len(RUNS), 4, 4)), dma((len(RUNS), 4, 4)),
            dma((len(RUNS), 4)), dma((len(RUNS), 4)),
            dma((8, 4)), dma((8, 4)), dma((len(PARTS),)), dma((len(PARTS),)),
            dma((len(PARTS), 4, 4)), dma((len(PARTS), 4, 4)), dma((8,)), dma((8,)),
        ],
        compiler_params=pltpu.CompilerParams(
            collective_id=0, has_side_effects=True, vmem_limit_bytes=60 * 1024 * 1024),
    )(query, cache_keys, cache_values, new_keys, new_values, lengths, residual_in, out_proj,
      norm_gain.reshape(64, 128), adapter_down, tenant_adapter_up_matrix, tenant, w_gate, w_up, w_down).astype(BF16)


def solution(mesh):
    placed = (
        P("req", "role"),
        P("req", "ctx", "role"),
        P("req", "ctx", "role"),
        P("req", "role"),
        P("req", "role"),
        P("req"),
        P(None, "req"),
        P(("role", "ctx"), "req"),
        P(),
        P("req", None),
        P(None, ("role", "req", "ctx")),
        P(),
        P(None, ("role", "req", "ctx")),
        P(None, ("role", "req", "ctx")),
        P(("role", "req", "ctx"), None),
    )
    return jax.shard_map(
        shards, mesh=mesh, in_specs=placed, out_specs=P("req", ("role", "ctx")), check_vma=False
    )
```

```python
import functools
import math

import jax
import jax.numpy as jnp
from jax import lax
from jax.experimental import pallas as pl
from jax.experimental.pallas import tpu as pltpu
from jax.sharding import PartitionSpec as P

MESH = pl.DeviceIdType.MESH
F32 = jnp.float32
BF16 = jnp.bfloat16
HD = 128
EPS = 1e-05
LOW = -1e30
NT = (((1,), (1,)), ((), ()))
Z_FAR = (4, 3, 5, 2, 6, 1, 7)
XY_FAR = ((2, 2), (1, 2), (3, 2), (2, 1), (2, 3), (1, 1), (1, 3), (3, 1), (3, 3),
          (2, 0), (0, 2), (1, 0), (3, 0), (0, 1), (0, 3))
XY_COLUMN = ((0, 2), (0, 1), (0, 3)) + XY_FAR[:9] + ((2, 0), (1, 0), (3, 0))
PARTS = ((0, 3), (3, 6), (6, 8))
Z_ALL = Z_FAR + (0,)
RING = (0, 1, 7, 2, 6, 3, 5, 4)
RUNS = ((0, 4), (4, 8))
PLANE = tuple((dx, dc, dy) for dx in (2, 1, 3, 0) for dy in (2, 1, 3, 0) for dc in (1, 0) if dx or dc or dy)
YZ_FAR = tuple((dy, dz) for dz in Z_FAR + (0,) for dy in (2, 1, 3, 0) if dy or dz)
HALF_FAR = tuple((dx, dc, dh) for dh in (1, 0) for dx in (2, 1, 3, 0) for dc in (1, 0) if dx or dc or dh)
REQ_FAR = ((2, 1), (2, 0), (1, 1), (3, 1), (1, 0), (3, 0), (0, 1))


def rcopy(src, dst, ssem, rsem, dev):
    return pltpu.make_async_remote_copy(
        src_ref=src, dst_ref=dst, send_sem=ssem, recv_sem=rsem, device_id=dev, device_id_type=MESH
    )


def loop(lo, hi, body):
    def step(i, carry):
        body(i)
        return carry

    lax.fori_loop(lo, hi, step, 0)


def kernel(
    stop,
    q_h, ck_h, cv_h, nk_h, nv_h, len_s, res_h, wo_h, gain_h, ad_h, tu_h, ten_s, wg_h, wu_h, wd_h,
    out_ref,
    q_v, ck_v, cv_v, nk_v, nv_v, res_v, wo_v, gain_v, ad_v, tu_v, wgu_v, wd_v,
    acc_s, stat_s, racc, rstat, rt_v, lse_s, oh_s,
    ogath, psend, rpart, xs, ad_s, rad, dbuf, rcore, r1, rx, r3, rz,
    lsem,
    go, sa_s, sa_r, ss_s, ss_r, so_s, so_r, sp_s, sp_r, sz_s, sz_r, sx_s, sx_r, sc_s, sc_r,
    sd_s, sd_r, ec_s, ec_r, ex_s, ex_r, ez_s, ez_r,
):
    role = lax.axis_index("role")
    req = lax.axis_index("req")
    ctx = lax.axis_index("ctx")
    x = lax.div(req, 2)
    core = lax.rem(req, 2)
    yhi = lax.div(ctx, 8)
    z = lax.rem(ctx, 8)
    y = yhi * 2 + role
    yz = role * 16 + ctx
    me = (role, req, ctx)

    def at_req(i):
        return (role, i, ctx)

    def at_xy(xo, yo):
        return (lax.rem(yo, 2), xo * 2 + core, lax.div(yo, 2) * 8 + z)

    def at_y(i):
        return (lax.rem(i, 2), req, lax.div(i, 2) * 8 + z)

    def at_z(i):
        return (role, req, yhi * 8 + i)

    barrier = pltpu.get_barrier_semaphore()

    def greet(dev):
        pl.semaphore_signal(barrier, inc=1, device_id=dev, device_id_type=MESH)

    for o in Z_FAR:
        greet(at_z(lax.rem(z + o, 8)))
    for dx, dc in REQ_FAR:
        greet(at_req(lax.rem(x + dx, 4) * 2 + lax.rem(core + dc, 2)))
    for o in (2, 1, 3):
        greet(at_y(lax.rem(y + o, 4)))

    drains = []

    def drain():
        while drains:
            drains.pop(0)()

    local = [
        pltpu.make_async_copy(q_h, q_v, lsem.at[0]),
        pltpu.make_async_copy(ck_h, ck_v, lsem.at[1]),
        pltpu.make_async_copy(cv_h, cv_v, lsem.at[2]),
        pltpu.make_async_copy(nk_h, nk_v, lsem.at[3]),
        pltpu.make_async_copy(nv_h, nv_v, lsem.at[4]),
        pltpu.make_async_copy(wo_h, wo_v, lsem.at[5]),
        pltpu.make_async_copy(
            res_h.at[pl.ds(pl.multiple_of(y * 16, 16), 16), pl.ds(pl.multiple_of(z * 128, 128), 128)],
            res_v, lsem.at[6],
        ),
        pltpu.make_async_copy(gain_h, gain_v, lsem.at[7]),
        pltpu.make_async_copy(ad_h, ad_v, lsem.at[8]),
        pltpu.make_async_copy(tu_h, tu_v, lsem.at[9]),
        pltpu.make_async_copy(wg_h, wgu_v.at[:, pl.ds(0, 128)], lsem.at[10]),
        pltpu.make_async_copy(wu_h, wgu_v.at[:, pl.ds(128, 128)], lsem.at[11]),
        pltpu.make_async_copy(wd_h, wd_v, lsem.at[12]),
    ]
    for i in (0, 1, 3, 2, 4):
        local[i].start()

    factor = 1.0 / math.sqrt(HD)
    sub = lax.broadcasted_iota(jnp.int32, (8, 128), 0)
    lane = lax.broadcasted_iota(jnp.int32, (8, 128), 1)
    lens = jnp.zeros((8, 128), jnp.int32)
    for r in range(8):
        lens = jnp.where(sub == r, len_s[r], lens)
    usable = (ctx * 128 + lane < lens)[None]
    rowmod = lax.broadcasted_iota(jnp.int32, (16, 8, 128), 1)
    stat_lane = lax.broadcasted_iota(jnp.int32, (128, 128), 1)
    local[0].wait()
    local[1].wait()
    local[3].wait()
    probs = []
    fresh = []
    stat = jnp.zeros((128, 128), F32)
    for k in range(4):
        qk = jnp.concatenate(
            [q_v[:, (k * 16 + g) * 128:(k * 16 + g + 1) * 128].astype(F32) for g in range(16)], axis=0)
        nk = nk_v[:, k * 128:(k + 1) * 128].astype(F32)
        own = jnp.sum(qk.reshape(16, 8, 128) * nk[None], axis=-1, keepdims=True) * factor
        own = jnp.where(ctx == 0, own, LOW)
        kk = ck_v[:, :, k * 128:(k + 1) * 128].reshape(1024, 128)
        full = lax.dot_general(qk.astype(BF16), kk, NT, preferred_element_type=F32)
        sc = jnp.zeros((16, 8, 128), F32)
        for r in range(8):
            sc = jnp.where(rowmod == r, full[:, r * 128:(r + 1) * 128].reshape(16, 8, 128), sc)
        sc = jnp.where(usable, sc * factor, LOW)
        top = jnp.maximum(jnp.max(sc, axis=-1, keepdims=True), own)
        w = jnp.where(usable, jnp.exp(sc - top), 0.0)
        wb = w.astype(BF16).astype(F32)
        w_own = jnp.where(ctx == 0, jnp.exp(own - top), 0.0)
        tot = jnp.sum(wb, axis=-1, keepdims=True) + w_own
        probs.append(wb)
        fresh.append(w_own)
        stat = jnp.where(stat_lane == 2 * k, top.reshape(128, 1), stat)
        stat = jnp.where(stat_lane == 2 * k + 1, tot.reshape(128, 1), stat)
    stat_s[...] = stat.T[0:8, :]

    pl.semaphore_wait(barrier, 17)
    for o in (2, 1, 3):
        pl.semaphore_signal(go, inc=1, device_id=at_y(lax.rem(y + o, 4)), device_id_type=MESH)

    def stat_copy(o):
        return rcopy(stat_s, rstat.at[z], ss_s.at[o], ss_r.at[z], at_z(lax.rem(z + o, 8)))

    def half(n):
        return 1 - yhi if n == 0 else yhi

    def acc_copy(n, o):
        zo = lax.rem(z + o, 8)
        return rcopy(acc_s.at[half(n), zo], racc.at[z, half(n)], sa_s.at[n, o], sa_r.at[n, z], at_z(zo))

    for o in Z_FAR:
        stat_copy(o).start()
        drains.append(lambda o=o: stat_copy(o).wait_send())
    rstat[z] = stat_s[...]
    local[2].wait()
    local[4].wait()
    for k in range(4):
        big = jnp.concatenate(
            [jnp.where(rowmod == r, probs[k], 0.0).reshape(128, 128).astype(BF16) for r in range(8)], axis=1)
        vk = cv_v[:, :, k * 128:(k + 1) * 128].reshape(1024, 128)
        acc = jnp.dot(big, vk, preferred_element_type=F32).reshape(16, 8, 128)
        acc = acc + fresh[k] * nv_v[:, k * 128:(k + 1) * 128].astype(F32)[None]
        acc_s[k // 2, (k % 2) * 4:(k % 2) * 4 + 4] = acc.reshape(4, 32, 128).astype(BF16)
    for n in range(2):
        for o in Z_FAR:
            acc_copy(n, o).start()
            drains.append(lambda n=n, o=o: acc_copy(n, o).wait_send())
    for j in range(2):
        racc[z, j] = acc_s[j, z]
    for i in range(5, 13):
        local[i].start()

    def wait_stat(o):
        c = lax.rem(z + o, 8)
        rcopy(stat_s, rstat.at[c], ss_s.at[o], ss_r.at[c], me).wait_recv()

    loop(1, 8, wait_stat)
    rs = rstat[...]
    high = jnp.max(rs, axis=0)
    scale = jnp.exp(rs - high[None])
    den = jnp.maximum(jnp.sum(scale * pltpu.roll(rs, 7, 1), axis=0), 1e-30)
    lse = high + jnp.log(den)
    lse_s[...] = lse
    flat = (scale / den[None]).reshape(64, 128)
    rt_v[...] = jnp.concatenate([flat, flat], axis=0).T
    kz = lax.div(z, 4)
    rows_z = pl.ds(pl.multiple_of(lax.rem(z, 4) * 32, 32), 32)
    st = rt_v[rows_z, :]
    st = jnp.where(kz == 0, st, pltpu.roll(st, 126, 1))
    def h_peer(dx, dc, dh):
        return lax.rem(yhi + dh, 2), lax.rem(x + dx, 4) * 2 + lax.rem(core + dc, 2)

    def o_copy(dx, dc, dh):
        h, b = h_peer(dx, dc, dh)
        return rcopy(oh_s.at[h], ogath.at[yhi, req], so_s.at[dh, dx * 2 + dc], so_r.at[yhi, req],
                     (role, b, h * 8 + z))

    for n in range(2):
        def wait_acc(o):
            c = lax.rem(z + o, 8)
            ref = racc.at[c, half(n)]
            rcopy(ref, ref, sa_s.at[n, o], sa_r.at[n, c], me).wait_recv()

        loop(1, 8, wait_acc)
        mine = jnp.where(half(n) == 0, st, pltpu.roll(st, 124, 1))
        part = jnp.zeros((32, 128), F32)
        for c in range(8):
            part = part + mine[:, 8 * c:8 * c + 1] * racc[c, half(n)].astype(F32)
        row = lse_s[pl.ds(4 * half(n) + 2 * kz, 1), :]
        head = row.astype(BF16).astype(F32)
        middle = (row - head).astype(BF16).astype(F32)
        oh_s[half(n)] = jnp.concatenate(
            [part, head, middle, row - head - middle, jnp.zeros((13, 128), F32)], axis=0).astype(BF16)
        if n == 0:
            pl.semaphore_wait(go, 3)
        for o in HALF_FAR:
            if o[2] == 1 - n:
                o_copy(*o).start()
    drain()

    def drain_o():
        for o in HALF_FAR:
            o_copy(*o).wait_send()

    drains.append(drain_o)
    ogath[yhi, req] = oh_s[yhi]

    def wait_o(o):
        i = lax.rem(yhi * 8 + req + o, 16)
        h, b = lax.div(i, 8), lax.rem(i, 8)
        rcopy(ogath.at[h, b], ogath.at[h, b], so_s.at[h, b], so_r.at[h, b], me).wait_recv()

    loop(1, 16, wait_o)
    logs = jnp.sum(ogath[:, :, 32:48, :].astype(F32), axis=2)
    gap = logs[1] - logs[0]
    both = jnp.concatenate(
        [1.0 / (1.0 + jnp.exp(gap)), 1.0 / (1.0 + jnp.exp(-gap)), jnp.zeros((112, 128), F32)], axis=0)
    rt_v[...] = both.T
    st = rt_v[rows_z, :]
    heads = []
    for b in range(8):
        heads.append(st[:, b:b + 1] * ogath[0, b, 0:32].astype(F32)
                     + st[:, 8 + b:9 + b] * ogath[1, b, 0:32].astype(F32))
    attn = jnp.concatenate(
        [jnp.concatenate([heads[b][8 * g:8 * g + 8, :] for b in range(8)], axis=0) for g in range(4)],
        axis=1).astype(BF16)
    local[5].wait()
    proj = jnp.dot(attn, wo_v[...], preferred_element_type=F32)
    for yy in range(4):
        for zz in range(8):
            psend[yy, zz] = proj[16 * yy:16 * yy + 16, 128 * zz:128 * zz + 128].astype(BF16)

    def p_copy(dy, dz):
        yo, zo = lax.rem(y + dy, 4), lax.rem(z + dz, 8)
        return rcopy(psend.at[yo, zo], rpart.at[yz], sp_s.at[dy * 8 + dz], sp_r.at[yz],
                     (lax.rem(yo, 2), req, lax.div(yo, 2) * 8 + zo))

    for o in YZ_FAR:
        p_copy(*o).start()
    drain()

    def drain_p():
        for o in YZ_FAR:
            p_copy(*o).wait_send()

    drains.append(drain_p)
    rpart[yz] = psend[y, z]

    def wait_p(o):
        c = lax.rem(yz + o, 32)
        rcopy(rpart.at[c], rpart.at[c], sp_s.at[o], sp_r.at[c], me).wait_recv()

    loop(1, 32, wait_p)
    local[6].wait()
    piece = res_v[...].astype(F32) + jnp.sum(rpart[...].astype(F32), axis=0)
    rows_y = pl.ds(pl.multiple_of(y * 16, 16), 16)
    xs[req, 0, rows_y, :] = piece.astype(BF16)

    def z_copy(o):
        at = RING.index((8 - o) % 8)
        return rcopy(xs.at[req, 0, rows_y], xs.at[req, at, rows_y], sz_s.at[o], sz_r.at[at],
                     at_z(lax.rem(z + o, 8)))

    def y_ref(g, b, yo):
        lo, hi = RUNS[g]
        return xs.at[b, pl.ds(lo, hi - lo), pl.ds(pl.multiple_of(yo * 16, 16), 16)]

    def xy_copy(g, dx, dy):
        return rcopy(y_ref(g, req, y), y_ref(g, req, y), sx_s.at[g, dx, dy], sx_r.at[g, x, y],
                     at_xy(lax.rem(x + dx, 4), lax.rem(y + dy, 4)))

    def xy_wait(g, dx, dy):
        xo, yo = lax.rem(x + dx, 4), lax.rem(y + dy, 4)
        ref = y_ref(g, xo * 2 + core, yo)
        rcopy(ref, ref, sx_s.at[g, dx, dy], sx_r.at[g, xo, yo], me).wait_recv()

    def b_ref(g, b):
        lo, hi = RUNS[g]
        return xs.at[b, pl.ds(lo, hi - lo)]

    def c_copy(g, o):
        xo = lax.rem(x + o, 4)
        ref = b_ref(g, xo * 2 + core)
        return rcopy(ref, ref, sc_s.at[g, o], sc_r.at[g, xo], at_req(x * 2 + 1 - core))

    def c_wait(g, o):
        xo = lax.rem(x + o, 4)
        ref = b_ref(g, xo * 2 + 1 - core)
        rcopy(ref, ref, sc_s.at[g, o], sc_r.at[g, xo], me).wait_recv()

    for o in Z_FAR:
        z_copy(o).start()
    for g, (lo, hi) in enumerate(RUNS):
        for at in range(max(lo, 1), hi):
            ref = xs.at[req, at, rows_y]
            rcopy(ref, ref, sz_s.at[at], sz_r.at[at], me).wait_recv()
        for o in XY_FAR:
            xy_copy(g, *o).start()
        if g == 0:
            drain()
    for o in Z_FAR:
        drains.append(lambda o=o: z_copy(o).wait_send())
    for g in range(len(RUNS)):
        for o in XY_COLUMN:
            drains.append(lambda g=g, o=o: xy_copy(g, *o).wait_send())
    def rows_of(lo, hi, b):
        return [b * 8 + lax.rem(z + RING[at], 8) for at in range(lo, hi)]

    def gained(xb, chunks):
        xg = [xb[i] * gain_v[pl.ds(c, 1), :] for i, c in enumerate(chunks)]
        return jnp.concatenate(xg, axis=1).astype(BF16)

    def block(g, b):
        lo, hi = RUNS[g]
        xb = xs[b, lo:hi].astype(F32)
        sq = jnp.sum(jnp.sum(xb * xb, axis=0), axis=-1, keepdims=True)
        return sq, gained(xb, rows_of(lo, hi, b))

    def weights(ref, chunks):
        return jnp.concatenate([ref[pl.ds(pl.multiple_of(c * 128, 128), 128), :] for c in chunks], axis=0)

    local[7].wait()
    local[8].wait()
    owner = lax.div(lane, 16)

    def tenants(first):
        t = jnp.zeros((8, 128), jnp.int32)
        for r in range(8):
            t = jnp.where(sub == r, ten_s[first + r], t)
        return t

    def spread(v):
        v = v + pltpu.roll(v, 64, 1)
        v = v + pltpu.roll(v, 32, 1)
        return v + pltpu.roll(v, 16, 1)

    mid = jnp.dot(gained(xs[req, :, rows_y, :].astype(F32), rows_of(0, 8, req)), weights(ad_v, rows_of(0, 8, 0)),
                  preferred_element_type=F32)
    for i in range(2):
        t = tenants(y * 16 + 8 * i)
        v = (jnp.where(owner == t, mid[8 * i:8 * i + 8, 0:128], 0.0)
             + jnp.where(owner + 8 == t, mid[8 * i:8 * i + 8, 128:256], 0.0))
        ad_s[i:i + 1, :] = jnp.sum(jnp.where(owner == sub, spread(v), 0.0), axis=0, keepdims=True)

    def rad_ref(b, yo):
        return rad.at[b, pl.ds(2 * yo, 2)]

    def d_copy(dx, dc, dy):
        yo, b = lax.rem(y + dy, 4), lax.rem(x + dx, 4) * 2 + lax.rem(core + dc, 2)
        return rcopy(ad_s, rad_ref(req, y), sd_s.at[dx * 2 + dc, dy], sd_r.at[req, y],
                     (lax.rem(yo, 2), b, lax.div(yo, 2) * 8 + z))

    for o in PLANE:
        d_copy(*o).start()
        drains.append(lambda o=o: d_copy(*o).wait_send())
    rad[req, pl.ds(2 * y, 2), :] = ad_s[...]

    def wait_d(o):
        i = lax.rem(req * 4 + y + o, 32)
        ref = rad_ref(lax.div(i, 4), lax.rem(i, 4))
        rcopy(ref, ref, sd_s.at[0, 0], sd_r.at[lax.div(i, 4), lax.rem(i, 4)], me).wait_recv()

    local[10].wait()
    local[11].wait()

    def gate_up(g, b, xg):
        return jnp.dot(xg, weights(wgu_v, rows_of(*RUNS[g], b)), preferred_element_type=F32)

    def forward(g, o):
        c_copy(g, o).start()
        drains.append(lambda: c_copy(g, o).wait_send())

    sq = jnp.zeros((64, 1), F32)
    gu = jnp.zeros((64, 256), F32)
    last = len(RUNS) - 1
    for g in range(len(RUNS)):
        for dy in (1, 3, 2):
            xy_wait(g, 0, dy)
        forward(g, 0)
        s1, xg = block(g, req)
        sq = sq + s1
        own_xg = xg
        if g == last:
            break
        gu = gu + gate_up(g, req, xg)
        for o in (1, 3, 2):
            for dy in (0, 1, 3, 2):
                xy_wait(g, o, dy)
            forward(g, o)
        for o in (1, 3, 2):
            b = lax.rem(x + o, 4) * 2 + core
            s1, xg = block(g, b)
            sq = sq + s1
            gu = gu + gate_up(g, b, xg)
        for o in (0, 1, 3, 2) if g else ():
            c_wait(g - 1, o)
            b = lax.rem(x + o, 4) * 2 + 1 - core
            s1, xg = block(g - 1, b)
            sq = sq + s1
            gu = gu + gate_up(g - 1, b, xg)
    gu = gu + gate_up(last, req, own_xg)
    for o in (1, 3, 2):
        for dy in (0, 1, 3, 2):
            xy_wait(last, o, dy)
        forward(last, o)
    for o in (1, 3, 2):
        b = lax.rem(x + o, 4) * 2 + core
        s1, xg = block(last, b)
        sq = sq + s1
        gu = gu + gate_up(last, b, xg)
    for g in range(max(last - 1, 0), last + 1):
        for o in (0, 1, 3, 2):
            c_wait(g, o)
            b = lax.rem(x + o, 4) * 2 + 1 - core
            s1, xg = block(g, b)
            sq = sq + s1
            gu = gu + gate_up(g, b, xg)

    loop(1, 32, wait_d)
    inv = lax.rsqrt(sq * (1.0 / 8192.0) + EPS)
    allmid = jnp.sum(rad[...], axis=0)
    chosen = []
    for i in range(8):
        t = tenants(8 * i)
        v = spread(jnp.where(owner == sub, jnp.broadcast_to(allmid[i:i + 1, :], (8, 128)), 0.0))
        v = v * inv[8 * i:8 * i + 8]
        chosen.append(jnp.concatenate(
            [jnp.where(owner == t, v, 0.0), jnp.where(owner + 8 == t, v, 0.0)], axis=1))
    local[9].wait()
    lowrank = jnp.dot(jnp.concatenate(chosen, axis=0).astype(BF16), tu_v[...], preferred_element_type=F32)
    gate = gu[:, 0:128] * inv
    up = gu[:, 128:256] * inv + 2.0 * lowrank
    hid = (gate / (1.0 + jnp.exp(-gate)) * up).astype(BF16)

    local[12].wait()

    def part_of(g):
        lo, hi = PARTS[g]
        return pl.ds(lo, hi - lo)

    def core_copy(g):
        return rcopy(dbuf.at[1 - core, :, :, part_of(g)], rcore.at[:, :, part_of(g)], ec_s.at[g], ec_r.at[g],
                     at_req(x * 2 + 1 - core))

    def ex_copy(g, dx, dy):
        xo, yo = lax.rem(x + dx, 4), lax.rem(y + dy, 4)
        return rcopy(r1.at[xo, yo, part_of(g)], rx.at[x, y, part_of(g)], ex_s.at[g, dx, dy], ex_r.at[g, x, y],
                     at_xy(xo, yo))

    def ez_copy(i):
        zo = lax.rem(z + Z_ALL[i], 8)
        return rcopy(r3.at[i], rz.at[z], ez_s.at[i], ez_r.at[z], at_z(zo))

    for g, (lo, hi) in enumerate(PARTS):
        for i in range(lo, hi):
            zo = lax.rem(z + Z_ALL[i], 8)
            for yy in range(4):
                col = pl.multiple_of(((yy % 2) * 16 + (yy // 2) * 8 + zo) * 256, 256)
                part = jnp.dot(hid, wd_v[:, pl.ds(col, 256)], preferred_element_type=F32)
                for b in range(8):
                    dbuf[b % 2, b // 2, yy, i] = jnp.concatenate(
                        [part[8 * b:8 * b + 8, 0:128], part[8 * b:8 * b + 8, 128:256]], axis=0).astype(BF16)
        core_copy(g).start()
        drains.append(lambda g=g: core_copy(g).wait_send())

    for g, (lo, hi) in enumerate(PARTS):
        core_copy(g).wait_recv()

        def fold_core(i):
            r1[i, :, lo:hi] = (dbuf[core, i, :, lo:hi].astype(F32) + rcore[i, :, lo:hi].astype(F32)).astype(BF16)

        loop(0, 4, fold_core)
        for o in XY_FAR:
            ex_copy(g, *o).start()
            drains.append(lambda g=g, o=o: ex_copy(g, *o).wait_send())
        rx[x, y, lo:hi] = r1[x, y, lo:hi]
        if g == 0:
            late, drains[:] = drains[-16:], drains[:-16]
            drain()
            drains.extend(late)

    own = []
    for h in range(2):
        c = yz * 2 + h
        away = lax.rem(lax.rem(c, 8) + 8 - z, 8)
        past = lax.div(away, 5)
        at = (1 - past) * (2 * away - 1) + past * (16 - 2 * away) + lax.div(8 - away, 8)
        t = xs[lax.div(c, 8), at, pl.ds(pl.multiple_of(x * 16, 16), 16), :].astype(F32)
        own.append(jnp.where(core == 0, t[0:8, :], t[8:16, :]))
    own = jnp.concatenate(own, axis=0)

    for g, (lo, hi) in enumerate(PARTS):
        def wait_ex(o):
            i = lax.rem(x * 4 + y + o, 16)
            xo, yo = lax.div(i, 4), lax.rem(i, 4)
            ref = rx.at[xo, yo, part_of(g)]
            rcopy(ref, ref, ex_s.at[g, xo, yo], ex_r.at[g, xo, yo], me).wait_recv()

        loop(1, 16, wait_ex)
        for i in range(lo, hi):
            part = rx[0, 0, i].astype(F32)
            for j in range(1, 16):
                part = part + rx[j // 4, j % 4, i].astype(F32)
            if Z_ALL[i]:
                r3[i] = part.astype(BF16)
                ez_copy(i).start()
                drains.append(lambda k=i: ez_copy(k).wait_send())
            else:
                own = own + part
                rz[z] = jnp.zeros((16, 128), BF16)

    late, drains[:] = drains[-7:], drains[:-7]
    drain()
    drains.extend(late)

    def wait_ez(o):
        zo = lax.rem(z + o, 8)
        rcopy(rz.at[zo], rz.at[zo], ez_s.at[o], ez_r.at[zo], me).wait_recv()

    loop(1, 8, wait_ez)
    res = own + jnp.sum(rz[...].astype(F32), axis=0)
    out_ref[:, 0:128] = res[0:8, :]
    out_ref[:, 128:256] = res[8:16, :]
    drain()


def shards(query, cache_keys, cache_values, new_keys, new_values, lengths, residual_in, out_proj,
           norm_gain, adapter_down, tenant_adapter_up_matrix, tenant, w_gate, w_up, w_down):
    hbm = pl.BlockSpec(memory_space=pl.ANY)
    smem = pl.BlockSpec(memory_space=pltpu.SMEM)
    v = pltpu.VMEM
    dma = pltpu.SemaphoreType.DMA
    return pl.pallas_call(
        functools.partial(kernel, None),
        out_shape=jax.ShapeDtypeStruct((8, 256), F32),
        in_specs=[hbm, hbm, hbm, hbm, hbm, smem, hbm, hbm, hbm, hbm, hbm, smem, hbm, hbm, hbm],
        out_specs=pl.BlockSpec(memory_space=pltpu.VMEM),
        scratch_shapes=[
            v((8, 8192), BF16), v((8, 128, 512), BF16), v((8, 128, 512), BF16), v((8, 512), BF16),
            v((8, 512), BF16), v((16, 128), BF16), v((512, 1024), BF16), v((64, 128), F32),
            v((1024, 256), BF16), v((256, 128), BF16), v((8192, 256), BF16), v((128, 8192), BF16),
            v((2, 8, 32, 128), BF16), v((8, 128), F32), v((8, 2, 32, 128), BF16), v((8, 8, 128), F32),
            v((128, 128), F32), v((8, 128), F32), v((2, 48, 128), BF16),
            v((2, 8, 48, 128), BF16), v((4, 8, 16, 128), BF16), v((32, 16, 128), BF16), v((8, 8, 64, 128), BF16),
            v((2, 128), F32), v((8, 8, 128), F32),
            v((2, 4, 4, 8, 16, 128), BF16), v((4, 4, 8, 16, 128), BF16), v((4, 4, 8, 16, 128), BF16),
            v((4, 4, 8, 16, 128), BF16), v((8, 16, 128), BF16), v((8, 16, 128), BF16),
            dma((13,)),
            pltpu.SemaphoreType.REGULAR, dma((2, 8)), dma((2, 8)), dma((8,)), dma((8,)),
            dma((2, 8)), dma((2, 8)), dma((32,)), dma((32,)),
            dma((8,)), dma((8,)), dma((len(RUNS), 4, 4)), dma((len(RUNS), 4, 4)),
            dma((len(RUNS), 4)), dma((len(RUNS), 4)),
            dma((8, 4)), dma((8, 4)), dma((len(PARTS),)), dma((len(PARTS),)),
            dma((len(PARTS), 4, 4)), dma((len(PARTS), 4, 4)), dma((8,)), dma((8,)),
        ],
        compiler_params=pltpu.CompilerParams(
            collective_id=0, has_side_effects=True, vmem_limit_bytes=60 * 1024 * 1024),
    )(query, cache_keys, cache_values, new_keys, new_values, lengths, residual_in, out_proj,
      norm_gain.reshape(64, 128), adapter_down, tenant_adapter_up_matrix, tenant, w_gate, w_up, w_down).astype(BF16)


def solution(mesh):
    placed = (
        P("req", "role"),
        P("req", "ctx", "role"),
        P("req", "ctx", "role"),
        P("req", "role"),
        P("req", "role"),
        P("req"),
        P(None, "req"),
        P(("role", "ctx"), "req"),
        P(),
        P("req", None),
        P(None, ("role", "req", "ctx")),
        P(),
        P(None, ("role", "req", "ctx")),
        P(None, ("role", "req", "ctx")),
        P(("role", "req", "ctx"), None),
    )
    return jax.shard_map(
        shards, mesh=mesh, in_specs=placed, out_specs=P("req", ("role", "ctx")), check_vma=False
    )
```
